32 devices in a mesh: docs: 4 (over x, core), seg: 8 (over z, y).
Axes of the slice: x: 2, y: 2, z: 4, core: 2. Of those that a mesh axis runs over, the one named last changes fastest.
Arguments:
- tokens: bfloat16 [32, 8, 128, 768], P('docs', 'seg'), may hold values from -6 to 6
- doc_length: int32 [32], P('docs'), may hold values from 1 to 1024, as said below
- attn_weight: bfloat16 [2, 768, 2304], replicated, may hold values from -0.3125 to 0.3125
- query_bias: bfloat16 [2, 768], replicated, may hold values from -3 to 3
- value_bias: bfloat16 [2, 768], replicated, may hold values from -3 to 3
- proj_weight: bfloat16 [2, 768, 768], replicated, may hold values from -0.875 to 0.875
- proj_bias: bfloat16 [2, 768], replicated, may hold values from -2 to 2
- norm1_gain: bfloat16 [2, 768], replicated, may hold values from 0.5 to 1.5
- norm1_shift: bfloat16 [2, 768], replicated, may hold values from -2 to 2
- inner_weight: bfloat16 [2, 768, 3072], replicated, may hold values from -0.21875 to 0.21875
- inner_bias: bfloat16 [2, 3072], replicated, may hold values from -3 to 3
- outer_weight: bfloat16 [2, 3072, 768], replicated, may hold values from -0.109375 to 0.109375
- outer_bias: bfloat16 [2, 768], replicated, may hold values from -2 to 2
- norm2_gain: bfloat16 [2, 768], replicated, may hold values from 0.5 to 1.5
- norm2_shift: bfloat16 [2, 768], replicated, may hold values from -2 to 2
- seg_position: bfloat16 [8, 768], replicated, may hold values from -6 to 6
- cotangent: bfloat16 [32, 8, 128, 768], P('docs', 'seg'), may hold values from -6 to 6
Outputs:
- layer_out: bfloat16 [32, 8, 128, 768], P('docs', 'seg')
- input_grad: float32 [32, 8, 128, 768], P('docs', 'seg')
- attn_weight_grad: float32 [2, 768, 2304], P(None, 'seg')
- query_bias_grad: float32 [2, 768], P(None, 'seg')
- value_bias_grad: float32 [2, 768], P(None, 'seg')
- proj_weight_grad: float32 [2, 768, 768], P(None, 'seg')
- proj_bias_grad: float32 [2, 768], P(None, 'seg')
- norm1_gain_grad: float32 [2, 768], P(None, 'seg')
- norm1_shift_grad: float32 [2, 768], P(None, 'seg')
- inner_weight_grad: float32 [2, 768, 3072], P(None, 'seg')
- inner_bias_grad: float32 [2, 3072], P(None, 'seg')
- outer_weight_grad: float32 [2, 3072, 768], P(None, 'seg')
- outer_bias_grad: float32 [2, 768], P(None, 'seg')
- norm2_gain_grad: float32 [2, 768], P(None, 'seg')
- norm2_shift_grad: float32 [2, 768], P(None, 'seg')
- position_grad: float32 [8, 768], P(None, 'seg')
The draws below stay inside these ranges and needn't reach their ends.
Inputs may be any that keep to these rules, and one draw needn't show every extreme that they name: `doc_length`: in each aligned block of 8 documents (those of one index of docs) one document has exactly 1024 tokens.
All inputs are finite; a program needn't handle non-finite values.
Results may differ from the reference program's by a relative error of at most 0.035.
Values may be sent and summed in bfloat16 or wider, within the bound.
No kernel may reach another device: no remote copies, remote signals or barrier semaphores. Data moves between devices by JAX's collectives and lax.ppermute only.
A program may use at most 256 MiB of HBM per device.

```python
import jax
import jax.numpy as jnp
from jax import lax

D = 768
HEADS = 12
FF = 3072
SEGLEN = 128
DOC_DEV = 8
HEAD = 64
SEGS = 8
DOCS = 32


def draw_doc_length(key, part):
    key = jax.random.fold_in(key, 11)
    first, second = jax.random.split(key)
    longest = SEGS * SEGLEN
    lengths = jax.random.randint(first, (DOCS,), 1, longest + 1)
    chosen = jax.random.randint(second, (DOCS // DOC_DEV, 1), 0, DOC_DEV)
    marked = (jnp.arange(DOC_DEV)[None, :] == chosen).reshape(DOCS)
    return jnp.where(marked, longest, lengths).astype(jnp.int32)


def with_spikes(result, key, source, target, blocks, factor):
    owner, partner = [(jnp.arange(result.shape[dim]) // (result.shape[dim] // blocks)).reshape([-1 if axis == dim else 1 for axis in range(result.ndim)]) for dim in (source, target)]
    chosen = jax.random.permutation(key, blocks)[partner]
    strong = (owner == chosen) | (owner == (partner + blocks // 2) % blocks)
    return jnp.where(strong, factor * result, result)


def block_scale(rng, extent, cuts, smallest, largest):
    level, own = 1.0, jax.random.fold_in(rng, 6)
    for dim, shards_of in cuts:
        heights = jnp.exp(jax.random.uniform(jax.random.fold_in(own, dim), (shards_of,), jnp.float32, smallest / len(cuts), largest / len(cuts)))
        level = level * jnp.repeat(heights, extent[dim] // shards_of).reshape([-1 if axis == dim else 1 for axis in range(len(extent))])
    return level


def normal_values(stream_key, dims, scale, bound, shards=(), held_as=jnp.bfloat16):
    drawn = jax.random.normal(stream_key, dims, jnp.float32) * scale
    if len(shards) > 0:
        drawn = block_scale(stream_key, dims, shards, -0.22, 0.18) * drawn
    return jnp.clip(drawn, min=-bound, max=bound).astype(held_as)


def noise_with(stream_key, dims, scale, most, shards, heavy, dtype=jnp.bfloat16):
    array = scale * jax.random.normal(stream_key, dims, jnp.float32)
    if shards:
        array = array * block_scale(stream_key, dims, shards, -0.22, 0.18)
    return jnp.clip(with_spikes(array, jax.random.fold_in(stream_key, 3), *heavy), -most, most).astype(dtype)


def setup_inputs(seed: int = 0) -> dict:
    splits = jax.random.split(jax.random.key(seed), 18)
    return {
        "tokens": normal_values(splits[0], (DOCS, SEGS, SEGLEN, D), 1.0, 6.0, ((0, 4), (1, 8))),
        "doc_length": draw_doc_length(jax.random.fold_in(splits[17], 71), 0),
        "attn_weight": normal_values(splits[2], (2, D, 3 * D), (D // 2) ** -0.5, 0.3125),
        "query_bias": normal_values(splits[3], (2, D), 0.5, 3.0),
        "value_bias": normal_values(splits[4], (2, D), 0.5, 3.0),
        "proj_weight": normal_values(splits[5], (2, D, D), (D // 16) ** -0.5, 0.875),
        "proj_bias": normal_values(splits[6], (2, D), 0.3, 2.0),
        "norm1_gain": jnp.clip(1.0 + 0.1 * jax.random.normal(splits[7], (2, D), jnp.float32), 0.5, 1.5).astype(jnp.bfloat16),
        "norm1_shift": normal_values(splits[8], (2, D), 0.3, 2.0),
        "inner_weight": normal_values(splits[9], (2, D, FF), D ** -0.5, 0.21875),
        "inner_bias": normal_values(splits[10], (2, FF), 0.5, 3.0),
        "outer_weight": normal_values(splits[11], (2, FF, D), FF ** -0.5, 0.109375),
        "outer_bias": normal_values(splits[12], (2, D), 0.3, 2.0),
        "norm2_gain": jnp.clip(1.0 + 0.1 * jax.random.normal(splits[13], (2, D), jnp.float32), 0.5, 1.5).astype(jnp.bfloat16),
        "norm2_shift": normal_values(splits[14], (2, D), 0.3, 2.0),
        "seg_position": normal_values(splits[15], (SEGS, D), 1.0, 6.0),
        "cotangent": noise_with(splits[16], (DOCS, SEGS, SEGLEN, D), 1.0, 6.0, ((0, 4), (1, 8)), (1, 3, 8, 2.0)),
    }


NEG = -1e+30
EPS = 1e-05

@jax.custom_vjp
def low(v):
    return lax.optimization_barrier(v.astype(jnp.bfloat16)).astype(jnp.float32)

@jax.custom_vjp
def low_back(v):
    return v

def low_keep(v):
    return (low(v), None)

def low_pass(kept, grad):
    return (grad,)

def back_keep(v):
    return (v, None)

def back_low(kept, grad):
    return (low(grad),)
low.defvjp(low_keep, low_pass)
low_back.defvjp(back_keep, back_low)

def matmul(left, right):
    return jnp.dot(left, right, precision=lax.Precision.HIGHEST)

def layer_norm(rows, gain, shift):
    center = rows - lax.optimization_barrier(jnp.mean(rows, axis=-1, keepdims=True))
    rstd = lax.rsqrt(lax.optimization_barrier(jnp.mean(center * center, axis=-1, keepdims=True)) + EPS)
    return center * rstd * gain + shift

def block(inputs, key_mask, params):
    attn_weight, query_bias, value_bias, proj_weight, proj_bias, gain_one, shift_one, inner_weight, inner_bias, outer_weight, outer_bias, gain_two, shift_two = params
    groups, length, width = inputs.shape
    rows = inputs.reshape(groups * length, width)
    rows_low = low(rows)
    mixed = matmul(rows_low, attn_weight)
    queries = low_back(low(mixed[:, :width] + query_bias)).reshape(groups, length, HEADS, HEAD)
    keys_low = low_back(low(mixed[:, width:2 * width])).reshape(groups, length, HEADS, HEAD)
    values_low = low_back(low(mixed[:, 2 * width:] + value_bias)).reshape(groups, length, HEADS, HEAD)
    scores = jnp.einsum('bqhd,bkhd->bhqk', queries, keys_low, precision=lax.Precision.HIGHEST)
    scores = low_back(scores * (1.0 / jnp.sqrt(jnp.float32(HEAD))))
    scores = jnp.where(key_mask[:, None, None, :], scores, NEG)
    probs = low(jax.nn.softmax(scores, axis=-1))
    attended = jnp.einsum('bhqk,bkhd->bqhd', probs, values_low, precision=lax.Precision.HIGHEST)
    attended = low_back(low(attended.reshape(groups * length, width)))
    branch_one = low_back(matmul(attended, proj_weight) + proj_bias)
    hidden_one = layer_norm(rows + branch_one, gain_one, shift_one)
    inner = low_back(matmul(low(hidden_one), inner_weight) + inner_bias)
    active = low(jax.nn.gelu(inner, approximate=False))
    branch_two = low_back(matmul(active, outer_weight) + outer_bias)
    hidden_two = layer_norm(hidden_one + branch_two, gain_two, shift_two)
    return hidden_two.reshape(groups, length, width)

def reference(tokens, doc_length, attn_weight, query_bias, value_bias, proj_weight, proj_bias, norm1_gain, norm1_shift, inner_weight, inner_bias, outer_weight, outer_bias, norm2_gain, norm2_shift, seg_position, cotangent):
    stacked = tuple((item.astype(jnp.float32) for item in (attn_weight, query_bias, value_bias, proj_weight, proj_bias, norm1_gain, norm1_shift, inner_weight, inner_bias, outer_weight, outer_bias, norm2_gain, norm2_shift)))
    position = seg_position.astype(jnp.float32)
    inputs = tokens.astype(jnp.float32)
    starts = (jnp.arange(SEGS) * SEGLEN).astype(jnp.int32)
    counts = jnp.clip(doc_length[:, None] - starts[None, :], 0, SEGLEN)
    token_mask = jnp.arange(SEGLEN)[None, None, :] < jnp.maximum(counts, 1)[:, :, None]
    cross_mask = starts[None, :] < doc_length[:, None]

    def forward(inputs, stacked, position):
        seg_params = tuple((item[0] for item in stacked))
        cross_params = tuple((item[1] for item in stacked))

        def one_doc(item):
            return block(item[0], item[1], seg_params)
        seg_out = lax.map(jax.checkpoint(one_doc), (inputs, token_mask))
        leaders = low(seg_out[:, :, 0, :])
        cross_out = block(leaders + position[None], cross_mask, cross_params)
        return seg_out.at[:, :, 0, :].set(cross_out)
    layer_out, pullback = jax.vjp(forward, inputs, stacked, position)
    input_grad, weight_grads, position_grad = pullback(cotangent.astype(jnp.float32))
    return (layer_out.astype(jnp.bfloat16), input_grad, weight_grads[0], weight_grads[1], weight_grads[2], weight_grads[3], weight_grads[4], weight_grads[5], weight_grads[6], weight_grads[7], weight_grads[8], weight_grads[9], weight_grads[10], weight_grads[11], weight_grads[12], position_grad)
```

```python
import functools
import math

import jax
import jax.numpy as jnp
from jax import lax
from jax.experimental import pallas as pl
from jax.experimental.pallas import tpu as pltpu
from jax.sharding import PartitionSpec as P

HEADS = 12
HEAD = 64
PAIR = 2 * HEAD


NEG = -1e30
EPS = 1e-05
LOW = jnp.bfloat16
F32 = jnp.float32
MIB = 1024 * 1024
TILE = 512


def dot(left, right):
    return lax.dot_general(left, right, (((1,), (0,)), ((), ())), preferred_element_type=F32)


def dot_rt(left, right):
    return lax.dot_general(left, right, (((1,), (1,)), ((), ())), preferred_element_type=F32)


def dot_lt(left, right):
    return lax.dot_general(left, right, (((0,), (0,)), ((), ())), preferred_element_type=F32)


def normalize(rows):
    center = rows - jnp.mean(rows, axis=-1, keepdims=True)
    rstd = lax.rsqrt(jnp.mean(center * center, axis=-1, keepdims=True) + EPS)
    return center * rstd, rstd


def norm_back(grad, gain, normed, rstd):
    scaled = grad * gain
    return rstd * (
        scaled
        - jnp.mean(scaled, axis=-1, keepdims=True)
        - normed * jnp.mean(scaled * normed, axis=-1, keepdims=True)
    )


def gelu_and_slope(inner):
    size = jnp.abs(inner)
    t = 1.0 / (1.0 + (0.3275911 * 0.7071067811865476) * size)
    bell = jnp.exp(-0.5 * inner * inner)
    series = 0.5 * 1.061405429 * t - 0.5 * 1.453152027
    series = series * t + 0.5 * 1.421413741
    series = series * t - 0.5 * 0.284496736
    series = series * t + 0.5 * 0.254829592
    tail = series * t * bell
    below = jnp.where(inner >= 0.0, 1.0 - tail, tail)
    return inner * below, below + inner * bell * 0.3989422804014327


def colsum(rows):
    return jnp.sum(rows, axis=0, keepdims=True)


def head_masks():
    lane = lax.broadcasted_iota(jnp.int32, (1, PAIR), 1)
    first = (lane < HEAD).astype(F32).astype(LOW)
    second = (lane >= HEAD).astype(F32).astype(LOW)
    return lane, first, second


def whole(shape):
    return pl.BlockSpec(shape, lambda *_: (0,) * len(shape))


def of_block(index, shape):
    return pl.BlockSpec((1,) + shape, lambda *_: (index,) + (0,) * len(shape))


def params():
    return pltpu.CompilerParams(vmem_limit_bytes=60 * MIB)


def token_specs(tokens):
    return [pl.BlockSpec(memory_space=pl.ANY)] * len(tokens)


def cost(*_):
    return pl.CostEstimate(flops=1024, bytes_accessed=1024, transcendentals=0)


def attend_kernel(
    groups, length, len_ref, x_ref, w_ref, qb_ref, vb_ref, pw_ref, pb_ref,
    qkv_ref, att_ref, normed_ref, rstd_ref,
):
    step = pl.program_id(0)
    start = lax.axis_index("seg") * length
    rows_low = x_ref[...]
    width = rows_low.shape[1]
    queries = (dot(rows_low, w_ref[0, :, :width]) + qb_ref[0:1, :].astype(F32)).astype(LOW)
    keys = dot(rows_low, w_ref[0, :, width : 2 * width]).astype(LOW)
    values = (dot(rows_low, w_ref[0, :, 2 * width :]) + vb_ref[0:1, :].astype(F32)).astype(LOW)
    qkv_ref[:, :width] = queries
    qkv_ref[:, width : 2 * width] = keys
    qkv_ref[:, 2 * width :] = values
    queries = queries * LOW(1.0 / math.sqrt(HEAD))
    lane, first, second = head_masks()
    key_lane = lax.broadcasted_iota(jnp.int32, (1, length), 1)
    ones = jnp.ones((length, PAIR), LOW)
    for group in range(groups):
        count = jnp.clip(len_ref[step * groups + group] - start, 1, length)
        valid = key_lane < count
        rows = slice(group * length, (group + 1) * length)
        for pair in range(HEADS // 2):
            cols = slice(pair * PAIR, (pair + 1) * PAIR)
            both = queries[rows, cols]
            both = jnp.concatenate([both * first, both * second], axis=0)
            scores = jnp.where(valid, dot_rt(both, keys[rows, cols]), NEG)
            weights = jnp.exp(scores - jnp.max(scores, axis=1, keepdims=True)).astype(LOW)
            mixed = dot(weights, jnp.concatenate([values[rows, cols], ones], axis=1))
            mixed = mixed[:, :PAIR] / mixed[:, PAIR:]
            att_ref[rows, cols] = jnp.where(
                lane < HEAD, mixed[:length], mixed[length:]
            ).astype(LOW)
    resid = rows_low.astype(F32) + dot(att_ref[...], pw_ref[0]) + pb_ref[0:1, :].astype(F32)
    normed, rstd = normalize(resid)
    normed_ref[...] = normed
    rstd_ref[...] = jnp.broadcast_to(rstd, rstd_ref.shape)


def attend(rows_low, doc_length, seg_len, attn_weight, query_bias, value_bias, proj_weight, proj_bias):
    total, width = rows_low.shape
    groups = 2
    size = groups * seg_len
    return pl.pallas_call(
        functools.partial(attend_kernel, groups, seg_len),
        grid=(total // size,),
        in_specs=[
            pl.BlockSpec(memory_space=pltpu.SMEM),
            pl.BlockSpec((size, width), lambda i: (i, 0)),
            of_block(0, (width, 3 * width)),
            whole(query_bias.shape),
            whole(value_bias.shape),
            of_block(0, (width, width)),
            whole(proj_bias.shape),
        ],
        out_specs=[
            pl.BlockSpec((size, 3 * width), lambda i: (i, 0)),
            pl.BlockSpec((size, width), lambda i: (i, 0)),
            pl.BlockSpec((size, width), lambda i: (i, 0)),
            pl.BlockSpec((size, 128), lambda i: (i, 0)),
        ],
        out_shape=[
            jax.ShapeDtypeStruct((total, 3 * width), LOW),
            jax.ShapeDtypeStruct((total, width), LOW),
            jax.ShapeDtypeStruct((total, width), F32),
            jax.ShapeDtypeStruct((total, 128), F32),
        ],
        compiler_params=params(),
        cost_estimate=cost(
            2 * total * width * 4 * width + 8 * total * seg_len * width, 16 * MIB, total * seg_len * HEADS
        ),
        name="attend",
    )(doc_length, rows_low, attn_weight, query_bias, value_bias, proj_weight, proj_bias)


def leader_kernel(
    normed_ref, cot_ref, w1_ref, b1_ref, w2_ref, b2_ref, g1_ref, s1_ref, g2_ref, s2_ref,
    out_ref, hidden_ref, acc_ref,
):
    step = pl.program_id(0)

    @pl.when(step == 0)
    def _():
        hidden_ref[...] = normed_ref[:, 0, :] * g1_ref[0:1, :].astype(F32) + s1_ref[0:1, :].astype(F32)
        acc_ref[...] = jnp.zeros_like(acc_ref)

    inner = dot(hidden_ref[...].astype(LOW), w1_ref[0]) + b1_ref[0:1, :].astype(F32)
    active, _ = gelu_and_slope(inner)
    acc_ref[...] += dot(active.astype(LOW), w2_ref[0])

    @pl.when(step == pl.num_programs(0) - 1)
    def _():
        normed, _ = normalize(hidden_ref[...] + acc_ref[...] + b2_ref[0:1, :].astype(F32))
        out = normed * g2_ref[0:1, :].astype(F32) + s2_ref[0:1, :].astype(F32)
        out_ref[0] = out.astype(LOW)
        out_ref[1] = cot_ref[:, 0, :]


def ff_specs(width, tile, pick=lambda i: i):
    return [
        pl.BlockSpec((1, width, tile), lambda i, *_: (0, 0, pick(i))),
        pl.BlockSpec((2, tile), lambda i, *_: (0, pick(i))),
        pl.BlockSpec((1, tile, width), lambda i, *_: (0, pick(i), 0)),
    ]


def lead(normed, cots, docs, inner_weight, inner_bias, outer_weight, outer_bias, g1, s1, g2, s2):
    width, hidden = inner_weight.shape[1:]
    normed = normed.reshape(docs, -1, width)
    cots = cots.reshape(docs, -1, width)
    return pl.pallas_call(
        leader_kernel,
        grid=(hidden // TILE,),
        in_specs=[whole((docs, 8, width)), whole((docs, 16, width))]
        + ff_specs(width, TILE)
        + [whole((2, width))] * 5,
        out_specs=whole((2, docs, width)),
        out_shape=jax.ShapeDtypeStruct((2, docs, width), LOW),
        scratch_shapes=[pltpu.VMEM((docs, width), F32), pltpu.VMEM((docs, width), F32)],
        compiler_params=params(),
        cost_estimate=cost(4 * docs * width * hidden, 4 * width * hidden),
        name="leaders",
    )(normed, cots, inner_weight, inner_bias, outer_weight, outer_bias, g1, s1, g2, s2)


CHUNK = 256


def feed_kernel(
    normed_ref, w1_ref, b1_ref, w2_ref, b2_ref, g1_ref, s1_ref, g2_ref, s2_ref,
    active_ref, slope_ref, out_ref, normed2_ref, rstd2_ref, low_ref, acc_ref,
):
    step = pl.program_id(0)
    total = normed_ref.shape[0]
    chunks = [slice(at, at + CHUNK) for at in range(0, total, CHUNK)]

    @pl.when(step == 0)
    def _():
        for rows in chunks:
            hidden = normed_ref[rows, :] * g1_ref[0:1, :].astype(F32) + s1_ref[0:1, :].astype(F32)
            low_ref[rows, :] = hidden.astype(LOW)
            acc_ref[rows, :] = hidden + b2_ref[0:1, :].astype(F32)

    bias = b1_ref[0:1, :].astype(F32)
    inner = dot(low_ref[chunks[0], :], w1_ref[0])
    for at, rows in enumerate(chunks):
        active, slope = gelu_and_slope(inner + bias)
        if at + 1 < len(chunks):
            inner = dot(low_ref[chunks[at + 1], :], w1_ref[0])
        active = active.astype(LOW)
        active_ref[rows, :] = active
        slope_ref[rows, :] = slope.astype(LOW)
        acc_ref[rows, :] += dot(active, w2_ref[0])

    @pl.when(step == pl.num_programs(0) - 1)
    def _():
        for rows in chunks:
            normed, rstd = normalize(acc_ref[rows, :])
            normed2_ref[rows, :] = normed
            rstd2_ref[rows, :] = jnp.broadcast_to(rstd, (CHUNK, 128))
            out = normed * g2_ref[0:1, :].astype(F32) + s2_ref[0:1, :].astype(F32)
            out_ref[rows, :] = out.astype(LOW)


def feed(normed, inner_weight, inner_bias, outer_weight, outer_bias, g1, s1, g2, s2):
    total, width = normed.shape
    hidden = inner_weight.shape[2]
    return pl.pallas_call(
        feed_kernel,
        grid=(hidden // TILE,),
        in_specs=[whole((total, width))] + ff_specs(width, TILE) + [whole((2, width))] * 5,
        out_specs=[
            pl.BlockSpec((total, TILE), lambda i: (0, i)),
            pl.BlockSpec((total, TILE), lambda i: (0, i)),
            whole((total, width)),
            whole((total, width)),
            whole((total, 128)),
            whole((total, width)),
        ],
        out_shape=[
            jax.ShapeDtypeStruct((total, hidden), LOW),
            jax.ShapeDtypeStruct((total, hidden), LOW),
            jax.ShapeDtypeStruct((total, width), LOW),
            jax.ShapeDtypeStruct((total, width), F32),
            jax.ShapeDtypeStruct((total, 128), F32),
            jax.ShapeDtypeStruct((total, width), LOW),
        ],
        scratch_shapes=[pltpu.VMEM((total, width), F32)],
        compiler_params=params(),
        cost_estimate=cost(
            4 * total * width * hidden, 4 * width * hidden + 4 * total * hidden + 10 * total * width, 2 * total * hidden
        ),
        name="feed",
    )(normed, inner_weight, inner_bias, outer_weight, outer_bias, g1, s1, g2, s2)


def slots(columns):
    return -(-columns // 128) * 128


def bundle_places(width, hidden, segments):
    own = slots(width // segments)
    sizes = [own, own, own, slots(hidden // segments), 3 * width, width, hidden, width, own]
    places, start = [], 0
    for size in sizes:
        places.append((start, size))
        start += size
    return places, start


def cross_kernel(
    docs, segments, length, len_ref, lead_ref, cot_ref, pos_ref,
    qb_ref, vb_ref, pb_ref, g1_ref, s1_ref, b1_ref, b2_ref, g2_ref, s2_ref,
    aw_hbm, pw_hbm, w1_hbm, w2_hbm,
    out_ref, back_ref, bundle_ref,
    aw_ref, pw_ref, w1_ref, w2_ref, inner_ref, probs_ref, low_ref, att_ref, hid_ref, act_ref, sems,
):
    width = lead_ref.shape[1]
    hidden = w1_ref.shape[1]
    places, _ = bundle_places(width, hidden, segments)
    dmix_ref, dproj_ref, dinner_ref, dout_ref = (
        bundle_ref.at[:, places[at][0] : places[at][0] + places[at][1]] for at in range(4, 8)
    )
    copies = [
        pltpu.make_async_copy(src.at[1], dst, sems.at[i])
        for i, (src, dst) in enumerate(
            [(aw_hbm, aw_ref), (pw_hbm, pw_ref), (w1_hbm, w1_ref), (w2_hbm, w2_ref)]
        )
    ]
    for copy in copies:
        copy.start()
    total = lead_ref.shape[0]
    scale = 1.0 / math.sqrt(HEAD)

    def row(ref):
        return ref[1:2, :].astype(F32)

    rows = lead_ref[...].astype(F32) + jnp.concatenate([pos_ref[...].astype(F32)] * docs, axis=0)
    rows_low = rows.astype(LOW)
    low_ref[...] = rows_low
    both_heads = (total, 2 * total)
    key = lax.broadcasted_iota(jnp.int32, both_heads, 0)
    query = lax.broadcasted_iota(jnp.int32, both_heads, 1) % total
    key_doc = key // segments
    reach = jnp.zeros(both_heads, jnp.int32)
    for doc in range(docs):
        reach = jnp.where(key_doc == doc, len_ref[doc], reach)
    valid = (key_doc == query // segments) & ((key - key_doc * segments) * length < reach)
    lane, first, second = head_masks()

    copies[0].wait()
    queries = (dot(rows_low, aw_ref[:, :width]) + row(qb_ref)).astype(LOW)
    keys = dot(rows_low, aw_ref[:, width : 2 * width]).astype(LOW)
    values = (dot(rows_low, aw_ref[:, 2 * width :]) + row(vb_ref)).astype(LOW)

    def stacked(both):
        return jnp.concatenate([both * first, both * second], axis=0)

    def picked(both):
        return jnp.where(lane < HEAD, both[:total], both[total:])

    for pair in range(HEADS // 2):
        cols = slice(pair * PAIR, (pair + 1) * PAIR)
        scores = dot_rt(keys[:, cols], stacked(queries[:, cols])) * scale
        scores = jnp.where(valid, scores, NEG)
        weights = jnp.exp(scores - jnp.max(scores, axis=0, keepdims=True))
        probs = weights / jnp.sum(weights, axis=0, keepdims=True)
        probs_ref[pair] = probs
        att_ref[:, cols] = picked(dot_lt(probs.astype(LOW), values[:, cols])).astype(LOW)
    copies[1].wait()
    resid = rows + dot(att_ref[...], pw_ref[...]) + row(pb_ref)
    normed_one, rstd_one = normalize(resid)
    hidden = normed_one * row(g1_ref) + row(s1_ref)
    hidden_low = hidden.astype(LOW)
    hid_ref[...] = hidden_low
    copies[2].wait()
    copies[3].wait()
    count = w1_ref.shape[1] // TILE
    branch = jnp.zeros((total, width), F32)
    for at in range(count):
        cols = slice(at * TILE, (at + 1) * TILE)
        active, slope = gelu_and_slope(dot(hidden_low, w1_ref[:, cols]) + b1_ref[1:2, cols].astype(F32))
        inner_ref[:, cols] = slope
        active = active.astype(LOW)
        act_ref[:, cols] = active
        branch += dot(active, w2_ref[cols, :])
    normed_two, rstd_two = normalize(hidden + branch + row(b2_ref))
    out_ref[...] = normed_two * row(g2_ref) + row(s2_ref)

    upper = cot_ref[...].astype(F32)
    sums = [colsum(upper * normed_two), colsum(upper)]
    resid_two = norm_back(upper, row(g2_ref), normed_two, rstd_two)
    branch_two = resid_two.astype(LOW)
    dout_ref[...] = branch_two
    hidden_grad = resid_two
    for at in range(count):
        cols = slice(at * TILE, (at + 1) * TILE)
        inner_grad = (dot_rt(branch_two, w2_ref[cols, :]) * inner_ref[:, cols]).astype(LOW)
        dinner_ref[:, cols] = inner_grad
        hidden_grad += dot_rt(inner_grad, w1_ref[:, cols])
    sums = [colsum(hidden_grad * normed_one), colsum(hidden_grad)] + sums
    resid_one = norm_back(hidden_grad, row(g1_ref), normed_one, rstd_one)
    branch_one = resid_one.astype(LOW)
    dproj_ref[...] = branch_one
    att_grad = dot_rt(branch_one, pw_ref[...]).astype(LOW)
    for pair in range(HEADS // 2):
        cols = slice(pair * PAIR, (pair + 1) * PAIR)
        probs = probs_ref[pair]
        att_both = stacked(att_grad[:, cols])
        prob_grad = dot_rt(values[:, cols], att_both)
        score_grad = probs * (prob_grad - jnp.sum(prob_grad * probs, axis=0, keepdims=True))
        score_grad = score_grad.astype(LOW)
        dmix_ref[:, cols] = (picked(dot_lt(score_grad, keys[:, cols])) * scale).astype(LOW)
        cols_k = slice(width + pair * PAIR, width + (pair + 1) * PAIR)
        dmix_ref[:, cols_k] = (dot(score_grad, stacked(queries[:, cols])) * scale).astype(LOW)
        cols_v = slice(2 * width + pair * PAIR, 2 * width + (pair + 1) * PAIR)
        dmix_ref[:, cols_v] = dot(probs.astype(LOW), att_both).astype(LOW)
    back = resid_one + dot_rt(dmix_ref[...], aw_ref[...])
    back_ref[...] = back
    seg = lax.axis_index("seg")

    def own(value, slot):
        step = value.shape[1] // segments
        return pltpu.roll(value.astype(F32), lax.rem(value.shape[1] - seg * step, value.shape[1]), 1)[:, :slot]

    for at, item in enumerate((low_ref, att_ref, hid_ref, act_ref)):
        start, slot = places[at]
        bundle_ref[:, start : start + slot] = own(item[...], slot).astype(LOW)
    start, slot = places[8]
    by_segment = back[:segments]
    for doc in range(1, docs):
        by_segment += back[doc * segments : (doc + 1) * segments]
    pieces = [own(jnp.concatenate(sums + [jnp.zeros((4, width), F32)], axis=0), slot), own(by_segment, slot)]
    rest = total - 8 - segments
    if rest:
        pieces.append(jnp.zeros((rest, slot), F32))
    bundle_ref[:, start : start + slot] = jnp.concatenate(pieces, axis=0).astype(LOW)


def cross_block(
    leaders, cots, position, doc_length, seg_len,
    attn_weight, query_bias, value_bias, proj_weight, proj_bias, g1, s1,
    inner_weight, inner_bias, outer_weight, outer_bias, g2, s2,
):
    total, width = leaders.shape
    segments = position.shape[0]
    docs = total // segments
    hidden = inner_weight.shape[2]
    vmem = pl.BlockSpec(memory_space=pltpu.VMEM)
    hbm = pl.BlockSpec(memory_space=pl.ANY)

    def shape(columns, dtype=LOW):
        return jax.ShapeDtypeStruct((total, columns), dtype)

    return pl.pallas_call(
        functools.partial(cross_kernel, docs, segments, seg_len),
        in_specs=[pl.BlockSpec(memory_space=pltpu.SMEM)] + [vmem] * 12 + [hbm] * 4,
        out_specs=[vmem] * 3,
        out_shape=[shape(width, F32), shape(width, F32), shape(bundle_places(width, hidden, segments)[1])],
        scratch_shapes=[
            pltpu.VMEM((width, 3 * width), LOW),
            pltpu.VMEM((width, width), LOW),
            pltpu.VMEM((width, hidden), LOW),
            pltpu.VMEM((hidden, width), LOW),
            pltpu.VMEM((total, hidden), F32),
            pltpu.VMEM((HEADS // 2, total, 2 * total), F32),
            pltpu.VMEM((total, width), LOW),
            pltpu.VMEM((total, width), LOW),
            pltpu.VMEM((total, width), LOW),
            pltpu.VMEM((total, hidden), LOW),
            pltpu.SemaphoreType.DMA((4,)),
        ],
        compiler_params=params(),
        cost_estimate=cost(4 * total * width * (4 * width + 2 * hidden) * 2, 2 * width * (4 * width + 2 * hidden)),
        name="cross_block",
    )(
        doc_length, leaders, cots, position, query_bias, value_bias, proj_bias, g1, s1,
        inner_bias, outer_bias, g2, s2, attn_weight, proj_weight, inner_weight, outer_weight,
    )


def top_kernel(
    length, segments, cot_ref, back_ref, cross_ref, low_ref, normed_ref, rstd_ref, g2_ref, active_ref,
    resid_ref, branch_ref, sums_ref, sent_ref, kept_ref, patched_ref, swap_ref,
):
    step = pl.program_id(0)
    width = cot_ref.shape[1]
    half = width // 2

    @pl.when(step == 0)
    def _():
        core = lax.axis_index("docs") % 2
        first_row = lax.broadcasted_iota(jnp.int32, (length, 1), 0) == 0
        gain = g2_ref[0:1, :].astype(F32)
        seg = lax.axis_index("seg")
        sums = [jnp.zeros((1, width), F32)] * 3
        first_low = lax.broadcasted_iota(jnp.int32, (low_ref.shape[1], 1), 0) == 0
        for group in range(cot_ref.shape[0] // length):
            rows = slice(group * length, (group + 1) * length)
            own = pl.ds(group * segments + seg, 1)
            patched = jnp.where(first_low, cross_ref[own, :], low_ref[group].astype(F32))
            patched_ref[group] = patched.astype(LOW)
            upper = jnp.where(first_row, back_ref[own, :], cot_ref[rows, :].astype(F32))
            normed = normed_ref[rows, :]
            resid = norm_back(upper, gain, normed, rstd_ref[rows, 0:1])
            branch = resid.astype(LOW)
            resid_ref[rows, :] = resid
            branch_ref[rows, :] = branch
            left, right = branch[:, :half], branch[:, half:]
            swap_ref[rows, :half] = jnp.where(core == 0, right, left)
            swap_ref[rows, half:] = jnp.where(core == 0, left, right)
            for at, item in enumerate((upper * normed, upper, branch.astype(F32))):
                sums[at] = sums[at] + colsum(item)
        for at in range(3):
            sums_ref[at : at + 1, :] = sums[at]
        sums_ref[3:8, :] = jnp.zeros((5, width), F32)

    grad = dot_lt(active_ref[...], swap_ref[...]).astype(LOW)
    sent_ref[...] = grad[:, :half]
    kept_ref[...] = grad[:, half:]


def top_back(cots, back, cross_out, seg_low, seg_len, normed, rstd, g2, active):
    total, width = cots.shape
    hidden = active.shape[1]
    docs = total // seg_len
    return pl.pallas_call(
        functools.partial(top_kernel, seg_len, back.shape[0] // docs),
        grid=(hidden // TILE,),
        in_specs=[
            whole((total, width)),
            whole(back.shape),
            whole(back.shape),
            whole((docs, 16, width)),
            whole((total, width)),
            whole((total, 128)),
            whole((2, width)),
            pl.BlockSpec((total, TILE), lambda i: (0, i)),
        ],
        out_specs=[
            whole((total, width)),
            whole((total, width)),
            whole((8, width)),
            pl.BlockSpec((TILE, width // 2), lambda i: (i, 0)),
            pl.BlockSpec((TILE, width // 2), lambda i: (i, 0)),
            whole((docs, 16, width)),
        ],
        out_shape=[
            jax.ShapeDtypeStruct((total, width), F32),
            jax.ShapeDtypeStruct((total, width), LOW),
            jax.ShapeDtypeStruct((8, width), F32),
            jax.ShapeDtypeStruct((hidden, width // 2), LOW),
            jax.ShapeDtypeStruct((hidden, width // 2), LOW),
            jax.ShapeDtypeStruct((docs, seg_len, width), LOW),
        ],
        input_output_aliases={3: 5},
        scratch_shapes=[pltpu.VMEM((total, width), LOW)],
        compiler_params=params(),
        cost_estimate=cost(2 * total * width * hidden, 2 * total * hidden + 14 * total * width + 2 * width * hidden),
        name="top_back",
    )(cots, back, cross_out, seg_low.reshape(docs, seg_len, width), normed, rstd, g2, active)


def middle_step(branch_ref, low_ref, slope_ref, w1_ref, w2_ref, acc_ref, bias_ref, grad_ref):
    parts = []
    for at in range(0, branch_ref.shape[0], CHUNK):
        rows = slice(at, at + CHUNK)
        part = dot_rt(branch_ref[rows, :], w2_ref[0]) * slope_ref[rows, :].astype(F32)
        part = part.astype(LOW)
        acc_ref[rows, :] += dot_rt(part, w1_ref[0])
        parts.append(part)
    inner_grad = jnp.concatenate(parts, axis=0)
    bias_ref[...] = jnp.broadcast_to(colsum(inner_grad.astype(F32)), bias_ref.shape)
    grad_ref[...] = dot_lt(low_ref[...], inner_grad).astype(LOW)


def middle_first_kernel(core_ref, branch_ref, low_ref, slope_ref, w1_ref, w2_ref, *refs):
    acc_ref, bias_ref, sent_ref = refs[-3:]

    @pl.when(pl.program_id(0) == 0)
    def _():
        acc_ref[...] = jnp.zeros_like(acc_ref)

    middle_step(branch_ref, low_ref, slope_ref, w1_ref, w2_ref, acc_ref, bias_ref, sent_ref)


def middle_last_kernel(core_ref, branch_ref, low_ref, slope_ref, w1_ref, w2_ref, g1_ref, *refs):
    half_hbm, resid_hbm, normed_hbm, rstd_hbm = refs[:4]
    resid1_ref, branch1_ref, sums_ref, bias_ref, kept_ref, acc_ref = refs[-11:-5]
    half_ref, resid_ref, normed_ref, rstd_ref, sems = refs[-5:]
    step = pl.program_id(0)
    total, width = branch_ref.shape
    copies = [
        pltpu.make_async_copy(source, target, sems.at[at])
        for at, (source, target) in enumerate(
            ((half_hbm, half_ref), (resid_hbm, resid_ref), (normed_hbm, normed_ref), (rstd_hbm, rstd_ref))
        )
    ]

    @pl.when(step == 0)
    def _():
        for copy in copies:
            copy.start()
        acc_ref[...] = jnp.zeros_like(acc_ref)

    middle_step(branch_ref, low_ref, slope_ref, w1_ref, w2_ref, acc_ref, bias_ref, kept_ref)

    @pl.when(step == pl.num_programs(0) - 1)
    def _():
        for copy in copies:
            copy.wait()
        sums = [jnp.zeros((1, width), F32)] * 3
        for at in range(0, total, CHUNK):
            rows = slice(at, at + CHUNK)
            hidden_grad = acc_ref[rows, :] + half_ref[rows, :] + resid_ref[rows, :]
            normed = normed_ref[rows, :]
            resid = norm_back(hidden_grad, g1_ref[0:1, :].astype(F32), normed, rstd_ref[rows, 0:1])
            branch = resid.astype(LOW)
            resid1_ref[rows, :] = resid
            branch1_ref[rows, :] = branch
            for at_sum, item in enumerate((hidden_grad * normed, hidden_grad, branch.astype(F32))):
                sums[at_sum] = sums[at_sum] + colsum(item)
        for at_sum in range(3):
            sums_ref[at_sum : at_sum + 1, :] = sums[at_sum]
        sums_ref[3:8, :] = jnp.zeros((5, width), F32)


def half_order(steps):
    half = steps // 2

    def pick(step, core_ref):
        return jnp.where(step < half, 1 - core_ref[0], core_ref[0]) * half + step % half

    return pick


def middle_specs(total, width, steps, offset):
    pick = half_order(2 * steps)
    return [
        whole((total, width)),
        whole((total, width)),
        pl.BlockSpec((total, TILE), lambda i, c: (0, pick(i + offset, c))),
        pl.BlockSpec((1, width, TILE), lambda i, c: (0, 0, pick(i + offset, c))),
        pl.BlockSpec((1, TILE, width), lambda i, c: (0, pick(i + offset, c), 0)),
    ]


def middle_first(core, branch, low, slope, inner_weight, outer_weight, tokens=()):
    total, width = branch.shape
    steps = slope.shape[1] // TILE // 2
    return pl.pallas_call(
        middle_first_kernel,
        grid_spec=pltpu.PrefetchScalarGridSpec(
            num_scalar_prefetch=1,
            grid=(steps,),
            in_specs=middle_specs(total, width, steps, 0) + token_specs(tokens),
            out_specs=[
                whole((total, width)),
                pl.BlockSpec((8, TILE), lambda i, c: (0, i)),
                pl.BlockSpec((width, TILE), lambda i, c: (0, i)),
            ],
        ),
        out_shape=[
            jax.ShapeDtypeStruct((total, width), F32),
            jax.ShapeDtypeStruct((8, steps * TILE), F32),
            jax.ShapeDtypeStruct((width, steps * TILE), LOW),
        ],
        compiler_params=params(),
        cost_estimate=cost(),
        name="middle_first",
    )(core, branch, low, slope, inner_weight, outer_weight, *tokens)


def middle_last(core, branch, low, slope, inner_weight, outer_weight, g1, half, resid, normed, rstd, tokens=()):
    total, width = branch.shape
    steps = slope.shape[1] // TILE // 2
    return pl.pallas_call(
        middle_last_kernel,
        grid_spec=pltpu.PrefetchScalarGridSpec(
            num_scalar_prefetch=1,
            grid=(steps,),
            in_specs=middle_specs(total, width, steps, steps)
            + [whole((2, width))]
            + token_specs((half, resid, normed, rstd) + tuple(tokens)),
            out_specs=[
                whole((total, width)),
                whole((total, width)),
                whole((8, width)),
                pl.BlockSpec((8, TILE), lambda i, c: (0, i)),
                pl.BlockSpec((width, TILE), lambda i, c: (0, i)),
            ],
            scratch_shapes=[
                pltpu.VMEM((total, width), F32),
                pltpu.VMEM((total, width), F32),
                pltpu.VMEM((total, width), F32),
                pltpu.VMEM((total, width), F32),
                pltpu.VMEM((total, 128), F32),
                pltpu.SemaphoreType.DMA((4,)),
            ],
        ),
        out_shape=[
            jax.ShapeDtypeStruct((total, width), F32),
            jax.ShapeDtypeStruct((total, width), LOW),
            jax.ShapeDtypeStruct((8, width), F32),
            jax.ShapeDtypeStruct((8, steps * TILE), F32),
            jax.ShapeDtypeStruct((width, steps * TILE), LOW),
        ],
        compiler_params=params(),
        cost_estimate=cost(),
        name="middle_last",
    )(core, branch, low, slope, inner_weight, outer_weight, g1, half, resid, normed, rstd, *tokens)


def attend_back_kernel(groups, length, *refs):
    len_ref, branch_ref, resid_ref, qkv_ref, w_ref, pw_ref = refs[:6]
    dmix_ref, back_ref, sums_ref = refs[-3:]
    step = pl.program_id(0)
    start = lax.axis_index("seg") * length
    width = branch_ref.shape[1]
    scale = LOW(1.0 / math.sqrt(HEAD))
    att_grad = dot_rt(branch_ref[...], pw_ref[0]).astype(LOW)
    lane, first, second = head_masks()
    key_row = lax.broadcasted_iota(jnp.int32, (length, 1), 0)

    def stacked(both):
        return jnp.concatenate([both * first, both * second], axis=0)

    for group in range(groups):
        count = jnp.clip(len_ref[step * groups + group] - start, 1, length)
        valid = key_row < count
        rows = slice(group * length, (group + 1) * length)
        for pair in range(HEADS // 2):
            cols = slice(pair * PAIR, (pair + 1) * PAIR)
            cols_k = slice(width + pair * PAIR, width + (pair + 1) * PAIR)
            cols_v = slice(2 * width + pair * PAIR, 2 * width + (pair + 1) * PAIR)
            keys = qkv_ref[rows, cols_k]
            queries = stacked(qkv_ref[rows, cols] * scale)
            scores = jnp.where(valid, dot_rt(keys, queries), NEG)
            weights = jnp.exp(scores - jnp.max(scores, axis=0, keepdims=True))
            probs = weights * (1.0 / jnp.sum(weights, axis=0, keepdims=True))
            att_both = stacked(att_grad[rows, cols])
            prob_grad = dot_rt(qkv_ref[rows, cols_v], att_both)
            score_grad = probs * (prob_grad - jnp.sum(prob_grad * probs, axis=0, keepdims=True))
            score_grad = score_grad.astype(LOW)
            by_query = dot_lt(score_grad, keys * scale)
            dmix_ref[rows, cols] = jnp.where(
                lane < HEAD, by_query[:length], by_query[length:]
            ).astype(LOW)
            dmix_ref[rows, cols_k] = dot(score_grad, queries).astype(LOW)
            dmix_ref[rows, cols_v] = dot(probs.astype(LOW), att_both).astype(LOW)
    mixed = dmix_ref[...]
    back_ref[...] = resid_ref[...] + dot_rt(mixed, w_ref[0])

    @pl.when(step == 0)
    def _():
        sums_ref[...] = jnp.zeros_like(sums_ref)

    sums_ref[0:1, :] += colsum(mixed[:, :width].astype(F32))
    sums_ref[1:2, :] += colsum(mixed[:, 2 * width :].astype(F32))


def attend_back(branch, resid, qkv, doc_length, seg_len, attn_weight, proj_weight, tokens=()):
    total, width = branch.shape
    groups = 2
    size = groups * seg_len
    return pl.pallas_call(
        functools.partial(attend_back_kernel, groups, seg_len),
        grid=(total // size,),
        in_specs=[
            pl.BlockSpec(memory_space=pltpu.SMEM),
            pl.BlockSpec((size, width), lambda i: (i, 0)),
            pl.BlockSpec((size, width), lambda i: (i, 0)),
            pl.BlockSpec((size, 3 * width), lambda i: (i, 0)),
            of_block(0, (width, 3 * width)),
            of_block(0, (width, width)),
        ]
        + token_specs(tokens),
        out_specs=[
            pl.BlockSpec((size, 3 * width), lambda i: (i, 0)),
            pl.BlockSpec((size, width), lambda i: (i, 0)),
            whole((8, width)),
        ],
        out_shape=[
            jax.ShapeDtypeStruct((total, 3 * width), LOW),
            jax.ShapeDtypeStruct((total, width), F32),
            jax.ShapeDtypeStruct((8, width), F32),
        ],
        compiler_params=params(),
        cost_estimate=cost(
            2 * total * width * 4 * width + 20 * total * seg_len * width, 20 * MIB, total * seg_len * HEADS
        ),
        name="attend_back",
    )(doc_length, branch, resid, qkv, attn_weight, proj_weight, *tokens)


def last_grads_kernel(core_ref, rows_ref, att_ref, mixed_ref, branch_ref, *refs):
    left, right = refs[-2:]
    step = pl.program_id(0)

    def attn(out):
        out[...] = dot_lt(rows_ref[...], mixed_ref[...]).astype(LOW)

    @pl.when(step == 1)
    def _():
        left[...] = dot_lt(att_ref[...], branch_ref[...]).astype(LOW)

    pl.when(step == 0)(functools.partial(attn, left))
    pl.when(step > 1)(functools.partial(attn, right))


def last_grads(core, rows, attended, mixed, branch, tokens=()):
    total, width = rows.shape
    tile = width // 2

    def third(step, core_ref):
        return core_ref[0] * 3 + jnp.maximum(step - 1, 0)

    out = jax.ShapeDtypeStruct((width, width), LOW)
    return pl.pallas_call(
        last_grads_kernel,
        grid_spec=pltpu.PrefetchScalarGridSpec(
            num_scalar_prefetch=1,
            grid=(4,),
            in_specs=[
                whole((total, width)),
                whole((total, width)),
                pl.BlockSpec((total, tile), lambda i, c: (0, third(i, c))),
                pl.BlockSpec((total, tile), lambda i, c: (0, c[0])),
            ]
            + token_specs(tokens),
            out_specs=[pl.BlockSpec((width, tile), lambda i, c, f=first: (0, jnp.clip(i - f, 0, 1))) for first in (0, 2)],
        ),
        out_shape=[out] * 2,
        compiler_params=params(),
        cost_estimate=cost(),
        name="last_grads",
    )(core, rows, attended, mixed, branch, *tokens)


def bits_of(axis):
    return lax.axis_size(axis).bit_length() - 1


def partner(value, axis, bit):
    return flipped(value, axis, 1 << bit)


def flipped(value, axis, mask):
    return lax.ppermute(value, axis, [(i, i ^ mask) for i in range(lax.axis_size(axis))])


def my_bit(axis, bit):
    return (lax.axis_index(axis) >> bit) & 1


def gather_bit(value, axis, bit, dim):
    other = partner(value, axis, bit)
    first = my_bit(axis, bit) == 0
    return jnp.concatenate(
        [jnp.where(first, value, other), jnp.where(first, other, value)], axis=dim
    )


def gather_seg(value, dim):
    for bit in range(bits_of("seg")):
        value = gather_bit(value, "seg", bit, dim)
    return value


def pick_kernel(counts, blocks, place, skip, *refs):
    count = len(blocks)
    sources = refs[skip : skip + count]
    out_ref = refs[skip + count]
    buffers, sems = refs[skip + count + 1 : -1], refs[-1]
    lead, bits = place()
    copies = []
    for at, (seg_done, level) in enumerate(blocks):
        part = jnp.int32(0)
        for bit in bits[level:]:
            part = part * 2 + bit
        copies.append(pltpu.make_async_copy(sources[at].at[:, lead >> seg_done, part], buffers[at], sems.at[at]))
        copies[-1].start()
    for copy in copies:
        copy.wait()
    plain = sum(number for _, number in counts)
    for i in range(out_ref.shape[0]):
        at, start = 0, 0
        for rows, number in counts:
            span = slice(start, start + rows)
            total = buffers[at][i].astype(F32)
            for ref in buffers[at + 1 : at + number]:
                total = total + ref[i].astype(F32)
            for ref in buffers[plain:]:
                total = total + ref[i, span, :].astype(F32)
            out_ref[i, span, :] = total.astype(LOW)
            at += number
            start += rows


def gate_kernel(*_):
    pass


def gated(values, tokens):
    count = len(values)
    return pl.pallas_call(
        gate_kernel,
        in_specs=token_specs(values) + token_specs(tokens),
        out_specs=token_specs(values),
        out_shape=[jax.ShapeDtypeStruct(item.shape, item.dtype) for item in values],
        input_output_aliases={at: at for at in range(count)},
        cost_estimate=cost(),
        name="gate",
    )(*values, *tokens)


class Flow:
    def __init__(self, groups):
        self.groups = groups
        self.received = []
        self.seg_done = 0
        self.docs_done = []
        self.shards = groups[0][0].shape[0]
        self.columns = groups[0][0].shape[2]

    def picked(self, grid, lead, shift, last, tokens):
        docs_done = list(self.docs_done)
        level = len(docs_done) + (last is not None)
        blocks, operands, buffers, counts = [], [], [], []

        def add(array, seg_done, docs_level):
            parts = 1 << (level - docs_level)
            rows = array.shape[1] // parts
            operands.append(array.reshape(grid, 1 << (shift - seg_done), parts, rows, self.columns))
            buffers.append(pltpu.VMEM((grid, rows, self.columns), LOW))
            blocks.append((seg_done, docs_level))
            return rows

        for group in self.groups:
            depth = [add(array, 0, 0) for array in group][0]
            counts.append((depth, len(group)))
        for array, seg_done, docs_level in self.received:
            add(array, seg_done, docs_level)

        def place():
            bits = [my_bit("docs", bit) for bit in docs_done]
            return lead(), bits + ([last()] if last is not None else [])

        out = jax.ShapeDtypeStruct((grid, sum(depth for depth, _ in counts), self.columns), LOW)
        return pl.pallas_call(
            functools.partial(pick_kernel, tuple(counts), tuple(blocks), place, len(tokens)),
            in_specs=token_specs(tokens) + token_specs(operands),
            out_shape=out,
            scratch_shapes=buffers + [pltpu.SemaphoreType.DMA((len(blocks),))],
            compiler_params=params(),
            cost_estimate=cost(),
            name="pick",
        )(*tokens, *operands)

    def seg_step(self, tokens=(), send=True):
        bit = self.seg_done

        def lead():
            return (lax.axis_index("seg") & ((1 << bit) - 1)) | ((1 - my_bit("seg", bit)) << bit)

        sent = self.picked(self.shards >> (bit + 1), lead, bit + 1, None, tokens)
        self.seg_done += 1
        self.waiting = (sent, "seg", bit)
        return self.send() if send else sent

    def docs_step(self, bit, tokens=(), send=True):
        done = self.seg_done

        def lead():
            return lax.axis_index("seg") & ((1 << done) - 1)

        sent = self.picked(self.shards >> done, lead, done, lambda: 1 - my_bit("docs", bit), tokens)
        self.docs_done.append(bit)
        self.waiting = (sent, "docs", bit)
        return self.send() if send else sent

    def send(self):
        sent, axis, bit = self.waiting
        self.received.append((partner(sent, axis, bit), self.seg_done, len(self.docs_done)))
        return sent

    def settled(self, tokens=()):
        value = self.picked(1, lambda: lax.axis_index("seg"), bits_of("seg"), None, tokens)
        return value.reshape(value.shape[1:])


def finish_kernel(groups, outputs, small_at, *refs):
    me = lax.axis_index("docs")
    outs = refs[-outputs:]
    start = 0
    for count, reduce_x, rows, cuts in groups:
        pieces = refs[start : start + count]
        start += count

        def piece(target, pieces=pieces, rows=rows):
            value = pieces[0][:rows, :].astype(F32)
            for flip in range(1, len(pieces)):
                value = jnp.where(me ^ flip == target, pieces[flip][:rows, :].astype(F32), value)
            return value

        for core in range(2):
            parts = [piece(2 * x + core) for x in range(count // 2)]
            if reduce_x:
                total = parts[0]
                for part in parts[1:]:
                    total = total + part
                parts = [total]
            for x, part in enumerate(parts):
                place = slice(x * rows, (x + 1) * rows)
                for which, first, last, at in cuts:
                    out = outs[which]
                    base = core * (out.shape[2] // 2) + at
                    out[0, place, base : base + last - first] = part[:, first:last]
    if small_at is None:
        return
    count, _, rows, _ = groups[-1]
    pieces = refs[start - count : start]
    bias_ref, wide_ref, norm_ref = refs[start : start + 3]
    total = pieces[0][rows:, :].astype(F32)
    for flip in range(2, count, 2):
        total = total + pieces[flip][rows:, :].astype(F32)
    below = [(bias_ref, at) for at in range(4)] + [(norm_ref, at) for at in range(4)] + [(wide_ref, 0)]
    for row, (ref, at) in enumerate(below):
        out = outs[small_at + row]
        size = out.shape[1]
        out[0:1, :] = total[row : row + 1, :size]
        out[1:2, :] = ref[at : at + 1, :size]


def finish(groups, outputs, small=None, tokens=()):
    operands, layout = [], []
    for value, rows, reduce_x, cuts in groups:
        pieces = [value] + [flipped(value, "docs", flip) for flip in range(1, lax.axis_size("docs"))]
        operands += pieces
        layout.append((len(pieces), reduce_x, rows, cuts))
    out_specs = [pl.BlockSpec((1,) + item.shape[1:], lambda i: (0, 0, 0)) for item in outputs]
    out_shape = [jax.ShapeDtypeStruct(item.shape, F32) for item in outputs]
    if small:
        operands += small[0]
        out_specs += [whole((2, size)) for size in small[1]]
        out_shape += [jax.ShapeDtypeStruct((2, size), F32) for size in small[1]]
    count = len(operands)
    return pl.pallas_call(
        functools.partial(finish_kernel, layout, len(out_shape), len(outputs) if small else None),
        grid=(1,),
        in_specs=[whole(item.shape) for item in operands] + token_specs(outputs) + token_specs(tokens),
        out_specs=out_specs,
        out_shape=out_shape,
        input_output_aliases={count + at: at for at in range(len(outputs))},
        compiler_params=params(),
        cost_estimate=cost(),
        name="finish",
    )(*operands, *outputs, *tokens)


def small_kernel(low_ref, middle_ref, top_ref, kept_ref, sent_ref, out_ref):
    first = lax.axis_index("docs") % 2 == 0
    out_ref[...] = jnp.zeros_like(out_ref)
    shards, _, _ = out_ref.shape
    part = low_ref.shape[1] // shards
    items = [(low_ref, 0), (low_ref, 1), (middle_ref, 2), (top_ref, 2)]
    items += [(middle_ref, 0), (middle_ref, 1), (top_ref, 0), (top_ref, 1)]
    for shard in range(shards):
        for row, (ref, at) in enumerate(items):
            value = ref[at : at + 1, shard * part : (shard + 1) * part]
            out_ref[shard, row : row + 1, :part] = value.astype(LOW)
        half = shards // 2
        wide = kept_ref.shape[1] // half
        place = slice(shard % half * wide, (shard % half + 1) * wide)
        mine = first if shard < half else jnp.logical_not(first)
        value = jnp.where(mine, kept_ref[0:1, place], sent_ref[0:1, place])
        out_ref[shard, 8:9, :wide] = value.astype(LOW)


def small_rows(low, middle, top, kept, sent, segments):
    width = low.shape[1]
    return pl.pallas_call(
        small_kernel,
        out_shape=jax.ShapeDtypeStruct((segments, 16, width), LOW),
        compiler_params=params(),
        cost_estimate=cost(),
        name="small_rows",
    )(low, middle, top, kept, sent)


def cross_grad_kernel(segments, width, hidden, count, *refs):
    bundles = refs[:count]
    attn_ref, proj_ref, inner_ref, outer_ref, bias_ref, wide_ref, norm_ref, place_ref = refs[-8:]
    places, _ = bundle_places(width, hidden, segments)

    def rows(at):
        start, size = places[at]
        return jnp.concatenate([ref[:, start : start + size] for ref in bundles], axis=0)

    outs = (attn_ref, proj_ref, inner_ref, outer_ref)
    biases = []
    for at, out in enumerate(outs):
        right = rows(4 + at)
        out[0] = dot_lt(rows(at), right)[: out.shape[1]]
        biases.append(colsum(right.astype(F32)))
    seg = lax.axis_index("seg")

    def own(value, slot):
        step = value.shape[1] // segments
        value = jnp.broadcast_to(value, (8, value.shape[1]))
        return pltpu.roll(value, lax.rem(value.shape[1] - seg * step, value.shape[1]), 1)[0:1, :slot]

    slot = places[0][1]
    mixed = biases[0]
    parts = [mixed[:, :width], mixed[:, 2 * width :], biases[1], biases[3]]
    bias_ref[...] = jnp.concatenate([own(part, slot) for part in parts] + [jnp.zeros((4, slot), F32)], axis=0)
    wide_ref[...] = jnp.broadcast_to(own(biases[2], places[3][1]), wide_ref.shape)
    start, size = places[8]
    sums = bundles[0][:, start : start + size].astype(F32)
    for ref in bundles[1:]:
        sums = sums + ref[:, start : start + size].astype(F32)
    norm_ref[...] = sums[:8]
    place_ref[...] = sums[8 : 8 + segments, : place_ref.shape[1]]


def cross_grads(bundles, segments, width, hidden, tokens=()):
    part, wide = width // segments, hidden // segments
    places, _ = bundle_places(width, hidden, segments)
    slot = places[0][1]
    stacked = [(part, 3 * width), (part, width), (part, hidden), (wide, width)]
    plain = [(8, slot), (8, places[3][1]), (8, slot), (segments, part)]
    return pl.pallas_call(
        functools.partial(cross_grad_kernel, segments, width, hidden, len(bundles)),
        grid=(1,),
        in_specs=[whole(bundles[0].shape)] * len(bundles) + token_specs(tokens),
        out_specs=[pl.BlockSpec((1,) + item, lambda i: (1, 0, 0)) for item in stacked]
        + [whole(item) for item in plain],
        out_shape=[jax.ShapeDtypeStruct((2,) + item, F32) for item in stacked]
        + [jax.ShapeDtypeStruct(item, F32) for item in plain],
        compiler_params=params(),
        cost_estimate=cost(),
        name="cross_grads",
    )(*bundles, *tokens)


def on_device(
    tokens,
    doc_length,
    attn_weight,
    query_bias,
    value_bias,
    proj_weight,
    proj_bias,
    norm1_gain,
    norm1_shift,
    inner_weight,
    inner_bias,
    outer_weight,
    outer_bias,
    norm2_gain,
    norm2_shift,
    seg_position,
    cotangent,
):
    docs_here, _, seg_len, width = tokens.shape
    hidden = inner_weight.shape[2]
    segments = lax.axis_size("seg")
    core = (lax.axis_index("docs") % 2).astype(jnp.int32).reshape(1)
    total = docs_here * seg_len
    rows_low = tokens.reshape(total, width)
    cots = cotangent.reshape(total, width)
    seg_bits = bits_of("seg")
    across_bits = range(bits_of("docs") - 1, 0, -1)

    qkv, attended, normed_one, rstd_one = attend(
        rows_low, doc_length, seg_len, attn_weight, query_bias, value_bias, proj_weight, proj_bias
    )
    ff_weights = (inner_weight, inner_bias, outer_weight, outer_bias)
    norms = (norm1_gain, norm1_shift, norm2_gain, norm2_shift)
    leaders = lead(normed_one, cots, docs_here, *ff_weights, *norms)
    gathered = gather_seg(leaders[:, :, None, :], 2)
    active, slope, seg_low, normed_two, rstd_two, hidden_low = feed(normed_one, *ff_weights, *norms)

    gathered = gathered.reshape(2, docs_here * segments, width)
    cross_out, cross_back, bundle = cross_block(
        gathered[0], gathered[1], seg_position, doc_length, seg_len,
        attn_weight, query_bias, value_bias, proj_weight, proj_bias, norm1_gain, norm1_shift,
        inner_weight, inner_bias, outer_weight, outer_bias, norm2_gain, norm2_shift,
    )

    bundles = [bundle]
    for bit in across_bits:
        bundles = bundles + [partner(item, "docs", bit) for item in bundles]

    resid_two, branch_two, top_sums, outer_sent, outer_kept, layer_out = top_back(
        cots, cross_back, cross_out, seg_low, seg_len, normed_two, rstd_two, norm2_gain, active
    )
    outer_got = partner(outer_sent, "docs", 0)
    half_grad, inner_sums_sent, inner_sent = middle_first(
        core, branch_two, hidden_low, slope, inner_weight, outer_weight
    )

    def sharded(value):
        return value.reshape(segments, -1, value.shape[-1])

    outer = Flow([[sharded(outer_kept), sharded(outer_got)]])
    outer_first = outer.seg_step((inner_sent,))
    inner_got = partner(inner_sent, "docs", 0)
    resid_one, branch_one, mid_sums, inner_sums_kept, inner_kept = middle_last(
        core, branch_two, hidden_low, slope, inner_weight, outer_weight, norm1_gain,
        half_grad, resid_two, normed_one, rstd_one, (outer_first,),
    )
    inner = Flow([[sharded(inner_kept), sharded(inner_got)]])
    inner_first = [inner.docs_step(bit, tuple(bundles[1:])) for bit in across_bits][-1]
    outer_next = outer.seg_step((inner_first,))
    mixed_grad, input_grad, low_sums = attend_back(
        branch_one, resid_one, qkv, doc_length, seg_len, attn_weight, proj_weight, (inner_first, outer_next)
    )
    input_grad = input_grad.reshape(tokens.shape)
    others = [partner(item, "docs", 0) for item in bundles]
    outer_next = outer.seg_step((low_sums, *others))
    bundles = bundles + others
    inner_next = inner.seg_step((outer_next,))
    left_sent, right_sent = last_grads(
        1 - core, rows_low, attended, mixed_grad, branch_one, (outer_next, inner_next)
    )
    inner_next = inner.seg_step((left_sent,))
    for bit in range(3, seg_bits):
        outer.seg_step()
    outer = outer.settled((inner_next,))
    small = small_rows(low_sums, mid_sums, top_sums, inner_sums_kept, inner_sums_sent, segments)
    left_sent, right_sent, small = gated((left_sent, right_sent, small), (outer, inner_next))
    left_got, right_got, small_got = (partner(item, "docs", 0) for item in (left_sent, right_sent, small))
    left_kept, right_kept = last_grads(core, rows_low, attended, mixed_grad, branch_one, (left_sent,))
    left = Flow([[sharded(left_kept), sharded(left_got)]])
    for bit in across_bits:
        last = left.docs_step(bit)
    right = Flow([[sharded(right_kept), sharded(right_got)], [small, small_got]])
    last = right.seg_step((last,))
    last = inner.seg_step((last,))
    attn_out, proj_out, inner_out, outer_out, cross_bias, cross_wide, cross_norm, position_grad = cross_grads(
        bundles, segments, width, hidden, (last,)
    )
    part, wide = width // segments, hidden // segments
    for bit in range(3, seg_bits):
        inner.seg_step()
    inner = inner.settled((cross_bias,))
    last = left.seg_step((inner,))
    last = right.seg_step((last,))
    (outer_out,) = finish([(outer, wide, True, [(0, 0, width // 2, 0)])], [outer_out], tokens=(last,))
    last = left.seg_step((outer_out,))
    last = right.seg_step((last,))
    (inner_out,) = finish(
        [(inner, inner.shape[0], False, [(0, 0, hidden // 2, 0)])], [inner_out], tokens=(last,)
    )
    last = left.seg_step((inner_out,))
    for bit in range(3, seg_bits):
        last = left.seg_step((last,))
        last = right.seg_step((last,))
    right = right.settled((last,))
    left = left.settled((right,))
    third = width // 2
    attn_out, proj_out, *smalls = finish(
        [
            (left, left.shape[0], False, [(0, 0, third, 0), (1, third, width, 0)]),
            (right, part, True, [(0, 0, width, third)]),
        ],
        [attn_out, proj_out],
        ([cross_bias, cross_wide, cross_norm], [part] * 8 + [wide]),
    )
    qb, vb, pb, ob, g1, s1, g2, s2, ib = smalls
    return (
        layer_out.reshape(tokens.shape),
        input_grad,
        attn_out,
        qb,
        vb,
        proj_out,
        pb,
        g1,
        s1,
        inner_out,
        ib,
        outer_out,
        ob,
        g2,
        s2,
        position_grad,
    )


def solution(mesh):
    return jax.shard_map(
        on_device,
        mesh=mesh,
        in_specs=(
            P("docs", "seg", None, None),
            P("docs"),
            P(),
            P(),
            P(),
            P(),
            P(),
            P(),
            P(),
            P(),
            P(),
            P(),
            P(),
            P(),
            P(),
            P(),
            P("docs", "seg", None, None),
        ),
        out_specs=(
            P("docs", "seg", None, None),
            P("docs", "seg", None, None),
            P(None, "seg", None),
            P(None, "seg"),
            P(None, "seg"),
            P(None, "seg", None),
            P(None, "seg"),
            P(None, "seg"),
            P(None, "seg"),
            P(None, "seg", None),
            P(None, "seg"),
            P(None, "seg", None),
            P(None, "seg"),
            P(None, "seg"),
            P(None, "seg"),
            P(None, "seg"),
        ),
        check_vma=False,
    )
```

```python
import functools
import math

import jax
import jax.numpy as jnp
from jax import lax
from jax.experimental import pallas as pl
from jax.experimental.pallas import tpu as pltpu
from jax.sharding import PartitionSpec as P

HEADS = 12
HEAD = 64
PAIR = 2 * HEAD


NEG = -1e30
EPS = 1e-05
LOW = jnp.bfloat16
F32 = jnp.float32
MIB = 1024 * 1024
TILE = 512


def dot(left, right):
    return lax.dot_general(left, right, (((1,), (0,)), ((), ())), preferred_element_type=F32)


def dot_rt(left, right):
    return lax.dot_general(left, right, (((1,), (1,)), ((), ())), preferred_element_type=F32)


def dot_lt(left, right):
    return lax.dot_general(left, right, (((0,), (0,)), ((), ())), preferred_element_type=F32)


def normalize(rows):
    center = rows - jnp.mean(rows, axis=-1, keepdims=True)
    rstd = lax.rsqrt(jnp.mean(center * center, axis=-1, keepdims=True) + EPS)
    return center * rstd, rstd


def norm_back(grad, gain, normed, rstd):
    scaled = grad * gain
    return rstd * (
        scaled
        - jnp.mean(scaled, axis=-1, keepdims=True)
        - normed * jnp.mean(scaled * normed, axis=-1, keepdims=True)
    )


def gelu_and_slope(inner):
    kind = inner.dtype.type
    size = jnp.abs(inner)
    t = kind(1.0) / (kind(1.0) + kind(0.3275911 * 0.7071067811865476) * size)
    bell = jnp.exp(kind(-0.5) * inner * inner)
    series = kind(0.5 * 1.061405429) * t - kind(0.5 * 1.453152027)
    series = series * t + kind(0.5 * 1.421413741)
    series = series * t - kind(0.5 * 0.284496736)
    series = series * t + kind(0.5 * 0.254829592)
    tail = series * t * bell
    below = jnp.where(inner >= kind(0.0), kind(1.0) - tail, tail)
    return inner * below, below + inner * bell * kind(0.3989422804014327)


def colsum(rows):
    return jnp.sum(rows, axis=0, keepdims=True)


def head_masks():
    lane = lax.broadcasted_iota(jnp.int32, (1, PAIR), 1)
    first = (lane < HEAD).astype(F32).astype(LOW)
    second = (lane >= HEAD).astype(F32).astype(LOW)
    return lane, first, second


def whole(shape):
    return pl.BlockSpec(shape, lambda *_: (0,) * len(shape))


def of_block(index, shape):
    return pl.BlockSpec((1,) + shape, lambda *_: (index,) + (0,) * len(shape))


def params(limit_mib=64):
    return pltpu.CompilerParams(vmem_limit_bytes=limit_mib * MIB)


def token_specs(tokens):
    return [pl.BlockSpec(memory_space=pl.ANY)] * len(tokens)


def cost(*_):
    return pl.CostEstimate(flops=1024, bytes_accessed=1024, transcendentals=0)


def attend_kernel(
    groups, length, len_ref, x_ref, w_ref, qb_ref, vb_ref, pw_ref, pb_ref, g1_ref, s1_ref,
    qkv_ref, att_ref, normed_ref, hidden_ref, rstd_ref,
):
    step = pl.program_id(0)
    start = lax.axis_index("seg") * length
    rows_low = x_ref[...]
    width = rows_low.shape[1]
    queries = (dot(rows_low, w_ref[0, :, :width]) + qb_ref[0:1, :].astype(F32)).astype(LOW)
    keys = dot(rows_low, w_ref[0, :, width : 2 * width]).astype(LOW)
    values = (dot(rows_low, w_ref[0, :, 2 * width :]) + vb_ref[0:1, :].astype(F32)).astype(LOW)
    qkv_ref[:, :width] = queries
    qkv_ref[:, width : 2 * width] = keys
    qkv_ref[:, 2 * width :] = values
    queries = queries * LOW(1.0 / math.sqrt(HEAD))
    lane, first, second = head_masks()
    key_lane = lax.broadcasted_iota(jnp.int32, (1, length), 1)
    ones = jnp.ones((length, PAIR), LOW)
    places = []
    for group in range(groups):
        count = jnp.clip(len_ref[step * groups + group] - start, 1, length)
        rows = slice(group * length, (group + 1) * length)
        places += [(rows, slice(at, at + PAIR), key_lane < count) for at in range(0, width, PAIR)]
    scores = []
    for rows, cols, _ in places:
        both = queries[rows, cols]
        both = jnp.concatenate([both * first, both * second], axis=0)
        scores.append(dot_rt(both, keys[rows, cols]))
    weights = []
    for item, (_, _, valid) in zip(scores, places):
        item = jnp.where(valid, item, NEG)
        weights.append(jnp.exp(item - jnp.max(item, axis=1, keepdims=True)).astype(LOW))
    for item, (rows, cols, _) in zip(weights, places):
        mixed = dot(item, jnp.concatenate([values[rows, cols], ones], axis=1))
        mixed = mixed[:, :PAIR] / mixed[:, PAIR:]
        att_ref[rows, cols] = jnp.where(lane < HEAD, mixed[:length], mixed[length:]).astype(LOW)
    resid = rows_low.astype(F32) + dot(att_ref[...], pw_ref[0]) + pb_ref[0:1, :].astype(F32)
    normed, rstd = normalize(resid)
    normed_ref[...] = normed.astype(LOW)
    hidden_ref[...] = (normed * g1_ref[0:1, :].astype(F32) + s1_ref[0:1, :].astype(F32)).astype(LOW)
    rstd_ref[...] = jnp.broadcast_to(rstd, rstd_ref.shape)


def attend(rows_low, doc_length, seg_len, attn_weight, query_bias, value_bias, proj_weight, proj_bias, g1, s1):
    total, width = rows_low.shape
    groups = 2
    size = groups * seg_len
    return pl.pallas_call(
        functools.partial(attend_kernel, groups, seg_len),
        grid=(total // size,),
        in_specs=[
            pl.BlockSpec(memory_space=pltpu.SMEM),
            pl.BlockSpec((size, width), lambda i: (i, 0)),
            of_block(0, (width, 3 * width)),
            whole(query_bias.shape),
            whole(value_bias.shape),
            of_block(0, (width, width)),
            whole(proj_bias.shape),
            whole(g1.shape),
            whole(s1.shape),
        ],
        out_specs=[
            pl.BlockSpec((size, 3 * width), lambda i: (i, 0)),
            pl.BlockSpec((size, width), lambda i: (i, 0)),
            pl.BlockSpec((size, width), lambda i: (i, 0)),
            pl.BlockSpec((size, width), lambda i: (i, 0)),
            pl.BlockSpec((size, 128), lambda i: (i, 0)),
        ],
        out_shape=[
            jax.ShapeDtypeStruct((total, 3 * width), LOW),
            jax.ShapeDtypeStruct((total, width), LOW),
            jax.ShapeDtypeStruct((total, width), LOW),
            jax.ShapeDtypeStruct((total, width), LOW),
            jax.ShapeDtypeStruct((total, 128), F32),
        ],
        compiler_params=params(),
        cost_estimate=cost(
            2 * total * width * 4 * width + 8 * total * seg_len * width, 16 * MIB, total * seg_len * HEADS
        ),
        name="attend",
    )(doc_length, rows_low, attn_weight, query_bias, value_bias, proj_weight, proj_bias, g1, s1)


def leader_kernel(
    hidden_ref, cot_ref, b1_ref, b2_ref, g2_ref, s2_ref, w1_hbm, w2_hbm, out_ref, w1_ref, w2_ref, sems,
):
    tiles = w1_ref.shape[1] // TILE
    copies = []
    for at in range(tiles):
        cols = slice(at * TILE, (at + 1) * TILE)
        copies.append(
            (
                pltpu.make_async_copy(w1_hbm.at[0, :, cols], w1_ref.at[:, cols], sems.at[0, at]),
                pltpu.make_async_copy(w2_hbm.at[0, cols, :], w2_ref.at[cols, :], sems.at[1, at]),
            )
        )
    for pair in copies:
        for copy in pair:
            copy.start()
    hidden = hidden_ref[:, 0, :]
    total = hidden.astype(F32) + b2_ref[0:1, :].astype(F32)
    for at, pair in enumerate(copies):
        cols = slice(at * TILE, (at + 1) * TILE)
        pair[0].wait()
        active, _ = gelu_and_slope(dot(hidden, w1_ref[:, cols]) + b1_ref[0:1, cols].astype(F32))
        pair[1].wait()
        total = total + dot(active.astype(LOW), w2_ref[cols, :])
    normed, _ = normalize(total)
    out = normed * g2_ref[0:1, :].astype(F32) + s2_ref[0:1, :].astype(F32)
    out_ref[0] = out.astype(LOW)
    out_ref[1] = cot_ref[:, 0, :]


def ff_specs(width, tile, pick=lambda i: i):
    return [
        pl.BlockSpec((1, width, tile), lambda i, *_: (0, 0, pick(i))),
        pl.BlockSpec((2, tile), lambda i, *_: (0, pick(i))),
        pl.BlockSpec((1, tile, width), lambda i, *_: (0, pick(i), 0)),
    ]


def lead(hidden_low, cots, docs, inner_weight, inner_bias, outer_weight, outer_bias, g2, s2):
    width, hidden = inner_weight.shape[1:]
    hidden_low = hidden_low.reshape(docs, -1, width)
    cots = cots.reshape(docs, -1, width)
    hbm = pl.BlockSpec(memory_space=pl.ANY)
    return pl.pallas_call(
        leader_kernel,
        grid=(1,),
        in_specs=[whole((docs, 16, width))] * 2 + [whole((2, hidden))] + [whole((2, width))] * 3 + [hbm] * 2,
        out_specs=whole((2, docs, width)),
        out_shape=jax.ShapeDtypeStruct((2, docs, width), LOW),
        scratch_shapes=[
            pltpu.VMEM((width, hidden), LOW),
            pltpu.VMEM((hidden, width), LOW),
            pltpu.SemaphoreType.DMA((2, hidden // TILE)),
        ],
        compiler_params=params(),
        cost_estimate=cost(),
        name="leaders",
    )(hidden_low, cots, inner_bias, outer_bias, g2, s2, inner_weight, outer_weight)


CHUNK = 256


def feed_kernel(
    low_ref, w1_ref, b1_ref, w2_ref, b2_ref, g2_ref, s2_ref,
    active_ref, slope_ref, out_ref, normed2_ref, rstd2_ref, acc_ref,
):
    step = pl.program_id(0)
    last = pl.num_programs(0) - 1
    chunks = [slice(at, at + CHUNK) for at in range(0, low_ref.shape[0], CHUNK)]
    bias = b1_ref[0:1, :].astype(F32)

    @pl.when(step == 0)
    def _():
        for rows in chunks:
            acc_ref[rows, :] = low_ref[rows, :].astype(F32) + b2_ref[0:1, :].astype(F32)

    inner = dot(low_ref[chunks[0], :], w1_ref[0])
    for at, rows in enumerate(chunks):
        active, slope = gelu_and_slope((inner + bias).astype(LOW))
        if at + 1 < len(chunks):
            inner = dot(low_ref[chunks[at + 1], :], w1_ref[0])
        active_ref[rows, :] = active
        slope_ref[rows, :] = slope
        acc_ref[rows, :] += dot(active, w2_ref[0])

    @pl.when(step == last)
    def _():
        for rows in chunks:
            normed, rstd = normalize(acc_ref[rows, :])
            normed2_ref[rows, :] = normed.astype(LOW)
            rstd2_ref[rows, :] = jnp.broadcast_to(rstd, (CHUNK, 128))
            out = normed * g2_ref[0:1, :].astype(F32) + s2_ref[0:1, :].astype(F32)
            out_ref[rows, :] = out.astype(LOW)


def feed(hidden_low, inner_weight, inner_bias, outer_weight, outer_bias, g2, s2):
    total, width = hidden_low.shape
    hidden = inner_weight.shape[2]
    return pl.pallas_call(
        feed_kernel,
        grid=(hidden // TILE,),
        in_specs=[whole((total, width))] + ff_specs(width, TILE) + [whole((2, width))] * 3,
        out_specs=[
            pl.BlockSpec((total, TILE), lambda i: (0, i)),
            pl.BlockSpec((total, TILE), lambda i: (0, i)),
            whole((total, width)),
            whole((total, width)),
            whole((total, 128)),
        ],
        out_shape=[
            jax.ShapeDtypeStruct((total, hidden), LOW),
            jax.ShapeDtypeStruct((total, hidden), LOW),
            jax.ShapeDtypeStruct((total, width), LOW),
            jax.ShapeDtypeStruct((total, width), LOW),
            jax.ShapeDtypeStruct((total, 128), F32),
        ],
        scratch_shapes=[pltpu.VMEM((total, width), F32)],
        compiler_params=params(),
        cost_estimate=cost(),
        name="feed",
    )(hidden_low, inner_weight, inner_bias, outer_weight, outer_bias, g2, s2)


def slots(columns):
    return -(-columns // 128) * 128


def bundle_places(width, hidden, segments):
    own = slots(width // segments)
    sizes = [own, own, own, slots(hidden // segments), 3 * width, width, hidden, width, own]
    places, start = [], 0
    for size in sizes:
        places.append((start, size))
        start += size
    return places, start


def cross_kernel(docs, segments, length, len_ref, *refs):
    pieces, refs = refs[: segments // 2], refs[segments // 2 :]
    (
        pos_ref, qb_ref, vb_ref, pb_ref, g1_ref, s1_ref, b1_ref, b2_ref, g2_ref, s2_ref,
        seg_cot_ref, seg_normed_ref, seg_rstd_ref, aw_hbm, pw_hbm, w1_hbm, w2_hbm,
        out_ref, back_ref, bundle_ref, seg_branch_ref, seg_sums_ref,
        aw_ref, pw_ref, w1_ref, w2_ref, inner_ref, probs_ref, low_ref, att_ref, hid_ref, act_ref,
        lead_ref, cot_ref, sems,
    ) = refs
    width = lead_ref.shape[1]
    hidden = w1_ref.shape[1]
    places, _ = bundle_places(width, hidden, segments)
    dmix_ref, dproj_ref, dinner_ref, dout_ref = (
        bundle_ref.at[:, places[at][0] : places[at][0] + places[at][1]] for at in range(4, 8)
    )
    copies = [
        pltpu.make_async_copy(src.at[1], dst, sems.at[i])
        for i, (src, dst) in enumerate(
            [(aw_hbm, aw_ref), (pw_hbm, pw_ref), (w1_hbm, w1_ref), (w2_hbm, w2_ref)]
        )
    ]
    for copy in copies:
        copy.start()
    total = lead_ref.shape[0]
    scale = 1.0 / math.sqrt(HEAD)

    def row(ref):
        return ref[1:2, :].astype(F32)

    me = lax.axis_index("seg")
    for at, piece in enumerate(pieces):
        for half in range(2):
            seg = me ^ (2 * at + half)
            for doc in range(docs):
                place = pl.ds(doc * segments + seg, 1)
                lead_ref[place, :] = piece[2 * half, doc : doc + 1, :].astype(F32)
                cot_ref[place, :] = piece[2 * half + 1, doc : doc + 1, :].astype(F32)
    rows = lead_ref[...] + jnp.concatenate([pos_ref[...].astype(F32)] * docs, axis=0)
    rows_low = rows.astype(LOW)
    low_ref[...] = rows_low
    both_heads = (total, 2 * total)
    key = lax.broadcasted_iota(jnp.int32, both_heads, 0)
    query = lax.broadcasted_iota(jnp.int32, both_heads, 1) % total
    key_doc = key // segments
    reach = jnp.zeros(both_heads, jnp.int32)
    for doc in range(docs):
        reach = jnp.where(key_doc == doc, len_ref[doc], reach)
    valid = (key_doc == query // segments) & ((key - key_doc * segments) * length < reach)
    lane, first, second = head_masks()

    later_row = lax.broadcasted_iota(jnp.int32, (length, 1), 0) > 0
    seg_gain = g2_ref[0:1, :].astype(F32)
    seg_sums = [jnp.zeros((1, width), F32)] * 3
    for at in range(0, seg_cot_ref.shape[0], length):
        span = slice(at, at + length)
        upper = jnp.where(later_row, seg_cot_ref[span, :].astype(F32), 0.0)
        normed = seg_normed_ref[span, :].astype(F32)
        branch = norm_back(upper, seg_gain, normed, seg_rstd_ref[span, 0:1]).astype(LOW)
        seg_branch_ref[span, :] = branch
        for which, item in enumerate((upper * normed, upper, branch.astype(F32))):
            seg_sums[which] = seg_sums[which] + colsum(item)
    seg_sums_ref[...] = jnp.concatenate(seg_sums + [jnp.zeros((5, width), F32)], axis=0)

    copies[0].wait()
    queries = (dot(rows_low, aw_ref[:, :width]) + row(qb_ref)).astype(LOW)
    keys = dot(rows_low, aw_ref[:, width : 2 * width]).astype(LOW)
    values = (dot(rows_low, aw_ref[:, 2 * width :]) + row(vb_ref)).astype(LOW)

    def stacked(both):
        return jnp.concatenate([both * first, both * second], axis=0)

    def picked(both):
        return jnp.where(lane < HEAD, both[:total], both[total:])

    pair_cols = [slice(at, at + PAIR) for at in range(0, width, PAIR)]
    query_both = [stacked(queries[:, cols]) for cols in pair_cols]
    scores = [dot_rt(keys[:, cols], both) for cols, both in zip(pair_cols, query_both)]
    probs_low = []
    for pair, item in enumerate(scores):
        item = jnp.where(valid, item * scale, NEG)
        weights = jnp.exp(item - jnp.max(item, axis=0, keepdims=True))
        probs = weights / jnp.sum(weights, axis=0, keepdims=True)
        probs_ref[pair] = probs
        probs_low.append(probs.astype(LOW))
    for cols, item in zip(pair_cols, probs_low):
        att_ref[:, cols] = picked(dot_lt(item, values[:, cols])).astype(LOW)
    copies[1].wait()
    resid = rows + dot(att_ref[...], pw_ref[...]) + row(pb_ref)
    normed_one, rstd_one = normalize(resid)
    hidden = normed_one * row(g1_ref) + row(s1_ref)
    hidden_low = hidden.astype(LOW)
    hid_ref[...] = hidden_low
    copies[2].wait()
    copies[3].wait()
    count = w1_ref.shape[1] // TILE
    branch = jnp.zeros((total, width), F32)
    for at in range(count):
        cols = slice(at * TILE, (at + 1) * TILE)
        active, slope = gelu_and_slope(dot(hidden_low, w1_ref[:, cols]) + b1_ref[1:2, cols].astype(F32))
        inner_ref[:, cols] = slope
        active = active.astype(LOW)
        act_ref[:, cols] = active
        branch += dot(active, w2_ref[cols, :])
    normed_two, rstd_two = normalize(hidden + branch + row(b2_ref))
    out_ref[...] = normed_two * row(g2_ref) + row(s2_ref)

    upper = cot_ref[...]
    sums = [colsum(upper * normed_two), colsum(upper)]
    resid_two = norm_back(upper, row(g2_ref), normed_two, rstd_two)
    branch_two = resid_two.astype(LOW)
    dout_ref[...] = branch_two
    hidden_grad = resid_two
    for at in range(count):
        cols = slice(at * TILE, (at + 1) * TILE)
        inner_grad = (dot_rt(branch_two, w2_ref[cols, :]) * inner_ref[:, cols]).astype(LOW)
        dinner_ref[:, cols] = inner_grad
        hidden_grad += dot_rt(inner_grad, w1_ref[:, cols])
    sums = [colsum(hidden_grad * normed_one), colsum(hidden_grad)] + sums
    resid_one = norm_back(hidden_grad, row(g1_ref), normed_one, rstd_one)
    branch_one = resid_one.astype(LOW)
    dproj_ref[...] = branch_one
    att_grad = dot_rt(branch_one, pw_ref[...]).astype(LOW)
    att_both = [stacked(att_grad[:, cols]) for cols in pair_cols]
    prob_grads = [dot_rt(values[:, cols], both) for cols, both in zip(pair_cols, att_both)]
    score_grads = []
    for pair, prob_grad in enumerate(prob_grads):
        probs = probs_ref[pair]
        score_grad = probs * (prob_grad - jnp.sum(prob_grad * probs, axis=0, keepdims=True))
        score_grads.append(score_grad.astype(LOW))
    for pair, cols in enumerate(pair_cols):
        cols_k, cols_v = (slice(cols.start + at * width, cols.stop + at * width) for at in (1, 2))
        dmix_ref[:, cols] = (picked(dot_lt(score_grads[pair], keys[:, cols])) * scale).astype(LOW)
        dmix_ref[:, cols_k] = (dot(score_grads[pair], query_both[pair]) * scale).astype(LOW)
        dmix_ref[:, cols_v] = dot(probs_ref[pair].astype(LOW), att_both[pair]).astype(LOW)
    back = resid_one + dot_rt(dmix_ref[...], aw_ref[...])
    back_ref[...] = back
    seg = lax.axis_index("seg")

    def own(value, slot):
        step = value.shape[1] // segments
        return pltpu.roll(value.astype(F32), lax.rem(value.shape[1] - seg * step, value.shape[1]), 1)[:, :slot]

    for at, item in enumerate((low_ref, att_ref, hid_ref, act_ref)):
        start, slot = places[at]
        bundle_ref[:, start : start + slot] = own(item[...], slot).astype(LOW)
    start, slot = places[8]
    by_segment = back[:segments]
    for doc in range(1, docs):
        by_segment += back[doc * segments : (doc + 1) * segments]
    pieces = [own(jnp.concatenate(sums + [jnp.zeros((4, width), F32)], axis=0), slot), own(by_segment, slot)]
    rest = total - 8 - segments
    if rest:
        pieces.append(jnp.zeros((rest, slot), F32))
    bundle_ref[:, start : start + slot] = jnp.concatenate(pieces, axis=0).astype(LOW)


def cross_block(
    pieces, position, doc_length, seg_len,
    attn_weight, query_bias, value_bias, proj_weight, proj_bias, g1, s1,
    inner_weight, inner_bias, outer_weight, outer_bias, g2, s2, seg_cots, seg_normed, seg_rstd,
):
    segments, width = position.shape
    docs = pieces[0].shape[1]
    total = docs * segments
    hidden = inner_weight.shape[2]
    vmem = pl.BlockSpec(memory_space=pltpu.VMEM)
    hbm = pl.BlockSpec(memory_space=pl.ANY)

    def shape(columns, dtype=LOW):
        return jax.ShapeDtypeStruct((total, columns), dtype)

    return pl.pallas_call(
        functools.partial(cross_kernel, docs, segments, seg_len),
        in_specs=[pl.BlockSpec(memory_space=pltpu.SMEM)] + [vmem] * (len(pieces) + 13) + [hbm] * 4,
        out_specs=[vmem] * 5,
        out_shape=[
            shape(width, F32),
            shape(width, F32),
            shape(bundle_places(width, hidden, segments)[1]),
            jax.ShapeDtypeStruct(seg_cots.shape, LOW),
            jax.ShapeDtypeStruct((8, width), F32),
        ],
        scratch_shapes=[
            pltpu.VMEM((width, 3 * width), LOW),
            pltpu.VMEM((width, width), LOW),
            pltpu.VMEM((width, hidden), LOW),
            pltpu.VMEM((hidden, width), LOW),
            pltpu.VMEM((total, hidden), F32),
            pltpu.VMEM((HEADS // 2, total, 2 * total), F32),
            pltpu.VMEM((total, width), LOW),
            pltpu.VMEM((total, width), LOW),
            pltpu.VMEM((total, width), LOW),
            pltpu.VMEM((total, hidden), LOW),
            pltpu.VMEM((total, width), F32),
            pltpu.VMEM((total, width), F32),
            pltpu.SemaphoreType.DMA((4,)),
        ],
        compiler_params=params(),
        cost_estimate=cost(4 * total * width * (4 * width + 2 * hidden) * 2, 2 * width * (4 * width + 2 * hidden)),
        name="cross_block",
    )(
        doc_length, *pieces, position, query_bias, value_bias, proj_bias, g1, s1,
        inner_bias, outer_bias, g2, s2, seg_cots, seg_normed, seg_rstd,
        attn_weight, proj_weight, inner_weight, outer_weight,
    )


def top_kernel(
    segments, back_ref, cross_ref, low_ref, normed_ref, rstd_ref, g2_ref, first_sums_ref, branch_ref, active_ref,
    sums_ref, sent_ref, kept_ref, patched_ref, branch_out_ref, swap_ref,
):
    step = pl.program_id(0)
    docs, length, width = branch_ref.shape
    half = width // 2

    @pl.when(step == 0)
    def _():
        core = lax.axis_index("docs") % 2
        seg = lax.axis_index("seg")
        first_row = lax.broadcasted_iota(jnp.int32, (low_ref.shape[1], 1), 0) == 0

        def own(ref):
            return jnp.concatenate([ref[pl.ds(doc * segments + seg, 1), :] for doc in range(docs)], axis=0)

        upper = own(back_ref)
        normed = normed_ref[:, 0, :].astype(F32)
        branch = norm_back(upper, g2_ref[0:1, :].astype(F32), normed, rstd_ref[:, 0, 0:1]).astype(LOW).astype(F32)
        for at, item in enumerate((upper * normed, upper, branch)):
            sums_ref[at : at + 1, :] = first_sums_ref[at : at + 1, :] + colsum(item)
        sums_ref[3:8, :] = jnp.zeros((5, width), F32)
        cross = own(cross_ref)
        top_rows = low_ref.shape[1]
        for doc in range(docs):
            patched_ref[doc] = jnp.where(first_row, cross[doc : doc + 1, :], low_ref[doc].astype(F32)).astype(LOW)
            top_part = jnp.where(first_row, branch[doc : doc + 1, :], branch_ref[doc, :top_rows, :].astype(F32))
            top_part = top_part.astype(LOW)
            branch_out_ref[doc] = top_part
            rows = slice(doc * length, (doc + 1) * length)
            whole_part = jnp.concatenate([top_part, branch_ref[doc, top_rows:, :]], axis=0)
            left, right = whole_part[:, :half], whole_part[:, half:]
            swap_ref[rows, :half] = jnp.where(core == 0, right, left)
            swap_ref[rows, half:] = jnp.where(core == 0, left, right)

    grad = dot_lt(active_ref[...], swap_ref[...]).astype(LOW)
    sent_ref[...] = grad[:, :half]
    kept_ref[...] = grad[:, half:]


def top_back(back, cross_out, seg_low, seg_len, normed, rstd, g2, sums, branch, active):
    total, width = branch.shape
    hidden = active.shape[1]
    docs = total // seg_len
    first = (docs, 16, width)
    by_doc = (docs, seg_len, width)
    out = pl.pallas_call(
        functools.partial(top_kernel, back.shape[0] // docs),
        grid=(hidden // TILE,),
        in_specs=[
            whole(back.shape),
            whole(back.shape),
            whole(first),
            whole(first),
            whole((docs, 8, 128)),
            whole((2, width)),
            whole((8, width)),
            whole(by_doc),
            pl.BlockSpec((total, TILE), lambda i: (0, i)),
        ],
        out_specs=[
            whole((8, width)),
            pl.BlockSpec((TILE, width // 2), lambda i: (i, 0)),
            pl.BlockSpec((TILE, width // 2), lambda i: (i, 0)),
            whole(first),
            whole(first),
        ],
        out_shape=[
            jax.ShapeDtypeStruct((8, width), F32),
            jax.ShapeDtypeStruct((hidden, width // 2), LOW),
            jax.ShapeDtypeStruct((hidden, width // 2), LOW),
            jax.ShapeDtypeStruct(by_doc, LOW),
            jax.ShapeDtypeStruct(by_doc, LOW),
        ],
        input_output_aliases={2: 3, 7: 4},
        scratch_shapes=[pltpu.VMEM((total, width), LOW)],
        compiler_params=params(),
        cost_estimate=cost(),
        name="top_back",
    )(
        back, cross_out, seg_low.reshape(by_doc), normed.reshape(by_doc), rstd.reshape(docs, seg_len, 128), g2, sums,
        branch.reshape(by_doc), active,
    )
    return out[0], out[1], out[2], out[3], out[4].reshape(total, width)


def middle_step(branch_ref, low_ref, slope_ref, w1_ref, w2_ref, acc_ref, bias_ref, grad_ref, finished=None):
    parts = []
    chunks = [slice(at, at + CHUNK) for at in range(0, branch_ref.shape[0], CHUNK)]
    following = dot_rt(branch_ref[chunks[0], :], w2_ref[0])
    for at, rows in enumerate(chunks):
        part = (following * slope_ref[rows, :].astype(F32)).astype(LOW)
        if at + 1 < len(chunks):
            following = dot_rt(branch_ref[chunks[at + 1], :], w2_ref[0])
        total = acc_ref[rows, :] + dot_rt(part, w1_ref[0])
        if finished:
            finished(rows, total)
        else:
            acc_ref[rows, :] = total
        parts.append(part)
    inner_grad = jnp.concatenate(parts, axis=0)
    bias_ref[...] = jnp.broadcast_to(colsum(inner_grad.astype(F32)), bias_ref.shape)
    grad_ref[...] = dot_lt(low_ref[...], inner_grad).astype(LOW)


def middle_first_kernel(core_ref, branch_ref, low_ref, slope_ref, w1_ref, w2_ref, *refs):
    half_ref, bias_ref, sent_ref, acc_ref = refs[-4:]
    step = pl.program_id(0)
    last = pl.num_programs(0) - 1

    @pl.when(step == 0)
    def _():
        acc_ref[...] = jnp.zeros_like(acc_ref)

    def finished(rows, total):
        half_ref[rows, :] = total.astype(LOW)

    operands = (branch_ref, low_ref, slope_ref, w1_ref, w2_ref, acc_ref, bias_ref, sent_ref)
    pl.when(step < last)(lambda: middle_step(*operands))
    pl.when(step == last)(lambda: middle_step(*operands, finished))


def middle_last_kernel(core_ref, branch_ref, low_ref, slope_ref, w1_ref, w2_ref, g1_ref, *refs):
    half_hbm, normed_hbm, rstd_hbm = refs[:3]
    branch1_ref, sums_ref, bias_ref, kept_ref, acc_ref, half_ref, normed_ref, rstd_ref, sems = refs[-9:]
    step = pl.program_id(0)
    last = pl.num_programs(0) - 1
    width = branch_ref.shape[1]
    copies = [
        pltpu.make_async_copy(source, target, sems.at[at])
        for at, (source, target) in enumerate(
            ((half_hbm, half_ref), (normed_hbm, normed_ref), (rstd_hbm, rstd_ref))
        )
    ]

    @pl.when(step == 0)
    def _():
        for copy in copies:
            copy.start()
        acc_ref[...] = jnp.zeros_like(acc_ref)

    sums = [jnp.zeros((1, width), F32)] * 3

    def finished(rows, total):
        hidden_grad = total + half_ref[rows, :].astype(F32) + branch_ref[rows, :].astype(F32)
        normed = normed_ref[rows, :].astype(F32)
        resid = norm_back(hidden_grad, g1_ref[0:1, :].astype(F32), normed, rstd_ref[rows, 0:1])
        branch = resid.astype(LOW)
        branch1_ref[rows, :] = branch
        for at, item in enumerate((hidden_grad * normed, hidden_grad, branch.astype(F32))):
            sums[at] = sums[at] + colsum(item)

    operands = (branch_ref, low_ref, slope_ref, w1_ref, w2_ref, acc_ref, bias_ref, kept_ref)
    pl.when(step < last)(lambda: middle_step(*operands))

    @pl.when(step == last)
    def _():
        for copy in copies:
            copy.wait()
        middle_step(*operands, finished)
        sums_ref[...] = jnp.concatenate(sums + [jnp.zeros((5, width), F32)], axis=0)


def half_order(steps):
    half = steps // 2

    def pick(step, core_ref):
        return jnp.where(step < half, 1 - core_ref[0], core_ref[0]) * half + step % half

    return pick


def middle_specs(total, width, steps, offset):
    pick = half_order(2 * steps)
    return [
        whole((total, width)),
        whole((total, width)),
        pl.BlockSpec((total, TILE), lambda i, c: (0, pick(i + offset, c))),
        pl.BlockSpec((1, width, TILE), lambda i, c: (0, 0, pick(i + offset, c))),
        pl.BlockSpec((1, TILE, width), lambda i, c: (0, pick(i + offset, c), 0)),
    ]


def middle_first(core, branch, low, slope, inner_weight, outer_weight, tokens=()):
    total, width = branch.shape
    steps = slope.shape[1] // TILE // 2
    return pl.pallas_call(
        middle_first_kernel,
        grid_spec=pltpu.PrefetchScalarGridSpec(
            num_scalar_prefetch=1,
            grid=(steps,),
            in_specs=middle_specs(total, width, steps, 0) + token_specs(tokens),
            out_specs=[
                whole((total, width)),
                pl.BlockSpec((8, TILE), lambda i, c: (0, i)),
                pl.BlockSpec((width, TILE), lambda i, c: (0, i)),
            ],
            scratch_shapes=[pltpu.VMEM((total, width), F32)],
        ),
        out_shape=[
            jax.ShapeDtypeStruct((total, width), LOW),
            jax.ShapeDtypeStruct((8, steps * TILE), F32),
            jax.ShapeDtypeStruct((width, steps * TILE), LOW),
        ],
        compiler_params=params(),
        cost_estimate=cost(),
        name="middle_first",
    )(core, branch, low, slope, inner_weight, outer_weight, *tokens)


def middle_last(core, branch, low, slope, inner_weight, outer_weight, g1, half, normed, rstd, tokens=()):
    total, width = branch.shape
    steps = slope.shape[1] // TILE // 2
    return pl.pallas_call(
        middle_last_kernel,
        grid_spec=pltpu.PrefetchScalarGridSpec(
            num_scalar_prefetch=1,
            grid=(steps,),
            in_specs=middle_specs(total, width, steps, steps)
            + [whole((2, width))]
            + token_specs((half, normed, rstd) + tuple(tokens)),
            out_specs=[
                whole((total, width)),
                whole((8, width)),
                pl.BlockSpec((8, TILE), lambda i, c: (0, i)),
                pl.BlockSpec((width, TILE), lambda i, c: (0, i)),
            ],
            scratch_shapes=[
                pltpu.VMEM((total, width), F32),
                pltpu.VMEM((total, width), LOW),
                pltpu.VMEM((total, width), LOW),
                pltpu.VMEM((total, 128), F32),
                pltpu.SemaphoreType.DMA((3,)),
            ],
        ),
        out_shape=[
            jax.ShapeDtypeStruct((total, width), LOW),
            jax.ShapeDtypeStruct((8, width), F32),
            jax.ShapeDtypeStruct((8, steps * TILE), F32),
            jax.ShapeDtypeStruct((width, steps * TILE), LOW),
        ],
        compiler_params=params(),
        cost_estimate=cost(),
        name="middle_last",
    )(core, branch, low, slope, inner_weight, outer_weight, g1, half, normed, rstd, *tokens)


def attend_back_kernel(groups, length, *refs):
    len_ref, branch_ref, qkv_ref, w_ref, pw_ref = refs[:5]
    dmix_ref, back_ref, sums_ref = refs[-3:]
    step = pl.program_id(0)
    start = lax.axis_index("seg") * length
    width = branch_ref.shape[1]
    scale = LOW(1.0 / math.sqrt(HEAD))
    att_grad = dot_rt(branch_ref[...], pw_ref[0]).astype(LOW)
    lane, first, second = head_masks()
    key_row = lax.broadcasted_iota(jnp.int32, (length, 1), 0)

    def stacked(both):
        return jnp.concatenate([both * first, both * second], axis=0)

    places = []
    for group in range(groups):
        count = jnp.clip(len_ref[step * groups + group] - start, 1, length)
        rows = slice(group * length, (group + 1) * length)
        for at in range(0, width, PAIR):
            cols, cols_k, cols_v = (slice(at + part * width, at + part * width + PAIR) for part in range(3))
            places.append((rows, cols, cols_k, cols_v, key_row < count))
    queries = [stacked(qkv_ref[rows, cols] * scale) for rows, cols, _, _, _ in places]
    att_both = [stacked(att_grad[rows, cols]) for rows, cols, _, _, _ in places]
    scores = [dot_rt(qkv_ref[rows, cols_k], item) for item, (rows, _, cols_k, _, _) in zip(queries, places)]
    prob_grads = [dot_rt(qkv_ref[rows, cols_v], item) for item, (rows, _, _, cols_v, _) in zip(att_both, places)]
    probs, score_grads = [], []
    for item, prob_grad, (_, _, _, _, valid) in zip(scores, prob_grads, places):
        item = jnp.where(valid, item, NEG)
        weights = jnp.exp(item - jnp.max(item, axis=0, keepdims=True))
        prob = weights * (1.0 / jnp.sum(weights, axis=0, keepdims=True))
        score_grad = prob * (prob_grad - jnp.sum(prob_grad * prob, axis=0, keepdims=True))
        probs.append(prob.astype(LOW))
        score_grads.append(score_grad.astype(LOW))
    for at, (rows, cols, cols_k, cols_v, _) in enumerate(places):
        by_query = dot_lt(score_grads[at], qkv_ref[rows, cols_k] * scale)
        dmix_ref[rows, cols] = jnp.where(lane < HEAD, by_query[:length], by_query[length:]).astype(LOW)
        dmix_ref[rows, cols_k] = dot(score_grads[at], queries[at]).astype(LOW)
        dmix_ref[rows, cols_v] = dot(probs[at], att_both[at]).astype(LOW)
    mixed = dmix_ref[...]
    back_ref[...] = branch_ref[...].astype(F32) + dot_rt(mixed, w_ref[0])

    @pl.when(step == 0)
    def _():
        sums_ref[...] = jnp.zeros_like(sums_ref)

    sums_ref[0:1, :] += colsum(mixed[:, :width].astype(F32))
    sums_ref[1:2, :] += colsum(mixed[:, 2 * width :].astype(F32))


def attend_back(branch, qkv, doc_length, seg_len, attn_weight, proj_weight, tokens=()):
    total, width = branch.shape
    groups = 2
    size = groups * seg_len
    return pl.pallas_call(
        functools.partial(attend_back_kernel, groups, seg_len),
        grid=(total // size,),
        in_specs=[
            pl.BlockSpec(memory_space=pltpu.SMEM),
            pl.BlockSpec((size, width), lambda i: (i, 0)),
            pl.BlockSpec((size, 3 * width), lambda i: (i, 0)),
            of_block(0, (width, 3 * width)),
            of_block(0, (width, width)),
        ]
        + token_specs(tokens),
        out_specs=[
            pl.BlockSpec((size, 3 * width), lambda i: (i, 0)),
            pl.BlockSpec((size, width), lambda i: (i, 0)),
            whole((8, width)),
        ],
        out_shape=[
            jax.ShapeDtypeStruct((total, 3 * width), LOW),
            jax.ShapeDtypeStruct((total, width), F32),
            jax.ShapeDtypeStruct((8, width), F32),
        ],
        compiler_params=params(),
        cost_estimate=cost(
            2 * total * width * 4 * width + 20 * total * seg_len * width, 20 * MIB, total * seg_len * HEADS
        ),
        name="attend_back",
    )(doc_length, branch, qkv, attn_weight, proj_weight, *tokens)


def last_grads_kernel(core_ref, rows_ref, att_ref, mixed_ref, branch_ref, *refs):
    left, right = refs[-2:]
    third = branch_ref.shape[1]
    turned = rows_ref[...].T
    left[:, :third] = dot(turned, mixed_ref[:, :third]).astype(LOW)
    right[...] = dot(turned, mixed_ref[:, third:]).astype(LOW)
    left[:, third:] = dot_lt(att_ref[...], branch_ref[...]).astype(LOW)


def last_grads(core, rows, attended, mixed, branch, tokens=()):
    total, width = rows.shape
    out = jax.ShapeDtypeStruct((width, width), LOW)
    return pl.pallas_call(
        last_grads_kernel,
        grid_spec=pltpu.PrefetchScalarGridSpec(
            num_scalar_prefetch=1,
            grid=(width // CHUNK,),
            in_specs=[
                pl.BlockSpec((total, CHUNK), lambda i, c: (0, i)),
                pl.BlockSpec((total, CHUNK), lambda i, c: (0, i)),
                pl.BlockSpec((total, mixed.shape[1] // 2), lambda i, c: (0, c[0])),
                pl.BlockSpec((total, width // 2), lambda i, c: (0, c[0])),
            ]
            + token_specs(tokens),
            out_specs=[pl.BlockSpec((CHUNK, width), lambda i, c: (i, 0))] * 2,
        ),
        out_shape=[out] * 2,
        compiler_params=params(),
        cost_estimate=cost(),
        name="last_grads",
    )(core, rows, attended, mixed, branch, *tokens)


def bits_of(axis):
    return lax.axis_size(axis).bit_length() - 1


def partner(value, axis, bit):
    return flipped(value, axis, 1 << bit)


def flipped(value, axis, mask):
    return lax.ppermute(value, axis, [(i, i ^ mask) for i in range(lax.axis_size(axis))])


def my_bit(axis, bit):
    return (lax.axis_index(axis) >> bit) & 1


def first_rows_pieces(value):
    pair = jnp.concatenate([value, partner(value, "seg", 0)], axis=0)
    return [pair] + [flipped(pair, "seg", flip) for flip in range(2, lax.axis_size("seg"), 2)]


class Job:
    def __init__(self, blocks, columns):
        self.blocks = blocks
        self.columns = columns
        self.operands = []
        self.parts = []

    def add(self, array, place):
        self.operands.append((array, place))
        return len(self.operands) - 1

    def rows(self):
        return sum(rows for rows, _ in self.parts)


def joined(first, second):
    job = Job(first.blocks, first.columns)
    job.operands = first.operands + second.operands
    shift = len(first.operands)
    job.parts = first.parts + [
        (rows, [(at + shift, start) for at, start in addends]) for rows, addends in second.parts
    ]
    return job


def run_kernel(jobs, skip, *refs):
    count = sum(len(job.operands) for job in jobs)
    sources = refs[skip : skip + count]
    outs = refs[skip + count : skip + count + len(jobs)]
    buffers = refs[skip + count + len(jobs) : -len(jobs) - 2]
    ready = refs[-len(jobs) - 2 : -2]
    in_sems, out_sems = refs[-2:]
    arriving, leaving = [], []
    at = sem = 0
    for job in jobs:
        copies = []
        for _, place in job.operands:
            lead, part = place()
            copies.append(
                [
                    pltpu.make_async_copy(sources[at].at[i, lead, part], buffers[at].at[i], in_sems.at[sem + i])
                    for i in range(job.blocks)
                ]
            )
            at += 1
            sem += job.blocks
        for i in range(job.blocks):
            for copy in copies:
                copy[i].start()
        arriving.append(copies)
    at = sem = 0
    for job, copies, out, value in zip(jobs, arriving, outs, ready):
        mine = buffers[at : at + len(job.operands)]
        at += len(job.operands)
        for i in range(job.blocks):
            for copy in copies:
                copy[i].wait()
            start = 0
            for rows, addends in job.parts:
                total = None
                for which, first in addends:
                    item = mine[which][i, first : first + rows, :].astype(F32)
                    total = item if total is None else total + item
                value[i, start : start + rows, :] = total.astype(LOW)
                start += rows
            leaving.append(pltpu.make_async_copy(value.at[i], out.at[i], out_sems.at[sem]))
            leaving[-1].start()
            sem += 1
    for copy in leaving:
        copy.wait()


def run(jobs, tokens=()):
    operands = [array for job in jobs for array, _ in job.operands]
    buffers = [pltpu.VMEM((job.blocks,) + array.shape[3:], LOW) for job in jobs for array, _ in job.operands]
    ready = [pltpu.VMEM((job.blocks, job.rows(), job.columns), LOW) for job in jobs]
    arrivals = sum(job.blocks * len(job.operands) for job in jobs)
    return pl.pallas_call(
        functools.partial(run_kernel, jobs, len(tokens)),
        in_specs=token_specs(tokens) + token_specs(operands),
        out_specs=token_specs(jobs),
        out_shape=[jax.ShapeDtypeStruct((job.blocks, job.rows(), job.columns), LOW) for job in jobs],
        scratch_shapes=buffers
        + ready
        + [pltpu.SemaphoreType.DMA((arrivals,)), pltpu.SemaphoreType.DMA((sum(job.blocks for job in jobs),))],
        compiler_params=params(),
        cost_estimate=cost(),
        name="pick",
    )(*tokens, *operands)


def gate_kernel(*_):
    pass


def gated(values, tokens):
    count = len(values)
    return pl.pallas_call(
        gate_kernel,
        in_specs=token_specs(values) + token_specs(tokens),
        out_specs=token_specs(values),
        out_shape=[jax.ShapeDtypeStruct(item.shape, item.dtype) for item in values],
        input_output_aliases={at: at for at in range(count)},
        cost_estimate=cost(),
        name="gate",
    )(*values, *tokens)


class Flow:
    def __init__(self, groups):
        self.groups = groups
        self.received = []
        self.seg_done = 0
        self.docs_done = []
        self.shards = groups[0][0].shape[0]
        self.columns = groups[0][0].shape[2]

    def job(self, blocks, lead, shift, last):
        docs_done = list(self.docs_done)
        level = len(docs_done) + (last is not None)
        job = Job(blocks, self.columns)

        def add(array, seg_done, docs_level):
            choices = 1 << (level - docs_level)
            rows = array.shape[1] // choices

            def place():
                part = 0
                for bit in [my_bit("docs", bit) for bit in docs_done][docs_level:] + ([last()] if last else []):
                    part = part * 2 + bit
                return lead() >> seg_done, part

            return rows, job.add(array.reshape(blocks, 1 << (shift - seg_done), choices, rows, self.columns), place)

        shares = 1 << (bits_of("docs") - 1 - level) if len(self.groups) > 1 else 1
        added = [[add(array, 0, 0) for array in group] for group in self.groups]
        for share in range(shares):
            for group in added:
                rows = group[0][0] // shares
                job.parts.append((rows, [(at, share * rows) for _, at in group]))
        for array, seg_done, docs_level in self.received:
            _, at = add(array, seg_done, docs_level)
            start = 0
            for rows, addends in job.parts:
                addends.append((at, start))
                start += rows
        return job

    def seg_job(self):
        bit = self.seg_done

        def lead():
            return (lax.axis_index("seg") & ((1 << bit) - 1)) | ((1 - my_bit("seg", bit)) << bit)

        job = self.job(self.shards >> (bit + 1), lead, bit + 1, None)
        self.seg_done += 1
        self.waiting = ("seg", bit)
        return job

    def docs_job(self, bit):
        done = self.seg_done

        def lead():
            return lax.axis_index("seg") & ((1 << done) - 1)

        job = self.job(self.shards >> done, lead, done, lambda: 1 - my_bit("docs", bit))
        self.docs_done.append(bit)
        self.waiting = ("docs", bit)
        return job

    def settle_job(self):
        return self.job(1, lambda: lax.axis_index("seg"), bits_of("seg"), None)

    def send(self, value):
        axis, bit = self.waiting
        self.received.append((partner(value, axis, bit), self.seg_done, len(self.docs_done)))

    def further(self, bits, tokens=()):
        while self.seg_done < bits:
            (value,) = run([self.seg_job()], tokens)
            self.send(value)


def finish_kernel(groups, outputs, small_at, *refs):
    me = lax.axis_index("docs")
    outs = refs[-outputs:]
    for first, count, reduce_x, span, cuts in groups:
        pieces = refs[first : first + count]
        rows = span[1] - span[0]

        def piece(target):
            value = pieces[0][span[0] : span[1], :].astype(F32)
            for flip in range(1, count):
                value = jnp.where(
                    (me & (count - 1)) ^ flip == target, pieces[flip][span[0] : span[1], :].astype(F32), value
                )
            return value

        for core in range(2):
            parts = [piece(2 * x + core) for x in range(count // 2)]
            if reduce_x:
                total = parts[0]
                for part in parts[1:]:
                    total = total + part
                parts = [total]
            for x, part in enumerate(parts):
                place = slice(x * rows, (x + 1) * rows)
                for which, start, end, at in cuts:
                    out = outs[which]
                    base = core * (out.shape[2] // 2) + at
                    out[0, place, base : base + end - start] = part[:, start:end]
    if small_at is None:
        return
    first, count, _, span, _ = groups[-1]
    pieces = refs[first : first + count]
    bias_ref, wide_ref, norm_ref = refs[first + count : first + count + 3]
    total = []
    for x in range(count // 2):
        value = pieces[0][span[1] :, :].astype(F32)
        for flip in range(2, count, 2):
            value = jnp.where((me ^ flip) >> 1 == x, pieces[flip][span[1] :, :].astype(F32), value)
        total.append(value)
    total = jnp.concatenate(total, axis=0)
    below = [(bias_ref, at) for at in range(4)] + [(norm_ref, at) for at in range(4)] + [(wide_ref, 0)]
    for row, (ref, at) in enumerate(below):
        out = outs[small_at + row]
        size = out.shape[1]
        out[0:1, :] = total[row : row + 1, :size]
        out[1:2, :] = ref[at : at + 1, :size]


def docs_pieces(value, count=None):
    pieces = []
    for flip in range(0, count or lax.axis_size("docs"), 2):
        pieces.append(flipped(value, "docs", flip) if flip else value)
        pieces.append(partner(pieces[-1], "docs", 0))
    return pieces


def finish(groups, outputs, small=None, tokens=()):
    operands, layout, seen = [], [], {}
    for pieces, reduce_x, span, cuts in groups:
        if id(pieces) not in seen:
            seen[id(pieces)] = len(operands)
            operands += pieces
        layout.append((seen[id(pieces)], len(pieces), reduce_x, span, cuts))
    out_specs = [pl.BlockSpec((1,) + item.shape[1:], lambda i: (0, 0, 0)) for item in outputs]
    out_shape = [jax.ShapeDtypeStruct(item.shape, F32) for item in outputs]
    if small:
        operands += small[0]
        out_specs += [whole((2, size)) for size in small[1]]
        out_shape += [jax.ShapeDtypeStruct((2, size), F32) for size in small[1]]
    count = len(operands)
    return pl.pallas_call(
        functools.partial(finish_kernel, layout, len(out_shape), len(outputs) if small else None),
        grid=(1,),
        in_specs=[whole(item.shape) for item in operands] + token_specs(outputs) + token_specs(tokens),
        out_specs=out_specs,
        out_shape=out_shape,
        input_output_aliases={count + at: at for at in range(len(outputs))},
        compiler_params=params(),
        cost_estimate=cost(),
        name="finish",
    )(*operands, *outputs, *tokens)


def small_kernel(low_ref, middle_ref, top_ref, kept_ref, sent_ref, out_ref):
    first = lax.axis_index("docs") % 2 == 0
    out_ref[...] = jnp.zeros_like(out_ref)
    shards, _, _ = out_ref.shape
    part = low_ref.shape[1] // shards
    items = [(low_ref, 0), (low_ref, 1), (middle_ref, 2), (top_ref, 2)]
    items += [(middle_ref, 0), (middle_ref, 1), (top_ref, 0), (top_ref, 1)]
    for shard in range(shards):
        for row, (ref, at) in enumerate(items):
            value = ref[at : at + 1, shard * part : (shard + 1) * part]
            out_ref[shard, row : row + 1, :part] = value.astype(LOW)
        half = shards // 2
        wide = kept_ref.shape[1] // half
        place = slice(shard % half * wide, (shard % half + 1) * wide)
        mine = first if shard < half else jnp.logical_not(first)
        value = jnp.where(mine, kept_ref[0:1, place], sent_ref[0:1, place])
        out_ref[shard, 8:9, :wide] = value.astype(LOW)


def small_rows(low, middle, top, kept, sent, segments):
    width = low.shape[1]
    return pl.pallas_call(
        small_kernel,
        out_shape=jax.ShapeDtypeStruct((segments, 16, width), LOW),
        compiler_params=params(),
        cost_estimate=cost(),
        name="small_rows",
    )(low, middle, top, kept, sent)


def cross_grad_kernel(segments, width, hidden, count, *refs):
    bundles = refs[:count]
    attn_ref, proj_ref, inner_ref, outer_ref, bias_ref, wide_ref, norm_ref, place_ref = refs[-8:]
    places, _ = bundle_places(width, hidden, segments)

    def rows(at):
        start, size = places[at]
        return jnp.concatenate([ref[:, start : start + size] for ref in bundles], axis=0)

    outs = (attn_ref, proj_ref, inner_ref, outer_ref)
    biases = []
    for at, out in enumerate(outs):
        right = rows(4 + at)
        out[0] = dot_lt(rows(at), right)[: out.shape[1]]
        biases.append(colsum(right.astype(F32)))
    seg = lax.axis_index("seg")

    def own(value, slot):
        step = value.shape[1] // segments
        value = jnp.broadcast_to(value, (8, value.shape[1]))
        return pltpu.roll(value, lax.rem(value.shape[1] - seg * step, value.shape[1]), 1)[0:1, :slot]

    slot = places[0][1]
    mixed = biases[0]
    parts = [mixed[:, :width], mixed[:, 2 * width :], biases[1], biases[3]]
    bias_ref[...] = jnp.concatenate([own(part, slot) for part in parts] + [jnp.zeros((4, slot), F32)], axis=0)
    wide_ref[...] = jnp.broadcast_to(own(biases[2], places[3][1]), wide_ref.shape)
    start, size = places[8]
    sums = bundles[0][:, start : start + size].astype(F32)
    for ref in bundles[1:]:
        sums = sums + ref[:, start : start + size].astype(F32)
    norm_ref[...] = sums[:8]
    place_ref[...] = sums[8 : 8 + segments, : place_ref.shape[1]]


def cross_grads(bundles, segments, width, hidden, tokens=()):
    part, wide = width // segments, hidden // segments
    places, _ = bundle_places(width, hidden, segments)
    slot = places[0][1]
    stacked = [(part, 3 * width), (part, width), (part, hidden), (wide, width)]
    plain = [(8, slot), (8, places[3][1]), (8, slot), (segments, part)]
    return pl.pallas_call(
        functools.partial(cross_grad_kernel, segments, width, hidden, len(bundles)),
        grid=(1,),
        in_specs=[whole(bundles[0].shape)] * len(bundles) + token_specs(tokens),
        out_specs=[pl.BlockSpec((1,) + item, lambda i: (1, 0, 0)) for item in stacked]
        + [whole(item) for item in plain],
        out_shape=[jax.ShapeDtypeStruct((2,) + item, F32) for item in stacked]
        + [jax.ShapeDtypeStruct(item, F32) for item in plain],
        compiler_params=params(),
        cost_estimate=cost(),
        name="cross_grads",
    )(*bundles, *tokens)


def on_device(
    tokens,
    doc_length,
    attn_weight,
    query_bias,
    value_bias,
    proj_weight,
    proj_bias,
    norm1_gain,
    norm1_shift,
    inner_weight,
    inner_bias,
    outer_weight,
    outer_bias,
    norm2_gain,
    norm2_shift,
    seg_position,
    cotangent,
):
    docs_here, _, seg_len, width = tokens.shape
    hidden = inner_weight.shape[2]
    segments = lax.axis_size("seg")
    core = (lax.axis_index("docs") % 2).astype(jnp.int32).reshape(1)
    total = docs_here * seg_len
    rows_low = tokens.reshape(total, width)
    cots = cotangent.reshape(total, width)
    seg_bits = bits_of("seg")
    across_bits = list(range(bits_of("docs") - 1, 0, -1))

    qkv, attended, normed_one, hidden_low, rstd_one = attend(
        rows_low, doc_length, seg_len, attn_weight, query_bias, value_bias, proj_weight, proj_bias,
        norm1_gain, norm1_shift,
    )
    ff_weights = (inner_weight, inner_bias, outer_weight, outer_bias, norm2_gain, norm2_shift)
    leaders = lead(hidden_low, cots, docs_here, *ff_weights)
    pieces = first_rows_pieces(leaders)
    active, slope, seg_low, normed_two, rstd_two = feed(hidden_low, *ff_weights)

    cross_out, cross_back, bundle, branch_two, top_sums = cross_block(
        pieces, seg_position, doc_length, seg_len,
        attn_weight, query_bias, value_bias, proj_weight, proj_bias, norm1_gain, norm1_shift,
        inner_weight, inner_bias, outer_weight, outer_bias, norm2_gain, norm2_shift, cots, normed_two, rstd_two,
    )

    bundles = [bundle]
    for bit in across_bits:
        bundles = bundles + [partner(item, "docs", bit) for item in bundles]

    top_sums, outer_sent, outer_kept, layer_out, branch_two = top_back(
        cross_back, cross_out, seg_low, seg_len, normed_two, rstd_two, norm2_gain, top_sums, branch_two, active
    )
    outer_got = partner(outer_sent, "docs", 0)
    half_grad, inner_sums_sent, inner_sent = middle_first(
        core, branch_two, hidden_low, slope, inner_weight, outer_weight
    )

    def sharded(value):
        return value.reshape(segments, -1, value.shape[-1])

    outer = Flow([[sharded(outer_kept), sharded(outer_got)]])
    (outer_next,) = run([outer.seg_job()], (inner_sent,))
    outer.send(outer_next)
    inner_got = partner(inner_sent, "docs", 0)
    branch_one, mid_sums, inner_sums_kept, inner_kept = middle_last(
        core, branch_two, hidden_low, slope, inner_weight, outer_weight, norm1_gain,
        half_grad, normed_one, rstd_one, (outer_next,),
    )
    inner = Flow([[sharded(inner_kept), sharded(inner_got)]])
    for bit in across_bits:
        (inner_next,) = run([inner.docs_job(bit)])
        inner.send(inner_next)
    mixed_grad, input_grad, low_sums = attend_back(
        branch_one, qkv, doc_length, seg_len, attn_weight, proj_weight, (inner_next,) + tuple(bundles[1:])
    )
    input_grad = input_grad.reshape(tokens.shape)
    others = [partner(item, "docs", 0) for item in bundles]
    left_sent, right_sent = last_grads(1 - core, rows_low, attended, mixed_grad, branch_one)
    for bit in across_bits[:-1]:
        (outer_next,) = run([outer.docs_job(bit)], (left_sent,))
        outer.send(outer_next)
    outer_next, inner_next = run([outer.docs_job(across_bits[-1]), inner.seg_job()], (left_sent, *others))
    outer.send(outer_next)
    inner.send(inner_next)
    bundles = bundles + others
    small = small_rows(low_sums, mid_sums, top_sums, inner_sums_kept, inner_sums_sent, segments)
    left_sent, right_sent, small = gated((left_sent, right_sent, small), (outer_next, inner_next))
    left_got, right_got, small_got = (partner(item, "docs", 0) for item in (left_sent, right_sent, small))
    left_kept, right_kept = last_grads(core, rows_low, attended, mixed_grad, branch_one, (left_sent,))
    attn_out, proj_out, inner_out, outer_out, cross_bias, cross_wide, cross_norm, position_grad = cross_grads(
        bundles, segments, width, hidden, (left_kept,)
    )
    left = Flow([[sharded(left_kept), sharded(left_got)]])
    right = Flow([[sharded(right_kept), sharded(right_got)], [small, small_got]])
    flows = (left, right, inner, outer)

    def advance(jobs, of, tokens=()):
        values = run(jobs, tokens)
        for flow, value in zip(of, values):
            flow.send(value)
        return values

    for bit in across_bits[:-1]:
        advance([left.docs_job(bit)], (left,))
    last = advance(
        [left.docs_job(across_bits[-1]), right.seg_job(), inner.seg_job(), outer.seg_job()], flows, (cross_bias,)
    )
    for bit in across_bits[:-1]:
        advance([right.docs_job(bit)], (right,))
    last = advance([left.seg_job(), right.docs_job(across_bits[-1]), inner.seg_job(), outer.seg_job()], flows)
    inner.further(seg_bits, last)
    outer.further(seg_bits, last)
    values = run([left.seg_job(), right.seg_job(), inner.settle_job(), outer.settle_job()])
    left.send(values[0])
    right.send(values[1])
    inner, outer = (docs_pieces(value.reshape(value.shape[1:])) for value in values[2:])
    while left.seg_done < seg_bits:
        last = advance([left.seg_job(), right.seg_job()], (left, right))
    (outer_out,) = finish(
        [(outer, False, (0, outer[0].shape[0]), [(0, 0, width // 2, 0)])], [outer_out], tokens=last
    )
    span = inner[0].shape[0]
    (inner_out,) = finish([(inner, False, (0, span), [(0, 0, hidden // 2, 0)])], [inner_out], tokens=(outer_out,))
    (last,) = run([joined(left.settle_job(), right.settle_job())], (inner_out,))
    last = docs_pieces(last.reshape(last.shape[1:]))
    part, wide = width // segments, hidden // segments
    third = width // 2
    attn_out, proj_out, *smalls = finish(
        [
            (last, False, (0, span), [(0, 0, third, 0), (1, third, width, 0)]),
            (last, False, (span, 2 * span), [(0, 0, width, third)]),
        ],
        [attn_out, proj_out],
        ([cross_bias, cross_wide, cross_norm], [part] * 8 + [wide]),
    )
    qb, vb, pb, ob, g1, s1, g2, s2, ib = smalls
    return (
        layer_out.reshape(tokens.shape),
        input_grad,
        attn_out,
        qb,
        vb,
        proj_out,
        pb,
        g1,
        s1,
        inner_out,
        ib,
        outer_out,
        ob,
        g2,
        s2,
        position_grad,
    )


def solution(mesh):
    return jax.shard_map(
        on_device,
        mesh=mesh,
        in_specs=(
            P("docs", "seg", None, None),
            P("docs"),
            P(),
            P(),
            P(),
            P(),
            P(),
            P(),
            P(),
            P(),
            P(),
            P(),
            P(),
            P(),
            P(),
            P(),
            P("docs", "seg", None, None),
        ),
        out_specs=(
            P("docs", "seg", None, None),
            P("docs", "seg", None, None),
            P(None, "seg", None),
            P(None, "seg"),
            P(None, "seg"),
            P(None, "seg", None),
            P(None, "seg"),
            P(None, "seg"),
            P(None, "seg"),
            P(None, "seg", None),
            P(None, "seg"),
            P(None, "seg", None),
            P(None, "seg"),
            P(None, "seg"),
            P(None, "seg"),
            P(None, "seg"),
        ),
        check_vma=False,
    )
```

```python
import functools
import math

import jax
import jax.numpy as jnp
from jax import lax
from jax.experimental import pallas as pl
from jax.experimental.pallas import tpu as pltpu
from jax.sharding import PartitionSpec as P

HEADS = 12
HEAD = 64
PAIR = 2 * HEAD


NEG = -1e30
EPS = 1e-05
LOW = jnp.bfloat16
F32 = jnp.float32
MIB = 1024 * 1024
TILE = 512
WIDE = 1024


def dot(left, right):
    return lax.dot_general(left, right, (((1,), (0,)), ((), ())), preferred_element_type=F32)


def dot_rt(left, right):
    return lax.dot_general(left, right, (((1,), (1,)), ((), ())), preferred_element_type=F32)


def dot_lt(left, right):
    return lax.dot_general(left, right, (((0,), (0,)), ((), ())), preferred_element_type=F32)


def normalize(rows):
    center = rows - jnp.mean(rows, axis=-1, keepdims=True)
    rstd = lax.rsqrt(jnp.mean(center * center, axis=-1, keepdims=True) + EPS)
    return center * rstd, rstd


def norm_back(grad, gain, normed, rstd):
    scaled = grad * gain
    return rstd * (
        scaled
        - jnp.mean(scaled, axis=-1, keepdims=True)
        - normed * jnp.mean(scaled * normed, axis=-1, keepdims=True)
    )


def gelu_and_slope(inner):
    kind = inner.dtype.type
    size = jnp.abs(inner)
    t = kind(1.0) / (kind(1.0) + kind(0.3275911 * 0.7071067811865476) * size)
    bell = jnp.exp(kind(-0.5) * inner * inner)
    series = kind(0.5 * 1.061405429) * t - kind(0.5 * 1.453152027)
    series = series * t + kind(0.5 * 1.421413741)
    series = series * t - kind(0.5 * 0.284496736)
    series = series * t + kind(0.5 * 0.254829592)
    tail = series * t * bell
    below = jnp.where(inner >= kind(0.0), kind(1.0) - tail, tail)
    return inner * below, below + inner * bell * kind(0.3989422804014327)


def colsum(rows):
    return jnp.sum(rows, axis=0, keepdims=True)


def head_masks():
    lane = lax.broadcasted_iota(jnp.int32, (1, PAIR), 1)
    first = (lane < HEAD).astype(F32).astype(LOW)
    second = (lane >= HEAD).astype(F32).astype(LOW)
    return lane, first, second


def whole(shape):
    return pl.BlockSpec(shape, lambda *_: (0,) * len(shape))


def of_block(index, shape):
    return pl.BlockSpec((1,) + shape, lambda *_: (index,) + (0,) * len(shape))


def params(limit_mib=64):
    return pltpu.CompilerParams(vmem_limit_bytes=limit_mib * MIB)


def token_specs(tokens):
    return [pl.BlockSpec(memory_space=pl.ANY)] * len(tokens)


def cost(*_):
    return pl.CostEstimate(flops=1024, bytes_accessed=1024, transcendentals=0)


def attend_kernel(
    groups, length, len_ref, x_ref, w_ref, qb_ref, vb_ref, pw_ref, pb_ref, g1_ref, s1_ref,
    qkv_ref, att_ref, normed_ref, hidden_ref, rstd_ref,
):
    step = pl.program_id(0)
    start = lax.axis_index("seg") * length
    rows_low = x_ref[...]
    width = rows_low.shape[1]
    queries = (dot(rows_low, w_ref[0, :, :width]) + qb_ref[0:1, :].astype(F32)).astype(LOW)
    keys = dot(rows_low, w_ref[0, :, width : 2 * width]).astype(LOW)
    values = (dot(rows_low, w_ref[0, :, 2 * width :]) + vb_ref[0:1, :].astype(F32)).astype(LOW)
    qkv_ref[:, :width] = queries
    qkv_ref[:, width : 2 * width] = keys
    qkv_ref[:, 2 * width :] = values
    queries = queries * LOW(1.0 / math.sqrt(HEAD))
    lane, first, second = head_masks()
    key_lane = lax.broadcasted_iota(jnp.int32, (1, length), 1)
    ones = jnp.ones((length, PAIR), LOW)
    places = []
    for group in range(groups):
        count = jnp.clip(len_ref[step * groups + group] - start, 1, length)
        rows = slice(group * length, (group + 1) * length)
        places += [(rows, slice(at, at + PAIR), key_lane < count) for at in range(0, width, PAIR)]
    scores = []
    for rows, cols, _ in places:
        both = queries[rows, cols]
        both = jnp.concatenate([both * first, both * second], axis=0)
        scores.append(dot_rt(both, keys[rows, cols]))
    weights = []
    for item, (_, _, valid) in zip(scores, places):
        item = jnp.where(valid, item, NEG)
        weights.append(jnp.exp(item - jnp.max(item, axis=1, keepdims=True)).astype(LOW))
    for item, (rows, cols, _) in zip(weights, places):
        mixed = dot(item, jnp.concatenate([values[rows, cols], ones], axis=1))
        mixed = mixed[:, :PAIR] / mixed[:, PAIR:]
        att_ref[rows, cols] = jnp.where(lane < HEAD, mixed[:length], mixed[length:]).astype(LOW)
    resid = rows_low.astype(F32) + dot(att_ref[...], pw_ref[0]) + pb_ref[0:1, :].astype(F32)
    normed, rstd = normalize(resid)
    normed_ref[...] = normed.astype(LOW)
    hidden_ref[...] = (normed * g1_ref[0:1, :].astype(F32) + s1_ref[0:1, :].astype(F32)).astype(LOW)
    rstd_ref[...] = jnp.broadcast_to(rstd, rstd_ref.shape)


def attend(rows_low, doc_length, seg_len, attn_weight, query_bias, value_bias, proj_weight, proj_bias, g1, s1):
    total, width = rows_low.shape
    groups = 2
    size = groups * seg_len
    return pl.pallas_call(
        functools.partial(attend_kernel, groups, seg_len),
        grid=(total // size,),
        in_specs=[
            pl.BlockSpec(memory_space=pltpu.SMEM),
            pl.BlockSpec((size, width), lambda i: (i, 0)),
            of_block(0, (width, 3 * width)),
            whole(query_bias.shape),
            whole(value_bias.shape),
            of_block(0, (width, width)),
            whole(proj_bias.shape),
            whole(g1.shape),
            whole(s1.shape),
        ],
        out_specs=[
            pl.BlockSpec((size, 3 * width), lambda i: (i, 0)),
            pl.BlockSpec((size, width), lambda i: (i, 0)),
            pl.BlockSpec((size, width), lambda i: (i, 0)),
            pl.BlockSpec((size, width), lambda i: (i, 0)),
            pl.BlockSpec((size, 128), lambda i: (i, 0)),
        ],
        out_shape=[
            jax.ShapeDtypeStruct((total, 3 * width), LOW),
            jax.ShapeDtypeStruct((total, width), LOW),
            jax.ShapeDtypeStruct((total, width), LOW),
            jax.ShapeDtypeStruct((total, width), LOW),
            jax.ShapeDtypeStruct((total, 128), F32),
        ],
        compiler_params=params(),
        cost_estimate=cost(
            2 * total * width * 4 * width + 8 * total * seg_len * width, 16 * MIB, total * seg_len * HEADS
        ),
        name="attend",
    )(doc_length, rows_low, attn_weight, query_bias, value_bias, proj_weight, proj_bias, g1, s1)


def leader_kernel(
    hidden_ref, cot_ref, b1_ref, b2_ref, g2_ref, s2_ref, w1_hbm, w2_hbm, out_ref, w1_ref, w2_ref, sems,
):
    tiles = w1_ref.shape[1] // TILE
    copies = []
    for at in range(tiles):
        cols = slice(at * TILE, (at + 1) * TILE)
        copies.append(
            (
                pltpu.make_async_copy(w1_hbm.at[0, :, cols], w1_ref.at[:, cols], sems.at[0, at]),
                pltpu.make_async_copy(w2_hbm.at[0, cols, :], w2_ref.at[cols, :], sems.at[1, at]),
            )
        )
    for pair in copies:
        for copy in pair:
            copy.start()
    hidden = hidden_ref[:, 0, :]
    total = hidden.astype(F32) + b2_ref[0:1, :].astype(F32)
    for at, pair in enumerate(copies):
        cols = slice(at * TILE, (at + 1) * TILE)
        pair[0].wait()
        active, _ = gelu_and_slope(dot(hidden, w1_ref[:, cols]) + b1_ref[0:1, cols].astype(F32))
        pair[1].wait()
        total = total + dot(active.astype(LOW), w2_ref[cols, :])
    normed, _ = normalize(total)
    out = normed * g2_ref[0:1, :].astype(F32) + s2_ref[0:1, :].astype(F32)
    out_ref[0] = out.astype(LOW)
    out_ref[1] = cot_ref[:, 0, :]


def ff_specs(width, tile, pick=lambda i: i):
    return [
        pl.BlockSpec((1, width, tile), lambda i, *_: (0, 0, pick(i))),
        pl.BlockSpec((2, tile), lambda i, *_: (0, pick(i))),
        pl.BlockSpec((1, tile, width), lambda i, *_: (0, pick(i), 0)),
    ]


def lead(hidden_low, cots, docs, inner_weight, inner_bias, outer_weight, outer_bias, g2, s2):
    width, hidden = inner_weight.shape[1:]
    hidden_low = hidden_low.reshape(docs, -1, width)
    cots = cots.reshape(docs, -1, width)
    hbm = pl.BlockSpec(memory_space=pl.ANY)
    return pl.pallas_call(
        leader_kernel,
        grid=(1,),
        in_specs=[whole((docs, 16, width))] * 2 + [whole((2, hidden))] + [whole((2, width))] * 3 + [hbm] * 2,
        out_specs=whole((2, docs, width)),
        out_shape=jax.ShapeDtypeStruct((2, docs, width), LOW),
        scratch_shapes=[
            pltpu.VMEM((width, hidden), LOW),
            pltpu.VMEM((hidden, width), LOW),
            pltpu.SemaphoreType.DMA((2, hidden // TILE)),
        ],
        compiler_params=params(),
        cost_estimate=cost(),
        name="leaders",
    )(hidden_low, cots, inner_bias, outer_bias, g2, s2, inner_weight, outer_weight)


CHUNK = 256


def feed_kernel(
    low_ref, w1_ref, b1_ref, w2_ref, b2_ref, g2_ref, s2_ref,
    active_ref, slope_ref, out_ref, normed2_ref, rstd2_ref, acc_ref,
):
    step = pl.program_id(0)
    last = pl.num_programs(0) - 1
    chunks = [slice(at, at + CHUNK) for at in range(0, low_ref.shape[0], CHUNK)]
    bias = b1_ref[0:1, :].astype(F32)

    @pl.when(step == 0)
    def _():
        for rows in chunks:
            acc_ref[rows, :] = low_ref[rows, :].astype(F32) + b2_ref[0:1, :].astype(F32)

    inner = dot(low_ref[chunks[0], :], w1_ref[0])
    for at, rows in enumerate(chunks):
        active, slope = gelu_and_slope((inner + bias).astype(LOW))
        if at + 1 < len(chunks):
            inner = dot(low_ref[chunks[at + 1], :], w1_ref[0])
        active_ref[rows, :] = active
        slope_ref[rows, :] = slope
        acc_ref[rows, :] += dot(active, w2_ref[0])

    @pl.when(step == last)
    def _():
        for rows in chunks:
            normed, rstd = normalize(acc_ref[rows, :])
            normed2_ref[rows, :] = normed.astype(LOW)
            rstd2_ref[rows, :] = jnp.broadcast_to(rstd, (CHUNK, 128))
            out = normed * g2_ref[0:1, :].astype(F32) + s2_ref[0:1, :].astype(F32)
            out_ref[rows, :] = out.astype(LOW)


def feed(hidden_low, inner_weight, inner_bias, outer_weight, outer_bias, g2, s2):
    total, width = hidden_low.shape
    hidden = inner_weight.shape[2]
    return pl.pallas_call(
        feed_kernel,
        grid=(hidden // TILE,),
        in_specs=[whole((total, width))] + ff_specs(width, TILE) + [whole((2, width))] * 3,
        out_specs=[
            pl.BlockSpec((total, TILE), lambda i: (0, i)),
            pl.BlockSpec((total, TILE), lambda i: (0, i)),
            whole((total, width)),
            whole((total, width)),
            whole((total, 128)),
        ],
        out_shape=[
            jax.ShapeDtypeStruct((total, hidden), LOW),
            jax.ShapeDtypeStruct((total, hidden), LOW),
            jax.ShapeDtypeStruct((total, width), LOW),
            jax.ShapeDtypeStruct((total, width), LOW),
            jax.ShapeDtypeStruct((total, 128), F32),
        ],
        scratch_shapes=[pltpu.VMEM((total, width), F32)],
        compiler_params=params(),
        cost_estimate=cost(),
        name="feed",
    )(hidden_low, inner_weight, inner_bias, outer_weight, outer_bias, g2, s2)


def slots(columns):
    return -(-columns // 128) * 128


def bundle_places(width, hidden, segments):
    own = slots(width // segments)
    sizes = [own, own, own, slots(hidden // segments), 3 * width, width, hidden, width, own]
    places, start = [], 0
    for size in sizes:
        places.append((start, size))
        start += size
    return places, start


def cross_kernel(docs, segments, length, len_ref, *refs):
    pieces, refs = refs[: segments // 2], refs[segments // 2 :]
    (
        pos_ref, qb_ref, vb_ref, pb_ref, g1_ref, s1_ref, b1_ref, b2_ref, g2_ref, s2_ref,
        seg_cot_ref, seg_normed_ref, seg_rstd_ref, aw_hbm, pw_hbm, w1_hbm, w2_hbm,
        out_ref, back_ref, bundle_ref, seg_branch_ref, seg_sums_ref,
        aw_ref, pw_ref, w1_ref, w2_ref, inner_ref, probs_ref, low_ref, att_ref, hid_ref, act_ref,
        lead_ref, cot_ref, sems,
    ) = refs
    width = lead_ref.shape[1]
    hidden = w1_ref.shape[1]
    places, _ = bundle_places(width, hidden, segments)
    dmix_ref, dproj_ref, dinner_ref, dout_ref = (
        bundle_ref.at[:, places[at][0] : places[at][0] + places[at][1]] for at in range(4, 8)
    )
    copies = [
        pltpu.make_async_copy(src.at[1], dst, sems.at[i])
        for i, (src, dst) in enumerate(
            [(aw_hbm, aw_ref), (pw_hbm, pw_ref), (w1_hbm, w1_ref), (w2_hbm, w2_ref)]
        )
    ]
    for copy in copies:
        copy.start()
    total = lead_ref.shape[0]
    scale = 1.0 / math.sqrt(HEAD)

    def row(ref):
        return ref[1:2, :].astype(F32)

    me = lax.axis_index("seg")
    for at, piece in enumerate(pieces):
        for half in range(2):
            seg = me ^ (2 * at + half)
            for doc in range(docs):
                place = pl.ds(doc * segments + seg, 1)
                lead_ref[place, :] = piece[2 * half, doc : doc + 1, :].astype(F32)
                cot_ref[place, :] = piece[2 * half + 1, doc : doc + 1, :].astype(F32)
    rows = lead_ref[...] + jnp.concatenate([pos_ref[...].astype(F32)] * docs, axis=0)
    rows_low = rows.astype(LOW)
    low_ref[...] = rows_low
    both_heads = (total, 2 * total)
    key = lax.broadcasted_iota(jnp.int32, both_heads, 0)
    query = lax.broadcasted_iota(jnp.int32, both_heads, 1) % total
    key_doc = key // segments
    reach = jnp.zeros(both_heads, jnp.int32)
    for doc in range(docs):
        reach = jnp.where(key_doc == doc, len_ref[doc], reach)
    valid = (key_doc == query // segments) & ((key - key_doc * segments) * length < reach)
    lane, first, second = head_masks()

    later_row = lax.broadcasted_iota(jnp.int32, (length, 1), 0) > 0
    seg_gain = g2_ref[0:1, :].astype(F32)
    seg_sums = [jnp.zeros((1, width), F32)] * 3
    for at in range(0, seg_cot_ref.shape[0], length):
        span = slice(at, at + length)
        upper = jnp.where(later_row, seg_cot_ref[span, :].astype(F32), 0.0)
        normed = seg_normed_ref[span, :].astype(F32)
        branch = norm_back(upper, seg_gain, normed, seg_rstd_ref[span, 0:1]).astype(LOW)
        seg_branch_ref[span, :] = branch
        for which, item in enumerate((upper * normed, upper, branch.astype(F32))):
            seg_sums[which] = seg_sums[which] + colsum(item)
    seg_sums_ref[...] = jnp.concatenate(seg_sums + [jnp.zeros((5, width), F32)], axis=0)

    copies[0].wait()
    queries = (dot(rows_low, aw_ref[:, :width]) + row(qb_ref)).astype(LOW)
    keys = dot(rows_low, aw_ref[:, width : 2 * width]).astype(LOW)
    values = (dot(rows_low, aw_ref[:, 2 * width :]) + row(vb_ref)).astype(LOW)

    def stacked(both):
        return jnp.concatenate([both * first, both * second], axis=0)

    def picked(both):
        return jnp.where(lane < HEAD, both[:total], both[total:])

    pair_cols = [slice(at, at + PAIR) for at in range(0, width, PAIR)]
    query_both = [stacked(queries[:, cols]) for cols in pair_cols]
    scores = [dot_rt(keys[:, cols], both) for cols, both in zip(pair_cols, query_both)]
    probs_low = []
    for pair, item in enumerate(scores):
        item = jnp.where(valid, item * scale, NEG)
        weights = jnp.exp(item - jnp.max(item, axis=0, keepdims=True))
        probs = weights / jnp.sum(weights, axis=0, keepdims=True)
        probs_ref[pair] = probs
        probs_low.append(probs.astype(LOW))
    for cols, item in zip(pair_cols, probs_low):
        att_ref[:, cols] = picked(dot_lt(item, values[:, cols])).astype(LOW)
    copies[1].wait()
    resid = rows + dot(att_ref[...], pw_ref[...]) + row(pb_ref)
    normed_one, rstd_one = normalize(resid)
    hidden = normed_one * row(g1_ref) + row(s1_ref)
    hidden_low = hidden.astype(LOW)
    hid_ref[...] = hidden_low
    copies[2].wait()
    copies[3].wait()
    count = w1_ref.shape[1] // WIDE
    branch = jnp.zeros((total, width), F32)
    for at in range(count):
        cols = slice(at * WIDE, (at + 1) * WIDE)
        active, slope = gelu_and_slope(dot(hidden_low, w1_ref[:, cols]) + b1_ref[1:2, cols].astype(F32))
        inner_ref[:, cols] = slope
        active = active.astype(LOW)
        act_ref[:, cols] = active
        branch += dot(active, w2_ref[cols, :])
    normed_two, rstd_two = normalize(hidden + branch + row(b2_ref))
    out_ref[...] = normed_two * row(g2_ref) + row(s2_ref)

    upper = cot_ref[...]
    sums = [colsum(upper * normed_two), colsum(upper)]
    resid_two = norm_back(upper, row(g2_ref), normed_two, rstd_two)
    branch_two = resid_two.astype(LOW)
    dout_ref[...] = branch_two
    hidden_grad = resid_two
    for at in range(count):
        cols = slice(at * WIDE, (at + 1) * WIDE)
        inner_grad = (dot_rt(branch_two, w2_ref[cols, :]) * inner_ref[:, cols]).astype(LOW)
        dinner_ref[:, cols] = inner_grad
        hidden_grad += dot_rt(inner_grad, w1_ref[:, cols])
    sums = [colsum(hidden_grad * normed_one), colsum(hidden_grad)] + sums
    resid_one = norm_back(hidden_grad, row(g1_ref), normed_one, rstd_one)
    branch_one = resid_one.astype(LOW)
    dproj_ref[...] = branch_one
    att_grad = dot_rt(branch_one, pw_ref[...]).astype(LOW)
    att_both = [stacked(att_grad[:, cols]) for cols in pair_cols]
    prob_grads = [dot_rt(values[:, cols], both) for cols, both in zip(pair_cols, att_both)]
    score_grads = []
    for pair, prob_grad in enumerate(prob_grads):
        probs = probs_ref[pair]
        score_grad = probs * (prob_grad - jnp.sum(prob_grad * probs, axis=0, keepdims=True))
        score_grads.append(score_grad.astype(LOW))
    for pair, cols in enumerate(pair_cols):
        cols_k, cols_v = (slice(cols.start + at * width, cols.stop + at * width) for at in (1, 2))
        dmix_ref[:, cols] = (picked(dot_lt(score_grads[pair], keys[:, cols])) * scale).astype(LOW)
        dmix_ref[:, cols_k] = (dot(score_grads[pair], query_both[pair]) * scale).astype(LOW)
        dmix_ref[:, cols_v] = dot(probs_ref[pair].astype(LOW), att_both[pair]).astype(LOW)
    back = resid_one + dot_rt(dmix_ref[...], aw_ref[...])
    back_ref[...] = back
    seg = lax.axis_index("seg")

    def own(value, slot):
        step = value.shape[1] // segments
        return pltpu.roll(value.astype(F32), lax.rem(value.shape[1] - seg * step, value.shape[1]), 1)[:, :slot]

    for at, item in enumerate((low_ref, att_ref, hid_ref, act_ref)):
        start, slot = places[at]
        bundle_ref[:, start : start + slot] = own(item[...], slot).astype(LOW)
    start, slot = places[8]
    by_segment = back[:segments]
    for doc in range(1, docs):
        by_segment += back[doc * segments : (doc + 1) * segments]
    pieces = [own(jnp.concatenate(sums + [jnp.zeros((4, width), F32)], axis=0), slot), own(by_segment, slot)]
    rest = total - 8 - segments
    if rest:
        pieces.append(jnp.zeros((rest, slot), F32))
    bundle_ref[:, start : start + slot] = jnp.concatenate(pieces, axis=0).astype(LOW)


def cross_block(
    pieces, position, doc_length, seg_len,
    attn_weight, query_bias, value_bias, proj_weight, proj_bias, g1, s1,
    inner_weight, inner_bias, outer_weight, outer_bias, g2, s2, seg_cots, seg_normed, seg_rstd,
):
    segments, width = position.shape
    docs = pieces[0].shape[1]
    total = docs * segments
    hidden = inner_weight.shape[2]
    vmem = pl.BlockSpec(memory_space=pltpu.VMEM)
    hbm = pl.BlockSpec(memory_space=pl.ANY)

    def shape(columns, dtype=LOW):
        return jax.ShapeDtypeStruct((total, columns), dtype)

    return pl.pallas_call(
        functools.partial(cross_kernel, docs, segments, seg_len),
        in_specs=[pl.BlockSpec(memory_space=pltpu.SMEM)] + [vmem] * (len(pieces) + 13) + [hbm] * 4,
        out_specs=[vmem] * 5,
        out_shape=[
            shape(width, F32),
            shape(width, F32),
            shape(bundle_places(width, hidden, segments)[1]),
            jax.ShapeDtypeStruct(seg_cots.shape, LOW),
            jax.ShapeDtypeStruct((8, width), F32),
        ],
        scratch_shapes=[
            pltpu.VMEM((width, 3 * width), LOW),
            pltpu.VMEM((width, width), LOW),
            pltpu.VMEM((width, hidden), LOW),
            pltpu.VMEM((hidden, width), LOW),
            pltpu.VMEM((total, hidden), F32),
            pltpu.VMEM((HEADS // 2, total, 2 * total), F32),
            pltpu.VMEM((total, width), LOW),
            pltpu.VMEM((total, width), LOW),
            pltpu.VMEM((total, width), LOW),
            pltpu.VMEM((total, hidden), LOW),
            pltpu.VMEM((total, width), F32),
            pltpu.VMEM((total, width), F32),
            pltpu.SemaphoreType.DMA((4,)),
        ],
        compiler_params=params(),
        cost_estimate=cost(4 * total * width * (4 * width + 2 * hidden) * 2, 2 * width * (4 * width + 2 * hidden)),
        name="cross_block",
    )(
        doc_length, *pieces, position, query_bias, value_bias, proj_bias, g1, s1,
        inner_bias, outer_bias, g2, s2, seg_cots, seg_normed, seg_rstd,
        attn_weight, proj_weight, inner_weight, outer_weight,
    )


def top_kernel(
    segments, back_ref, cross_ref, low_ref, normed_ref, rstd_ref, g2_ref, first_sums_ref, branch_ref, active_ref,
    sums_ref, sent_ref, kept_ref, patched_ref, branch_out_ref, swap_ref,
):
    step = pl.program_id(0)
    docs, length, width = branch_ref.shape
    half = width // 2

    @pl.when(step == 0)
    def _():
        core = lax.axis_index("docs") % 2
        seg = lax.axis_index("seg")
        first_row = lax.broadcasted_iota(jnp.int32, (low_ref.shape[1], 1), 0) == 0

        def own(ref):
            return jnp.concatenate([ref[pl.ds(doc * segments + seg, 1), :] for doc in range(docs)], axis=0)

        upper = own(back_ref)
        normed = normed_ref[:, 0, :].astype(F32)
        branch = norm_back(upper, g2_ref[0:1, :].astype(F32), normed, rstd_ref[:, 0, 0:1]).astype(LOW).astype(F32)
        for at, item in enumerate((upper * normed, upper, branch)):
            sums_ref[at : at + 1, :] = first_sums_ref[at : at + 1, :] + colsum(item)
        sums_ref[3:8, :] = jnp.zeros((5, width), F32)
        cross = own(cross_ref)
        top_rows = low_ref.shape[1]
        for doc in range(docs):
            patched_ref[doc] = jnp.where(first_row, cross[doc : doc + 1, :], low_ref[doc].astype(F32)).astype(LOW)
            top_part = jnp.where(first_row, branch[doc : doc + 1, :], branch_ref[doc, :top_rows, :].astype(F32))
            top_part = top_part.astype(LOW)
            branch_out_ref[doc] = top_part
            rows = slice(doc * length, (doc + 1) * length)
            whole_part = jnp.concatenate([top_part, branch_ref[doc, top_rows:, :]], axis=0)
            left, right = whole_part[:, :half], whole_part[:, half:]
            swap_ref[rows, :half] = jnp.where(core == 0, right, left)
            swap_ref[rows, half:] = jnp.where(core == 0, left, right)

    grad = dot_lt(active_ref[...], swap_ref[...]).astype(LOW)
    sent_ref[...] = grad[:, :half]
    kept_ref[...] = grad[:, half:]


def top_back(back, cross_out, seg_low, seg_len, normed, rstd, g2, sums, branch, active):
    total, width = branch.shape
    hidden = active.shape[1]
    docs = total // seg_len
    first = (docs, 16, width)
    by_doc = (docs, seg_len, width)
    out = pl.pallas_call(
        functools.partial(top_kernel, back.shape[0] // docs),
        grid=(hidden // TILE,),
        in_specs=[
            whole(back.shape),
            whole(back.shape),
            whole(first),
            whole(first),
            whole((docs, 8, 128)),
            whole((2, width)),
            whole((8, width)),
            whole(by_doc),
            pl.BlockSpec((total, TILE), lambda i: (0, i)),
        ],
        out_specs=[
            whole((8, width)),
            pl.BlockSpec((TILE, width // 2), lambda i: (i, 0)),
            pl.BlockSpec((TILE, width // 2), lambda i: (i, 0)),
            whole(first),
            whole(first),
        ],
        out_shape=[
            jax.ShapeDtypeStruct((8, width), F32),
            jax.ShapeDtypeStruct((hidden, width // 2), LOW),
            jax.ShapeDtypeStruct((hidden, width // 2), LOW),
            jax.ShapeDtypeStruct(by_doc, LOW),
            jax.ShapeDtypeStruct(by_doc, LOW),
        ],
        input_output_aliases={2: 3, 7: 4},
        scratch_shapes=[pltpu.VMEM((total, width), LOW)],
        compiler_params=params(),
        cost_estimate=cost(),
        name="top_back",
    )(
        back, cross_out, seg_low.reshape(by_doc), normed.reshape(by_doc), rstd.reshape(docs, seg_len, 128), g2, sums,
        branch.reshape(by_doc), active,
    )
    return out[0], out[1], out[2], out[3], out[4].reshape(total, width)


def middle_step(branch_ref, low_ref, slope_ref, w1_ref, w2_ref, acc_ref, bias_ref, grad_ref, finished=None):
    parts = []
    chunks = [slice(at, at + CHUNK) for at in range(0, branch_ref.shape[0], CHUNK)]
    following = dot_rt(branch_ref[chunks[0], :], w2_ref[0])
    for at, rows in enumerate(chunks):
        part = (following * slope_ref[rows, :].astype(F32)).astype(LOW)
        if at + 1 < len(chunks):
            following = dot_rt(branch_ref[chunks[at + 1], :], w2_ref[0])
        total = acc_ref[rows, :] + dot_rt(part, w1_ref[0])
        if finished:
            finished(rows, total)
        else:
            acc_ref[rows, :] = total
        parts.append(part)
    inner_grad = jnp.concatenate(parts, axis=0)
    bias_ref[...] = jnp.broadcast_to(colsum(inner_grad.astype(F32)), bias_ref.shape)
    grad_ref[...] = dot_lt(low_ref[...], inner_grad).astype(LOW)


def middle_first_kernel(core_ref, branch_ref, low_ref, slope_ref, w1_ref, w2_ref, *refs):
    half_ref, bias_ref, sent_ref, acc_ref = refs[-4:]
    step = pl.program_id(0)
    last = pl.num_programs(0) - 1

    @pl.when(step == 0)
    def _():
        acc_ref[...] = jnp.zeros_like(acc_ref)

    def finished(rows, total):
        half_ref[rows, :] = total.astype(LOW)

    operands = (branch_ref, low_ref, slope_ref, w1_ref, w2_ref, acc_ref, bias_ref, sent_ref)
    pl.when(step < last)(lambda: middle_step(*operands))
    pl.when(step == last)(lambda: middle_step(*operands, finished))


def middle_last_kernel(core_ref, branch_ref, low_ref, slope_ref, w1_ref, w2_ref, g1_ref, *refs):
    half_hbm, normed_hbm, rstd_hbm = refs[:3]
    branch1_ref, sums_ref, bias_ref, kept_ref, acc_ref, half_ref, normed_ref, rstd_ref, sems = refs[-9:]
    step = pl.program_id(0)
    last = pl.num_programs(0) - 1
    width = branch_ref.shape[1]
    copies = [
        pltpu.make_async_copy(source, target, sems.at[at])
        for at, (source, target) in enumerate(
            ((half_hbm, half_ref), (normed_hbm, normed_ref), (rstd_hbm, rstd_ref))
        )
    ]

    @pl.when(step == 0)
    def _():
        for copy in copies:
            copy.start()
        acc_ref[...] = jnp.zeros_like(acc_ref)

    sums = [jnp.zeros((1, width), F32)] * 3

    def finished(rows, total):
        hidden_grad = total + half_ref[rows, :].astype(F32) + branch_ref[rows, :].astype(F32)
        normed = normed_ref[rows, :].astype(F32)
        resid = norm_back(hidden_grad, g1_ref[0:1, :].astype(F32), normed, rstd_ref[rows, 0:1])
        branch = resid.astype(LOW)
        branch1_ref[rows, :] = branch
        for at, item in enumerate((hidden_grad * normed, hidden_grad, branch.astype(F32))):
            sums[at] = sums[at] + colsum(item)

    operands = (branch_ref, low_ref, slope_ref, w1_ref, w2_ref, acc_ref, bias_ref, kept_ref)
    pl.when(step < last)(lambda: middle_step(*operands))

    @pl.when(step == last)
    def _():
        for copy in copies:
            copy.wait()
        middle_step(*operands, finished)
        sums_ref[...] = jnp.concatenate(sums + [jnp.zeros((5, width), F32)], axis=0)


def half_order(steps):
    half = steps // 2

    def pick(step, core_ref):
        return jnp.where(step < half, 1 - core_ref[0], core_ref[0]) * half + step % half

    return pick


def middle_specs(total, width, steps, offset):
    pick = half_order(2 * steps)
    return [
        whole((total, width)),
        whole((total, width)),
        pl.BlockSpec((total, TILE), lambda i, c: (0, pick(i + offset, c))),
        pl.BlockSpec((1, width, TILE), lambda i, c: (0, 0, pick(i + offset, c))),
        pl.BlockSpec((1, TILE, width), lambda i, c: (0, pick(i + offset, c), 0)),
    ]


def middle_first(core, branch, low, slope, inner_weight, outer_weight, tokens=()):
    total, width = branch.shape
    steps = slope.shape[1] // TILE // 2
    return pl.pallas_call(
        middle_first_kernel,
        grid_spec=pltpu.PrefetchScalarGridSpec(
            num_scalar_prefetch=1,
            grid=(steps,),
            in_specs=middle_specs(total, width, steps, 0) + token_specs(tokens),
            out_specs=[
                whole((total, width)),
                pl.BlockSpec((8, TILE), lambda i, c: (0, i)),
                pl.BlockSpec((width, TILE), lambda i, c: (0, i)),
            ],
            scratch_shapes=[pltpu.VMEM((total, width), F32)],
        ),
        out_shape=[
            jax.ShapeDtypeStruct((total, width), LOW),
            jax.ShapeDtypeStruct((8, steps * TILE), F32),
            jax.ShapeDtypeStruct((width, steps * TILE), LOW),
        ],
        compiler_params=params(),
        cost_estimate=cost(),
        name="middle_first",
    )(core, branch, low, slope, inner_weight, outer_weight, *tokens)


def middle_last(core, branch, low, slope, inner_weight, outer_weight, g1, half, normed, rstd, tokens=()):
    total, width = branch.shape
    steps = slope.shape[1] // TILE // 2
    return pl.pallas_call(
        middle_last_kernel,
        grid_spec=pltpu.PrefetchScalarGridSpec(
            num_scalar_prefetch=1,
            grid=(steps,),
            in_specs=middle_specs(total, width, steps, steps)
            + [whole((2, width))]
            + token_specs((half, normed, rstd) + tuple(tokens)),
            out_specs=[
                whole((total, width)),
                whole((8, width)),
                pl.BlockSpec((8, TILE), lambda i, c: (0, i)),
                pl.BlockSpec((width, TILE), lambda i, c: (0, i)),
            ],
            scratch_shapes=[
                pltpu.VMEM((total, width), F32),
                pltpu.VMEM((total, width), LOW),
                pltpu.VMEM((total, width), LOW),
                pltpu.VMEM((total, 128), F32),
                pltpu.SemaphoreType.DMA((3,)),
            ],
        ),
        out_shape=[
            jax.ShapeDtypeStruct((total, width), LOW),
            jax.ShapeDtypeStruct((8, width), F32),
            jax.ShapeDtypeStruct((8, steps * TILE), F32),
            jax.ShapeDtypeStruct((width, steps * TILE), LOW),
        ],
        compiler_params=params(),
        cost_estimate=cost(),
        name="middle_last",
    )(core, branch, low, slope, inner_weight, outer_weight, g1, half, normed, rstd, *tokens)


def attend_back_kernel(groups, length, *refs):
    len_ref, branch_ref, qkv_ref, w_ref, pw_ref = refs[:5]
    dmix_ref, back_ref, sums_ref = refs[-3:]
    step = pl.program_id(0)
    start = lax.axis_index("seg") * length
    width = branch_ref.shape[1]
    scale = LOW(1.0 / math.sqrt(HEAD))
    att_grad = dot_rt(branch_ref[...], pw_ref[0]).astype(LOW)
    lane, first, second = head_masks()
    key_row = lax.broadcasted_iota(jnp.int32, (length, 1), 0)

    def stacked(both):
        return jnp.concatenate([both * first, both * second], axis=0)

    places = []
    for group in range(groups):
        count = jnp.clip(len_ref[step * groups + group] - start, 1, length)
        rows = slice(group * length, (group + 1) * length)
        for at in range(0, width, PAIR):
            cols, cols_k, cols_v = (slice(at + part * width, at + part * width + PAIR) for part in range(3))
            places.append((rows, cols, cols_k, cols_v, key_row < count))
    queries = [stacked(qkv_ref[rows, cols] * scale) for rows, cols, _, _, _ in places]
    att_both = [stacked(att_grad[rows, cols]) for rows, cols, _, _, _ in places]
    scores = [dot_rt(qkv_ref[rows, cols_k], item) for item, (rows, _, cols_k, _, _) in zip(queries, places)]
    prob_grads = [dot_rt(qkv_ref[rows, cols_v], item) for item, (rows, _, _, cols_v, _) in zip(att_both, places)]
    probs, score_grads = [], []
    for item, prob_grad, (_, _, _, _, valid) in zip(scores, prob_grads, places):
        item = jnp.where(valid, item, NEG)
        weights = jnp.exp(item - jnp.max(item, axis=0, keepdims=True))
        prob = weights * (1.0 / jnp.sum(weights, axis=0, keepdims=True))
        score_grad = prob * (prob_grad - jnp.sum(prob_grad * prob, axis=0, keepdims=True))
        probs.append(prob.astype(LOW))
        score_grads.append(score_grad.astype(LOW))
    for at, (rows, cols, cols_k, cols_v, _) in enumerate(places):
        by_query = dot_lt(score_grads[at], qkv_ref[rows, cols_k] * scale)
        dmix_ref[rows, cols] = jnp.where(lane < HEAD, by_query[:length], by_query[length:]).astype(LOW)
        dmix_ref[rows, cols_k] = dot(score_grads[at], queries[at]).astype(LOW)
        dmix_ref[rows, cols_v] = dot(probs[at], att_both[at]).astype(LOW)
    mixed = dmix_ref[...]
    back_ref[...] = branch_ref[...].astype(F32) + dot_rt(mixed, w_ref[0])

    @pl.when(step == 0)
    def _():
        sums_ref[...] = jnp.zeros_like(sums_ref)

    sums_ref[0:1, :] += colsum(mixed[:, :width].astype(F32))
    sums_ref[1:2, :] += colsum(mixed[:, 2 * width :].astype(F32))


def attend_back(branch, qkv, doc_length, seg_len, attn_weight, proj_weight, tokens=()):
    total, width = branch.shape
    groups = 2
    size = groups * seg_len
    return pl.pallas_call(
        functools.partial(attend_back_kernel, groups, seg_len),
        grid=(total // size,),
        in_specs=[
            pl.BlockSpec(memory_space=pltpu.SMEM),
            pl.BlockSpec((size, width), lambda i: (i, 0)),
            pl.BlockSpec((size, 3 * width), lambda i: (i, 0)),
            of_block(0, (width, 3 * width)),
            of_block(0, (width, width)),
        ]
        + token_specs(tokens),
        out_specs=[
            pl.BlockSpec((size, 3 * width), lambda i: (i, 0)),
            pl.BlockSpec((size, width), lambda i: (i, 0)),
            whole((8, width)),
        ],
        out_shape=[
            jax.ShapeDtypeStruct((total, 3 * width), LOW),
            jax.ShapeDtypeStruct((total, width), F32),
            jax.ShapeDtypeStruct((8, width), F32),
        ],
        compiler_params=params(),
        cost_estimate=cost(
            2 * total * width * 4 * width + 20 * total * seg_len * width, 20 * MIB, total * seg_len * HEADS
        ),
        name="attend_back",
    )(doc_length, branch, qkv, attn_weight, proj_weight, *tokens)


def last_grads_kernel(core_ref, rows_ref, att_ref, mixed_ref, branch_ref, *refs):
    left, right = refs[-2:]
    third = branch_ref.shape[1]
    turned = rows_ref[...].T
    left[:, :third] = dot(turned, mixed_ref[:, :third]).astype(LOW)
    right[...] = dot(turned, mixed_ref[:, third:]).astype(LOW)
    left[:, third:] = dot_lt(att_ref[...], branch_ref[...]).astype(LOW)


def last_grads(core, rows, attended, mixed, branch, tokens=()):
    total, width = rows.shape
    out = jax.ShapeDtypeStruct((width, width), LOW)
    return pl.pallas_call(
        last_grads_kernel,
        grid_spec=pltpu.PrefetchScalarGridSpec(
            num_scalar_prefetch=1,
            grid=(width // CHUNK,),
            in_specs=[
                pl.BlockSpec((total, CHUNK), lambda i, c: (0, i)),
                pl.BlockSpec((total, CHUNK), lambda i, c: (0, i)),
                pl.BlockSpec((total, mixed.shape[1] // 2), lambda i, c: (0, c[0])),
                pl.BlockSpec((total, width // 2), lambda i, c: (0, c[0])),
            ]
            + token_specs(tokens),
            out_specs=[pl.BlockSpec((CHUNK, width), lambda i, c: (i, 0))] * 2,
        ),
        out_shape=[out] * 2,
        compiler_params=params(),
        cost_estimate=cost(),
        name="last_grads",
    )(core, rows, attended, mixed, branch, *tokens)


def bits_of(axis):
    return lax.axis_size(axis).bit_length() - 1


def partner(value, axis, bit):
    return flipped(value, axis, 1 << bit)


def flipped(value, axis, mask):
    return lax.ppermute(value, axis, [(i, i ^ mask) for i in range(lax.axis_size(axis))])


def my_bit(axis, bit):
    return (lax.axis_index(axis) >> bit) & 1


def first_rows_pieces(value):
    pair = jnp.concatenate([value, partner(value, "seg", 0)], axis=0)
    return [pair] + [flipped(pair, "seg", flip) for flip in range(2, lax.axis_size("seg"), 2)]


class Job:
    def __init__(self, blocks, columns):
        self.blocks = blocks
        self.columns = columns
        self.operands = []
        self.parts = []

    def add(self, array, place):
        self.operands.append((array, place))
        return len(self.operands) - 1

    def rows(self):
        return sum(rows for rows, _ in self.parts)


def joined(first, second):
    job = Job(first.blocks, first.columns)
    job.operands = first.operands + second.operands
    shift = len(first.operands)
    job.parts = first.parts + [
        (rows, [(at + shift, start) for at, start in addends]) for rows, addends in second.parts
    ]
    return job


def run_kernel(jobs, skip, *refs):
    count = sum(len(job.operands) for job in jobs)
    sources = refs[skip : skip + count]
    outs = refs[skip + count : skip + count + len(jobs)]
    buffers = refs[skip + count + len(jobs) : -len(jobs) - 2]
    ready = refs[-len(jobs) - 2 : -2]
    in_sems, out_sems = refs[-2:]
    arriving, leaving = [], []
    at = sem = 0
    for job in jobs:
        copies = []
        for _, place in job.operands:
            before, after, part = place()
            copies.append(
                [
                    pltpu.make_async_copy(
                        sources[at].at[before, i, after, part], buffers[at].at[i], in_sems.at[sem + i]
                    )
                    for i in range(job.blocks)
                ]
            )
            at += 1
            sem += job.blocks
        for i in range(job.blocks):
            for copy in copies:
                copy[i].start()
        arriving.append(copies)
    at = sem = 0
    for job, copies, out, value in zip(jobs, arriving, outs, ready):
        mine = buffers[at : at + len(job.operands)]
        at += len(job.operands)
        for i in range(job.blocks):
            for copy in copies:
                copy[i].wait()
            start = 0
            for rows, addends in job.parts:
                total = None
                for which, first in addends:
                    item = mine[which][i, first : first + rows, :].astype(F32)
                    total = item if total is None else total + item
                value[i, start : start + rows, :] = total.astype(LOW)
                start += rows
            leaving.append(pltpu.make_async_copy(value.at[i], out.at[i], out_sems.at[sem]))
            leaving[-1].start()
            sem += 1
    for copy in leaving:
        copy.wait()


def run(jobs, tokens=()):
    operands = [array for job in jobs for array, _ in job.operands]
    buffers = [pltpu.VMEM((job.blocks,) + array.shape[4:], LOW) for job in jobs for array, _ in job.operands]
    ready = [pltpu.VMEM((job.blocks, job.rows(), job.columns), LOW) for job in jobs]
    arrivals = sum(job.blocks * len(job.operands) for job in jobs)
    return pl.pallas_call(
        functools.partial(run_kernel, jobs, len(tokens)),
        in_specs=token_specs(tokens) + token_specs(operands),
        out_specs=token_specs(jobs),
        out_shape=[jax.ShapeDtypeStruct((job.blocks, job.rows(), job.columns), LOW) for job in jobs],
        scratch_shapes=buffers
        + ready
        + [pltpu.SemaphoreType.DMA((arrivals,)), pltpu.SemaphoreType.DMA((sum(job.blocks for job in jobs),))],
        compiler_params=params(),
        cost_estimate=cost(),
        name="pick",
    )(*tokens, *operands)


def gate_kernel(*_):
    pass


def gated(values, tokens):
    count = len(values)
    return pl.pallas_call(
        gate_kernel,
        in_specs=token_specs(values) + token_specs(tokens),
        out_specs=token_specs(values),
        out_shape=[jax.ShapeDtypeStruct(item.shape, item.dtype) for item in values],
        input_output_aliases={at: at for at in range(count)},
        cost_estimate=cost(),
        name="gate",
    )(*values, *tokens)


class Flow:
    def __init__(self, groups, order):
        self.groups = groups
        self.received = []
        self.order = order
        self.seg_done = 0
        self.docs_done = []
        self.bits = list(range(bits_of("seg") - 1, -1, -1))
        self.columns = groups[0][0].shape[2]

    def job(self, sent_bit, last):
        docs_done = list(self.docs_done)
        level = len(docs_done) + (last is not None)
        done = self.order[: self.seg_done] + ([sent_bit] if sent_bit is not None else [])
        left = [bit for bit in self.bits if bit not in done]
        job = Job(1 << len(left), self.columns)

        def value(bits):
            index = 0
            for bit in bits:
                mine = my_bit("seg", bit)
                index = index * 2 + (1 - mine if bit == sent_bit else mine)
            return index

        def add(array, bits, docs_level):
            choices = 1 << (level - docs_level)
            rows = array.shape[1] // choices
            before = bits[: bits.index(left[0])] if left else []
            after = bits[bits.index(left[-1]) + 1 :] if left else bits

            def place():
                part = 0
                for bit in [my_bit("docs", bit) for bit in docs_done][docs_level:] + ([last()] if last else []):
                    part = part * 2 + bit
                return value(before), value(after), part

            array = array.reshape(1 << len(before), job.blocks, 1 << len(after), choices, rows, self.columns)
            return rows, job.add(array, place)

        shares = 1 << (bits_of("docs") - 1 - level) if len(self.groups) > 1 else 1
        added = [[add(array, self.bits, 0) for array in group] for group in self.groups]
        for share in range(shares):
            for group in added:
                rows = group[0][0] // shares
                job.parts.append((rows, [(at, share * rows) for _, at in group]))
        for array, bits, docs_level in self.received:
            _, at = add(array, bits, docs_level)
            start = 0
            for rows, addends in job.parts:
                addends.append((at, start))
                start += rows
        return job

    def seg_job(self):
        bit = self.order[self.seg_done]
        job = self.job(bit, None)
        self.seg_done += 1
        self.waiting = ("seg", bit)
        return job

    def docs_job(self, bit):
        job = self.job(None, lambda: 1 - my_bit("docs", bit))
        self.docs_done.append(bit)
        self.waiting = ("docs", bit)
        return job

    def settle_job(self):
        return self.job(None, None)

    def send(self, value):
        axis, bit = self.waiting
        left = [bit for bit in self.bits if bit not in self.order[: self.seg_done]]
        self.received.append((partner(value, axis, bit), left, len(self.docs_done)))

    def further(self, bits, tokens=()):
        while self.seg_done < bits:
            (value,) = run([self.seg_job()], tokens)
            self.send(value)


def finish_kernel(groups, outputs, small_at, *refs):
    me = lax.axis_index("docs")
    outs = refs[-outputs:]
    for first, count, reduce_x, span, cuts in groups:
        pieces = refs[first : first + count]
        rows = span[1] - span[0]

        def piece(target):
            value = pieces[0][span[0] : span[1], :].astype(F32)
            for flip in range(1, count):
                value = jnp.where(
                    (me & (count - 1)) ^ flip == target, pieces[flip][span[0] : span[1], :].astype(F32), value
                )
            return value

        for core in range(2):
            parts = [piece(2 * x + core) for x in range(count // 2)]
            if reduce_x:
                total = parts[0]
                for part in parts[1:]:
                    total = total + part
                parts = [total]
            for x, part in enumerate(parts):
                place = slice(x * rows, (x + 1) * rows)
                for which, start, end, at in cuts:
                    out = outs[which]
                    base = core * (out.shape[2] // 2) + at
                    out[0, place, base : base + end - start] = part[:, start:end]
    if small_at is None:
        return
    first, count, _, span, _ = groups[-1]
    pieces = refs[first : first + count]
    bias_ref, wide_ref, norm_ref = refs[first + count : first + count + 3]
    total = []
    for x in range(count // 2):
        value = pieces[0][span[1] :, :].astype(F32)
        for flip in range(2, count, 2):
            value = jnp.where((me ^ flip) >> 1 == x, pieces[flip][span[1] :, :].astype(F32), value)
        total.append(value)
    total = jnp.concatenate(total, axis=0)
    below = [(bias_ref, at) for at in range(4)] + [(norm_ref, at) for at in range(4)] + [(wide_ref, 0)]
    for row, (ref, at) in enumerate(below):
        out = outs[small_at + row]
        size = out.shape[1]
        out[0:1, :] = total[row : row + 1, :size]
        out[1:2, :] = ref[at : at + 1, :size]


def docs_pieces(value, count=None):
    pieces = []
    for flip in range(0, count or lax.axis_size("docs"), 2):
        pieces.append(flipped(value, "docs", flip) if flip else value)
        pieces.append(partner(pieces[-1], "docs", 0))
    return pieces


def finish(groups, outputs, small=None, tokens=()):
    operands, layout, seen = [], [], {}
    for pieces, reduce_x, span, cuts in groups:
        if id(pieces) not in seen:
            seen[id(pieces)] = len(operands)
            operands += pieces
        layout.append((seen[id(pieces)], len(pieces), reduce_x, span, cuts))
    out_specs = [pl.BlockSpec((1,) + item.shape[1:], lambda i: (0, 0, 0)) for item in outputs]
    out_shape = [jax.ShapeDtypeStruct(item.shape, F32) for item in outputs]
    if small:
        operands += small[0]
        out_specs += [whole((2, size)) for size in small[1]]
        out_shape += [jax.ShapeDtypeStruct((2, size), F32) for size in small[1]]
    count = len(operands)
    return pl.pallas_call(
        functools.partial(finish_kernel, layout, len(out_shape), len(outputs) if small else None),
        grid=(1,),
        in_specs=[whole(item.shape) for item in operands] + token_specs(outputs) + token_specs(tokens),
        out_specs=out_specs,
        out_shape=out_shape,
        input_output_aliases={count + at: at for at in range(len(outputs))},
        compiler_params=params(),
        cost_estimate=cost(),
        name="finish",
    )(*operands, *outputs, *tokens)


def small_kernel(low_ref, middle_ref, top_ref, kept_ref, sent_ref, out_ref):
    first = lax.axis_index("docs") % 2 == 0
    out_ref[...] = jnp.zeros_like(out_ref)
    shards, _, _ = out_ref.shape
    part = low_ref.shape[1] // shards
    items = [(low_ref, 0), (low_ref, 1), (middle_ref, 2), (top_ref, 2)]
    items += [(middle_ref, 0), (middle_ref, 1), (top_ref, 0), (top_ref, 1)]
    for shard in range(shards):
        for row, (ref, at) in enumerate(items):
            value = ref[at : at + 1, shard * part : (shard + 1) * part]
            out_ref[shard, row : row + 1, :part] = value.astype(LOW)
        half = shards // 2
        wide = kept_ref.shape[1] // half
        place = slice(shard % half * wide, (shard % half + 1) * wide)
        mine = first if shard < half else jnp.logical_not(first)
        value = jnp.where(mine, kept_ref[0:1, place], sent_ref[0:1, place])
        out_ref[shard, 8:9, :wide] = value.astype(LOW)


def small_rows(low, middle, top, kept, sent, segments):
    width = low.shape[1]
    return pl.pallas_call(
        small_kernel,
        out_shape=jax.ShapeDtypeStruct((segments, 16, width), LOW),
        compiler_params=params(),
        cost_estimate=cost(),
        name="small_rows",
    )(low, middle, top, kept, sent)


def cross_grad_kernel(segments, width, hidden, count, *refs):
    bundles = refs[:count]
    attn_ref, proj_ref, inner_ref, outer_ref, bias_ref, wide_ref, norm_ref, place_ref = refs[-8:]
    places, _ = bundle_places(width, hidden, segments)

    def rows(at):
        start, size = places[at]
        return jnp.concatenate([ref[:, start : start + size] for ref in bundles], axis=0)

    outs = (attn_ref, proj_ref, inner_ref, outer_ref)
    biases = []
    for at, out in enumerate(outs):
        right = rows(4 + at)
        out[0] = dot_lt(rows(at), right)[: out.shape[1]]
        biases.append(colsum(right.astype(F32)))
    seg = lax.axis_index("seg")

    def own(value, slot):
        step = value.shape[1] // segments
        value = jnp.broadcast_to(value, (8, value.shape[1]))
        return pltpu.roll(value, lax.rem(value.shape[1] - seg * step, value.shape[1]), 1)[0:1, :slot]

    slot = places[0][1]
    mixed = biases[0]
    parts = [mixed[:, :width], mixed[:, 2 * width :], biases[1], biases[3]]
    bias_ref[...] = jnp.concatenate([own(part, slot) for part in parts] + [jnp.zeros((4, slot), F32)], axis=0)
    wide_ref[...] = jnp.broadcast_to(own(biases[2], places[3][1]), wide_ref.shape)
    start, size = places[8]
    sums = bundles[0][:, start : start + size].astype(F32)
    for ref in bundles[1:]:
        sums = sums + ref[:, start : start + size].astype(F32)
    norm_ref[...] = sums[:8]
    place_ref[...] = sums[8 : 8 + segments, : place_ref.shape[1]]


def cross_grads(bundles, segments, width, hidden, tokens=()):
    part, wide = width // segments, hidden // segments
    places, _ = bundle_places(width, hidden, segments)
    slot = places[0][1]
    stacked = [(part, 3 * width), (part, width), (part, hidden), (wide, width)]
    plain = [(8, slot), (8, places[3][1]), (8, slot), (segments, part)]
    return pl.pallas_call(
        functools.partial(cross_grad_kernel, segments, width, hidden, len(bundles)),
        grid=(1,),
        in_specs=[whole(bundles[0].shape)] * len(bundles) + token_specs(tokens),
        out_specs=[pl.BlockSpec((1,) + item, lambda i: (1, 0, 0)) for item in stacked]
        + [whole(item) for item in plain],
        out_shape=[jax.ShapeDtypeStruct((2,) + item, F32) for item in stacked]
        + [jax.ShapeDtypeStruct(item, F32) for item in plain],
        compiler_params=params(),
        cost_estimate=cost(),
        name="cross_grads",
    )(*bundles, *tokens)


def on_device(
    tokens,
    doc_length,
    attn_weight,
    query_bias,
    value_bias,
    proj_weight,
    proj_bias,
    norm1_gain,
    norm1_shift,
    inner_weight,
    inner_bias,
    outer_weight,
    outer_bias,
    norm2_gain,
    norm2_shift,
    seg_position,
    cotangent,
):
    docs_here, _, seg_len, width = tokens.shape
    hidden = inner_weight.shape[2]
    segments = lax.axis_size("seg")
    core = (lax.axis_index("docs") % 2).astype(jnp.int32).reshape(1)
    total = docs_here * seg_len
    rows_low = tokens.reshape(total, width)
    cots = cotangent.reshape(total, width)
    seg_bits = bits_of("seg")
    across_bits = list(range(bits_of("docs") - 1, 0, -1))

    qkv, attended, normed_one, hidden_low, rstd_one = attend(
        rows_low, doc_length, seg_len, attn_weight, query_bias, value_bias, proj_weight, proj_bias,
        norm1_gain, norm1_shift,
    )
    ff_weights = (inner_weight, inner_bias, outer_weight, outer_bias, norm2_gain, norm2_shift)
    leaders = lead(hidden_low, cots, docs_here, *ff_weights)
    pieces = first_rows_pieces(leaders)
    active, slope, seg_low, normed_two, rstd_two = feed(hidden_low, *ff_weights)

    cross_out, cross_back, bundle, branch_two, top_sums = cross_block(
        pieces, seg_position, doc_length, seg_len,
        attn_weight, query_bias, value_bias, proj_weight, proj_bias, norm1_gain, norm1_shift,
        inner_weight, inner_bias, outer_weight, outer_bias, norm2_gain, norm2_shift, cots, normed_two, rstd_two,
    )

    bundles = [bundle]
    for bit in across_bits:
        bundles = bundles + [partner(item, "docs", bit) for item in bundles]

    top_sums, outer_sent, outer_kept, layer_out, branch_two = top_back(
        cross_back, cross_out, seg_low, seg_len, normed_two, rstd_two, norm2_gain, top_sums, branch_two, active
    )
    outer_got = partner(outer_sent, "docs", 0)
    half_grad, inner_sums_sent, inner_sent = middle_first(
        core, branch_two, hidden_low, slope, inner_weight, outer_weight
    )

    def sharded(value):
        return value.reshape(segments, -1, value.shape[-1])

    rising = list(range(seg_bits))
    far_first = [0] + rising[:0:-1]
    outer = Flow([[sharded(outer_kept), sharded(outer_got)]], far_first)
    (outer_next,) = run([outer.seg_job()], (inner_sent,))
    outer.send(outer_next)
    inner_got = partner(inner_sent, "docs", 0)
    branch_one, mid_sums, inner_sums_kept, inner_kept = middle_last(
        core, branch_two, hidden_low, slope, inner_weight, outer_weight, norm1_gain,
        half_grad, normed_one, rstd_one, (outer_next,),
    )
    inner = Flow([[sharded(inner_kept), sharded(inner_got)]], rising)
    for bit in across_bits:
        (inner_next,) = run([inner.docs_job(bit)])
        inner.send(inner_next)
    mixed_grad, input_grad, low_sums = attend_back(
        branch_one, qkv, doc_length, seg_len, attn_weight, proj_weight, (inner_next,) + tuple(bundles[1:])
    )
    input_grad = input_grad.reshape(tokens.shape)
    others = [partner(item, "docs", 0) for item in bundles]
    left_sent, right_sent = last_grads(1 - core, rows_low, attended, mixed_grad, branch_one)
    for bit in across_bits[:-1]:
        (outer_next,) = run([outer.docs_job(bit)], (left_sent,))
        outer.send(outer_next)
    outer_next, inner_next = run([outer.docs_job(across_bits[-1]), inner.seg_job()], (left_sent, *others))
    outer.send(outer_next)
    inner.send(inner_next)
    bundles = bundles + others
    small = small_rows(low_sums, mid_sums, top_sums, inner_sums_kept, inner_sums_sent, segments)
    left_sent, right_sent, small = gated((left_sent, right_sent, small), (outer_next, inner_next))
    left_got, right_got, small_got = (partner(item, "docs", 0) for item in (left_sent, right_sent, small))
    left_kept, right_kept = last_grads(core, rows_low, attended, mixed_grad, branch_one, (left_sent,))
    attn_out, proj_out, inner_out, outer_out, cross_bias, cross_wide, cross_norm, position_grad = cross_grads(
        bundles, segments, width, hidden, (left_kept,)
    )
    left = Flow([[sharded(left_kept), sharded(left_got)]], rising)
    right = Flow([[sharded(right_kept), sharded(right_got)], [small, small_got]], far_first)
    flows = (left, right, inner, outer)

    def advance(jobs, of, tokens=()):
        values = run(jobs, tokens)
        for flow, value in zip(of, values):
            flow.send(value)
        return values

    for bit in across_bits[:-1]:
        advance([left.docs_job(bit)], (left,))
    last = advance(
        [left.docs_job(across_bits[-1]), right.seg_job(), inner.seg_job(), outer.seg_job()], flows, (cross_bias,)
    )
    for bit in across_bits[:-1]:
        advance([right.docs_job(bit)], (right,))
    last = advance([left.seg_job(), right.docs_job(across_bits[-1]), inner.seg_job(), outer.seg_job()], flows)
    inner.further(seg_bits, last)
    outer.further(seg_bits, last)
    values = run([left.seg_job(), right.seg_job(), inner.settle_job(), outer.settle_job()])
    left.send(values[0])
    right.send(values[1])
    inner, outer = (docs_pieces(value.reshape(value.shape[1:])) for value in values[2:])
    while left.seg_done < seg_bits:
        last = advance([left.seg_job(), right.seg_job()], (left, right))
    (outer_out,) = finish(
        [(outer, False, (0, outer[0].shape[0]), [(0, 0, width // 2, 0)])], [outer_out], tokens=last
    )
    span = inner[0].shape[0]
    (inner_out,) = finish([(inner, False, (0, span), [(0, 0, hidden // 2, 0)])], [inner_out], tokens=(outer_out,))
    (last,) = run([joined(left.settle_job(), right.settle_job())], (inner_out,))
    last = docs_pieces(last.reshape(last.shape[1:]))
    part, wide = width // segments, hidden // segments
    third = width // 2
    attn_out, proj_out, *smalls = finish(
        [
            (last, False, (0, span), [(0, 0, third, 0), (1, third, width, 0)]),
            (last, False, (span, 2 * span), [(0, 0, width, third)]),
        ],
        [attn_out, proj_out],
        ([cross_bias, cross_wide, cross_norm], [part] * 8 + [wide]),
    )
    qb, vb, pb, ob, g1, s1, g2, s2, ib = smalls
    return (
        layer_out.reshape(tokens.shape),
        input_grad,
        attn_out,
        qb,
        vb,
        proj_out,
        pb,
        g1,
        s1,
        inner_out,
        ib,
        outer_out,
        ob,
        g2,
        s2,
        position_grad,
    )


def solution(mesh):
    return jax.shard_map(
        on_device,
        mesh=mesh,
        in_specs=(
            P("docs", "seg", None, None),
            P("docs"),
            P(),
            P(),
            P(),
            P(),
            P(),
            P(),
            P(),
            P(),
            P(),
            P(),
            P(),
            P(),
            P(),
            P(),
            P("docs", "seg", None, None),
        ),
        out_specs=(
            P("docs", "seg", None, None),
            P("docs", "seg", None, None),
            P(None, "seg", None),
            P(None, "seg"),
            P(None, "seg"),
            P(None, "seg", None),
            P(None, "seg"),
            P(None, "seg"),
            P(None, "seg"),
            P(None, "seg", None),
            P(None, "seg"),
            P(None, "seg", None),
            P(None, "seg"),
            P(None, "seg"),
            P(None, "seg"),
            P(None, "seg"),
        ),
        check_vma=False,
    )
```

```python
import functools
import math

import jax
import jax.numpy as jnp
from jax import lax
from jax.experimental import pallas as pl
from jax.experimental.pallas import tpu as pltpu
from jax.sharding import PartitionSpec as P

HEADS = 12
HEAD = 64
PAIR = 2 * HEAD


NEG = -1e30
EPS = 1e-05
LOW = jnp.bfloat16
F32 = jnp.float32
MIB = 1024 * 1024
TILE = 512
WIDE = 1024


def dot(left, right):
    return lax.dot_general(left, right, (((1,), (0,)), ((), ())), preferred_element_type=F32)


def dot_rt(left, right):
    return lax.dot_general(left, right, (((1,), (1,)), ((), ())), preferred_element_type=F32)


def dot_lt(left, right):
    return lax.dot_general(left, right, (((0,), (0,)), ((), ())), preferred_element_type=F32)


def normalize(rows):
    center = rows - jnp.mean(rows, axis=-1, keepdims=True)
    rstd = lax.rsqrt(jnp.mean(center * center, axis=-1, keepdims=True) + EPS)
    return center * rstd, rstd


def norm_back(grad, gain, normed, rstd):
    scaled = grad * gain
    return rstd * (
        scaled
        - jnp.mean(scaled, axis=-1, keepdims=True)
        - normed * jnp.mean(scaled * normed, axis=-1, keepdims=True)
    )


def gelu_and_slope(inner):
    kind = inner.dtype.type
    size = jnp.abs(inner)
    t = kind(1.0) / (kind(1.0) + kind(0.3275911 * 0.7071067811865476) * size)
    bell = jnp.exp(kind(-0.5) * inner * inner)
    series = kind(0.5 * 1.061405429) * t - kind(0.5 * 1.453152027)
    series = series * t + kind(0.5 * 1.421413741)
    series = series * t - kind(0.5 * 0.284496736)
    series = series * t + kind(0.5 * 0.254829592)
    tail = series * t * bell
    below = jnp.where(inner >= kind(0.0), kind(1.0) - tail, tail)
    return inner * below, below + inner * bell * kind(0.3989422804014327)


def colsum(rows):
    return jnp.sum(rows, axis=0, keepdims=True)


def head_masks():
    lane = lax.broadcasted_iota(jnp.int32, (1, PAIR), 1)
    first = (lane < HEAD).astype(F32).astype(LOW)
    second = (lane >= HEAD).astype(F32).astype(LOW)
    return lane, first, second


def whole(shape):
    return pl.BlockSpec(shape, lambda *_: (0,) * len(shape))


def of_block(index, shape):
    return pl.BlockSpec((1,) + shape, lambda *_: (index,) + (0,) * len(shape))


def params(limit_mib=64):
    return pltpu.CompilerParams(vmem_limit_bytes=limit_mib * MIB)


def token_specs(tokens):
    return [pl.BlockSpec(memory_space=pl.ANY)] * len(tokens)


def cost(*_):
    return pl.CostEstimate(flops=1024, bytes_accessed=1024, transcendentals=0)


def attend_kernel(
    groups, length, len_ref, x_ref, w_ref, qb_ref, vb_ref, pw_ref, pb_ref, g1_ref, s1_ref,
    qkv_ref, att_ref, normed_ref, hidden_ref, rstd_ref,
):
    step = pl.program_id(0)
    start = lax.axis_index("seg") * length
    rows_low = x_ref[...]
    width = rows_low.shape[1]
    queries = (dot(rows_low, w_ref[0, :, :width]) + qb_ref[0:1, :].astype(F32)).astype(LOW)
    keys = dot(rows_low, w_ref[0, :, width : 2 * width]).astype(LOW)
    values = (dot(rows_low, w_ref[0, :, 2 * width :]) + vb_ref[0:1, :].astype(F32)).astype(LOW)
    qkv_ref[:, :width] = queries
    qkv_ref[:, width : 2 * width] = keys
    qkv_ref[:, 2 * width :] = values
    queries = queries * LOW(1.0 / math.sqrt(HEAD))
    lane, first, second = head_masks()
    key_lane = lax.broadcasted_iota(jnp.int32, (1, length), 1)
    ones = jnp.ones((length, PAIR), LOW)
    places = []
    for group in range(groups):
        count = jnp.clip(len_ref[step * groups + group] - start, 1, length)
        rows = slice(group * length, (group + 1) * length)
        places += [(rows, slice(at, at + PAIR), key_lane < count) for at in range(0, width, PAIR)]
    scores = []
    for rows, cols, _ in places:
        both = queries[rows, cols]
        both = jnp.concatenate([both * first, both * second], axis=0)
        scores.append(dot_rt(both, keys[rows, cols]))
    weights = []
    for item, (_, _, valid) in zip(scores, places):
        item = jnp.where(valid, item, NEG)
        weights.append(jnp.exp(item - jnp.max(item, axis=1, keepdims=True)).astype(LOW))
    for item, (rows, cols, _) in zip(weights, places):
        mixed = dot(item, jnp.concatenate([values[rows, cols], ones], axis=1))
        mixed = mixed[:, :PAIR] / mixed[:, PAIR:]
        att_ref[rows, cols] = jnp.where(lane < HEAD, mixed[:length], mixed[length:]).astype(LOW)
    resid = rows_low.astype(F32) + dot(att_ref[...], pw_ref[0]) + pb_ref[0:1, :].astype(F32)
    normed, rstd = normalize(resid)
    normed_ref[...] = normed.astype(LOW)
    hidden_ref[...] = (normed * g1_ref[0:1, :].astype(F32) + s1_ref[0:1, :].astype(F32)).astype(LOW)
    rstd_ref[...] = jnp.broadcast_to(rstd, rstd_ref.shape)


def attend(rows_low, doc_length, seg_len, attn_weight, query_bias, value_bias, proj_weight, proj_bias, g1, s1):
    total, width = rows_low.shape
    groups = 2
    size = groups * seg_len
    return pl.pallas_call(
        functools.partial(attend_kernel, groups, seg_len),
        grid=(total // size,),
        in_specs=[
            pl.BlockSpec(memory_space=pltpu.SMEM),
            pl.BlockSpec((size, width), lambda i: (i, 0)),
            of_block(0, (width, 3 * width)),
            whole(query_bias.shape),
            whole(value_bias.shape),
            of_block(0, (width, width)),
            whole(proj_bias.shape),
            whole(g1.shape),
            whole(s1.shape),
        ],
        out_specs=[
            pl.BlockSpec((size, 3 * width), lambda i: (i, 0)),
            pl.BlockSpec((size, width), lambda i: (i, 0)),
            pl.BlockSpec((size, width), lambda i: (i, 0)),
            pl.BlockSpec((size, width), lambda i: (i, 0)),
            pl.BlockSpec((size, 128), lambda i: (i, 0)),
        ],
        out_shape=[
            jax.ShapeDtypeStruct((total, 3 * width), LOW),
            jax.ShapeDtypeStruct((total, width), LOW),
            jax.ShapeDtypeStruct((total, width), LOW),
            jax.ShapeDtypeStruct((total, width), LOW),
            jax.ShapeDtypeStruct((total, 128), F32),
        ],
        compiler_params=params(),
        cost_estimate=cost(
            2 * total * width * 4 * width + 8 * total * seg_len * width, 16 * MIB, total * seg_len * HEADS
        ),
        name="attend",
    )(doc_length, rows_low, attn_weight, query_bias, value_bias, proj_weight, proj_bias, g1, s1)


def leader_kernel(
    hidden_ref, cot_ref, b1_ref, b2_ref, g2_ref, s2_ref, w1_hbm, w2_hbm, out_ref, w1_ref, w2_ref, sems,
):
    tiles = w1_ref.shape[1] // TILE
    copies = []
    for at in range(tiles):
        cols = slice(at * TILE, (at + 1) * TILE)
        copies.append(
            (
                pltpu.make_async_copy(w1_hbm.at[0, :, cols], w1_ref.at[:, cols], sems.at[0, at]),
                pltpu.make_async_copy(w2_hbm.at[0, cols, :], w2_ref.at[cols, :], sems.at[1, at]),
            )
        )
    for pair in copies:
        for copy in pair:
            copy.start()
    hidden = hidden_ref[:, 0, :]
    total = hidden.astype(F32) + b2_ref[0:1, :].astype(F32)
    for at, pair in enumerate(copies):
        cols = slice(at * TILE, (at + 1) * TILE)
        pair[0].wait()
        active, _ = gelu_and_slope(dot(hidden, w1_ref[:, cols]) + b1_ref[0:1, cols].astype(F32))
        pair[1].wait()
        total = total + dot(active.astype(LOW), w2_ref[cols, :])
    normed, _ = normalize(total)
    out = normed * g2_ref[0:1, :].astype(F32) + s2_ref[0:1, :].astype(F32)
    out_ref[0] = out.astype(LOW)
    out_ref[1] = cot_ref[:, 0, :]


def ff_specs(width, tile, pick=lambda i: i):
    return [
        pl.BlockSpec((1, width, tile), lambda i, *_: (0, 0, pick(i))),
        pl.BlockSpec((2, tile), lambda i, *_: (0, pick(i))),
        pl.BlockSpec((1, tile, width), lambda i, *_: (0, pick(i), 0)),
    ]


def lead(hidden_low, cots, docs, inner_weight, inner_bias, outer_weight, outer_bias, g2, s2):
    width, hidden = inner_weight.shape[1:]
    hidden_low = hidden_low.reshape(docs, -1, width)
    cots = cots.reshape(docs, -1, width)
    hbm = pl.BlockSpec(memory_space=pl.ANY)
    return pl.pallas_call(
        leader_kernel,
        grid=(1,),
        in_specs=[whole((docs, 16, width))] * 2 + [whole((2, hidden))] + [whole((2, width))] * 3 + [hbm] * 2,
        out_specs=whole((2, docs, width)),
        out_shape=jax.ShapeDtypeStruct((2, docs, width), LOW),
        scratch_shapes=[
            pltpu.VMEM((width, hidden), LOW),
            pltpu.VMEM((hidden, width), LOW),
            pltpu.SemaphoreType.DMA((2, hidden // TILE)),
        ],
        compiler_params=params(),
        cost_estimate=cost(),
        name="leaders",
    )(hidden_low, cots, inner_bias, outer_bias, g2, s2, inner_weight, outer_weight)


CHUNK = 256


def feed_kernel(
    low_ref, w1_ref, b1_ref, w2_ref, b2_ref, g2_ref, s2_ref,
    active_ref, slope_ref, out_ref, normed2_ref, rstd2_ref, acc_ref,
):
    step = pl.program_id(0)
    last = pl.num_programs(0) - 1
    chunks = [slice(at, at + CHUNK) for at in range(0, low_ref.shape[0], CHUNK)]
    bias = b1_ref[0:1, :].astype(F32)

    @pl.when(step == 0)
    def _():
        for rows in chunks:
            acc_ref[rows, :] = low_ref[rows, :].astype(F32) + b2_ref[0:1, :].astype(F32)

    inner = dot(low_ref[chunks[0], :], w1_ref[0])
    for at, rows in enumerate(chunks):
        active, slope = gelu_and_slope((inner + bias).astype(LOW))
        if at + 1 < len(chunks):
            inner = dot(low_ref[chunks[at + 1], :], w1_ref[0])
        active_ref[rows, :] = active
        slope_ref[rows, :] = slope
        acc_ref[rows, :] += dot(active, w2_ref[0])

    @pl.when(step == last)
    def _():
        for rows in chunks:
            normed, rstd = normalize(acc_ref[rows, :])
            normed2_ref[rows, :] = normed.astype(LOW)
            rstd2_ref[rows, :] = jnp.broadcast_to(rstd, (CHUNK, 128))
            out = normed * g2_ref[0:1, :].astype(F32) + s2_ref[0:1, :].astype(F32)
            out_ref[rows, :] = out.astype(LOW)


def feed(hidden_low, inner_weight, inner_bias, outer_weight, outer_bias, g2, s2):
    total, width = hidden_low.shape
    hidden = inner_weight.shape[2]
    return pl.pallas_call(
        feed_kernel,
        grid=(hidden // TILE,),
        in_specs=[whole((total, width))] + ff_specs(width, TILE) + [whole((2, width))] * 3,
        out_specs=[
            pl.BlockSpec((total, TILE), lambda i: (0, i)),
            pl.BlockSpec((total, TILE), lambda i: (0, i)),
            whole((total, width)),
            whole((total, width)),
            whole((total, 128)),
        ],
        out_shape=[
            jax.ShapeDtypeStruct((total, hidden), LOW),
            jax.ShapeDtypeStruct((total, hidden), LOW),
            jax.ShapeDtypeStruct((total, width), LOW),
            jax.ShapeDtypeStruct((total, width), LOW),
            jax.ShapeDtypeStruct((total, 128), F32),
        ],
        scratch_shapes=[pltpu.VMEM((total, width), F32)],
        compiler_params=params(),
        cost_estimate=cost(),
        name="feed",
    )(hidden_low, inner_weight, inner_bias, outer_weight, outer_bias, g2, s2)


def slots(columns):
    return -(-columns // 128) * 128


def bundle_places(width, hidden, segments):
    own = slots(width // segments)
    sizes = [own, own, own, slots(hidden // segments), 3 * width, width, hidden, width, own]
    places, start = [], 0
    for size in sizes:
        places.append((start, size))
        start += size
    return places, start


def cross_kernel(docs, segments, length, len_ref, *refs):
    pieces, refs = refs[: segments // 2], refs[segments // 2 :]
    (
        pos_ref, qb_ref, vb_ref, pb_ref, g1_ref, s1_ref, b1_ref, b2_ref, g2_ref, s2_ref,
        seg_cot_ref, seg_normed_ref, seg_rstd_ref, aw_hbm, pw_hbm, w1_hbm, w2_hbm,
        out_ref, back_ref, bundle_ref, seg_branch_ref, seg_sums_ref,
        aw_ref, pw_ref, w1_ref, w2_ref, inner_ref, probs_ref, low_ref, att_ref, hid_ref, act_ref,
        lead_ref, cot_ref, sems,
    ) = refs
    width = lead_ref.shape[1]
    hidden = w1_ref.shape[1]
    places, _ = bundle_places(width, hidden, segments)
    dmix_ref, dproj_ref, dinner_ref, dout_ref = (
        bundle_ref.at[:, places[at][0] : places[at][0] + places[at][1]] for at in range(4, 8)
    )
    copies = [
        pltpu.make_async_copy(src.at[1], dst, sems.at[i])
        for i, (src, dst) in enumerate(
            [(aw_hbm, aw_ref), (pw_hbm, pw_ref), (w1_hbm, w1_ref), (w2_hbm, w2_ref)]
        )
    ]
    for copy in copies:
        copy.start()
    total = lead_ref.shape[0]
    scale = 1.0 / math.sqrt(HEAD)

    def row(ref):
        return ref[1:2, :].astype(F32)

    me = lax.axis_index("seg")
    for at, piece in enumerate(pieces):
        for half in range(2):
            seg = me ^ (2 * at + half)
            for doc in range(docs):
                place = pl.ds(doc * segments + seg, 1)
                lead_ref[place, :] = piece[2 * half, doc : doc + 1, :].astype(F32)
                cot_ref[place, :] = piece[2 * half + 1, doc : doc + 1, :].astype(F32)
    rows = lead_ref[...] + jnp.concatenate([pos_ref[...].astype(F32)] * docs, axis=0)
    rows_low = rows.astype(LOW)
    low_ref[...] = rows_low
    both_heads = (total, 2 * total)
    key = lax.broadcasted_iota(jnp.int32, both_heads, 0)
    query = lax.broadcasted_iota(jnp.int32, both_heads, 1) % total
    key_doc = key // segments
    reach = jnp.zeros(both_heads, jnp.int32)
    for doc in range(docs):
        reach = jnp.where(key_doc == doc, len_ref[doc], reach)
    valid = (key_doc == query // segments) & ((key - key_doc * segments) * length < reach)
    lane, first, second = head_masks()

    later_row = lax.broadcasted_iota(jnp.int32, (length, 1), 0) > 0
    seg_gain = g2_ref[0:1, :].astype(F32)
    seg_sums = [jnp.zeros((1, width), F32)] * 3
    for at in range(0, seg_cot_ref.shape[0], length):
        span = slice(at, at + length)
        upper = jnp.where(later_row, seg_cot_ref[span, :].astype(F32), 0.0)
        normed = seg_normed_ref[span, :].astype(F32)
        branch = norm_back(upper, seg_gain, normed, seg_rstd_ref[span, 0:1]).astype(LOW)
        seg_branch_ref[span, :] = branch
        for which, item in enumerate((upper * normed, upper, branch.astype(F32))):
            seg_sums[which] = seg_sums[which] + colsum(item)
    seg_sums_ref[...] = jnp.concatenate(seg_sums + [jnp.zeros((5, width), F32)], axis=0)

    copies[0].wait()
    queries = (dot(rows_low, aw_ref[:, :width]) + row(qb_ref)).astype(LOW)
    keys = dot(rows_low, aw_ref[:, width : 2 * width]).astype(LOW)
    values = (dot(rows_low, aw_ref[:, 2 * width :]) + row(vb_ref)).astype(LOW)

    def stacked(both):
        return jnp.concatenate([both * first, both * second], axis=0)

    def picked(both):
        return jnp.where(lane < HEAD, both[:total], both[total:])

    pair_cols = [slice(at, at + PAIR) for at in range(0, width, PAIR)]
    query_both = [stacked(queries[:, cols]) for cols in pair_cols]
    scores = [dot_rt(keys[:, cols], both) for cols, both in zip(pair_cols, query_both)]
    probs_low = []
    for pair, item in enumerate(scores):
        item = jnp.where(valid, item * scale, NEG)
        weights = jnp.exp(item - jnp.max(item, axis=0, keepdims=True))
        probs = weights / jnp.sum(weights, axis=0, keepdims=True)
        probs_ref[pair] = probs
        probs_low.append(probs.astype(LOW))
    for cols, item in zip(pair_cols, probs_low):
        att_ref[:, cols] = picked(dot_lt(item, values[:, cols])).astype(LOW)
    copies[1].wait()
    resid = rows + dot(att_ref[...], pw_ref[...]) + row(pb_ref)
    normed_one, rstd_one = normalize(resid)
    hidden = normed_one * row(g1_ref) + row(s1_ref)
    hidden_low = hidden.astype(LOW)
    hid_ref[...] = hidden_low
    copies[2].wait()
    copies[3].wait()
    count = w1_ref.shape[1] // WIDE
    branch = jnp.zeros((total, width), F32)
    for at in range(count):
        cols = slice(at * WIDE, (at + 1) * WIDE)
        active, slope = gelu_and_slope(dot(hidden_low, w1_ref[:, cols]) + b1_ref[1:2, cols].astype(F32))
        inner_ref[:, cols] = slope
        active = active.astype(LOW)
        act_ref[:, cols] = active
        branch += dot(active, w2_ref[cols, :])
    normed_two, rstd_two = normalize(hidden + branch + row(b2_ref))
    out_ref[...] = normed_two * row(g2_ref) + row(s2_ref)

    upper = cot_ref[...]
    sums = [colsum(upper * normed_two), colsum(upper)]
    resid_two = norm_back(upper, row(g2_ref), normed_two, rstd_two)
    branch_two = resid_two.astype(LOW)
    dout_ref[...] = branch_two
    hidden_grad = resid_two
    for at in range(count):
        cols = slice(at * WIDE, (at + 1) * WIDE)
        inner_grad = (dot_rt(branch_two, w2_ref[cols, :]) * inner_ref[:, cols]).astype(LOW)
        dinner_ref[:, cols] = inner_grad
        hidden_grad += dot_rt(inner_grad, w1_ref[:, cols])
    sums = [colsum(hidden_grad * normed_one), colsum(hidden_grad)] + sums
    resid_one = norm_back(hidden_grad, row(g1_ref), normed_one, rstd_one)
    branch_one = resid_one.astype(LOW)
    dproj_ref[...] = branch_one
    att_grad = dot_rt(branch_one, pw_ref[...]).astype(LOW)
    att_both = [stacked(att_grad[:, cols]) for cols in pair_cols]
    prob_grads = [dot_rt(values[:, cols], both) for cols, both in zip(pair_cols, att_both)]
    score_grads = []
    for pair, prob_grad in enumerate(prob_grads):
        probs = probs_ref[pair]
        score_grad = probs * (prob_grad - jnp.sum(prob_grad * probs, axis=0, keepdims=True))
        score_grads.append(score_grad.astype(LOW))
    for pair, cols in enumerate(pair_cols):
        cols_k, cols_v = (slice(cols.start + at * width, cols.stop + at * width) for at in (1, 2))
        dmix_ref[:, cols] = (picked(dot_lt(score_grads[pair], keys[:, cols])) * scale).astype(LOW)
        dmix_ref[:, cols_k] = (dot(score_grads[pair], query_both[pair]) * scale).astype(LOW)
        dmix_ref[:, cols_v] = dot(probs_ref[pair].astype(LOW), att_both[pair]).astype(LOW)
    back = resid_one + dot_rt(dmix_ref[...], aw_ref[...])
    back_ref[...] = back
    seg = lax.axis_index("seg")

    def own(value, slot):
        step = value.shape[1] // segments
        return pltpu.roll(value.astype(F32), lax.rem(value.shape[1] - seg * step, value.shape[1]), 1)[:, :slot]

    for at, item in enumerate((low_ref, att_ref, hid_ref, act_ref)):
        start, slot = places[at]
        bundle_ref[:, start : start + slot] = own(item[...], slot).astype(LOW)
    start, slot = places[8]
    by_segment = back[:segments]
    for doc in range(1, docs):
        by_segment += back[doc * segments : (doc + 1) * segments]
    pieces = [own(jnp.concatenate(sums + [jnp.zeros((4, width), F32)], axis=0), slot), own(by_segment, slot)]
    rest = total - 8 - segments
    if rest:
        pieces.append(jnp.zeros((rest, slot), F32))
    bundle_ref[:, start : start + slot] = jnp.concatenate(pieces, axis=0).astype(LOW)


def cross_block(
    pieces, position, doc_length, seg_len,
    attn_weight, query_bias, value_bias, proj_weight, proj_bias, g1, s1,
    inner_weight, inner_bias, outer_weight, outer_bias, g2, s2, seg_cots, seg_normed, seg_rstd,
):
    segments, width = position.shape
    docs = pieces[0].shape[1]
    total = docs * segments
    hidden = inner_weight.shape[2]
    vmem = pl.BlockSpec(memory_space=pltpu.VMEM)
    hbm = pl.BlockSpec(memory_space=pl.ANY)

    def shape(columns, dtype=LOW):
        return jax.ShapeDtypeStruct((total, columns), dtype)

    return pl.pallas_call(
        functools.partial(cross_kernel, docs, segments, seg_len),
        in_specs=[pl.BlockSpec(memory_space=pltpu.SMEM)] + [vmem] * (len(pieces) + 13) + [hbm] * 4,
        out_specs=[vmem] * 5,
        out_shape=[
            shape(width, F32),
            shape(width, F32),
            shape(bundle_places(width, hidden, segments)[1]),
            jax.ShapeDtypeStruct(seg_cots.shape, LOW),
            jax.ShapeDtypeStruct((8, width), F32),
        ],
        scratch_shapes=[
            pltpu.VMEM((width, 3 * width), LOW),
            pltpu.VMEM((width, width), LOW),
            pltpu.VMEM((width, hidden), LOW),
            pltpu.VMEM((hidden, width), LOW),
            pltpu.VMEM((total, hidden), F32),
            pltpu.VMEM((HEADS // 2, total, 2 * total), F32),
            pltpu.VMEM((total, width), LOW),
            pltpu.VMEM((total, width), LOW),
            pltpu.VMEM((total, width), LOW),
            pltpu.VMEM((total, hidden), LOW),
            pltpu.VMEM((total, width), F32),
            pltpu.VMEM((total, width), F32),
            pltpu.SemaphoreType.DMA((4,)),
        ],
        compiler_params=params(),
        cost_estimate=cost(4 * total * width * (4 * width + 2 * hidden) * 2, 2 * width * (4 * width + 2 * hidden)),
        name="cross_block",
    )(
        doc_length, *pieces, position, query_bias, value_bias, proj_bias, g1, s1,
        inner_bias, outer_bias, g2, s2, seg_cots, seg_normed, seg_rstd,
        attn_weight, proj_weight, inner_weight, outer_weight,
    )


def top_kernel(
    segments, back_ref, cross_ref, low_ref, normed_ref, rstd_ref, g2_ref, first_sums_ref, branch_ref, active_ref,
    sums_ref, sent_ref, kept_ref, patched_ref, branch_out_ref, swap_ref,
):
    step = pl.program_id(0)
    docs, length, width = branch_ref.shape
    half = width // 2

    @pl.when(step == 0)
    def _():
        core = lax.axis_index("docs") % 2
        seg = lax.axis_index("seg")
        first_row = lax.broadcasted_iota(jnp.int32, (low_ref.shape[1], 1), 0) == 0

        def own(ref):
            return jnp.concatenate([ref[pl.ds(doc * segments + seg, 1), :] for doc in range(docs)], axis=0)

        upper = own(back_ref)
        normed = normed_ref[:, 0, :].astype(F32)
        branch = norm_back(upper, g2_ref[0:1, :].astype(F32), normed, rstd_ref[:, 0, 0:1]).astype(LOW).astype(F32)
        for at, item in enumerate((upper * normed, upper, branch)):
            sums_ref[at : at + 1, :] = first_sums_ref[at : at + 1, :] + colsum(item)
        sums_ref[3:8, :] = jnp.zeros((5, width), F32)
        cross = own(cross_ref)
        top_rows = low_ref.shape[1]
        for doc in range(docs):
            patched_ref[doc] = jnp.where(first_row, cross[doc : doc + 1, :], low_ref[doc].astype(F32)).astype(LOW)
            top_part = jnp.where(first_row, branch[doc : doc + 1, :], branch_ref[doc, :top_rows, :].astype(F32))
            top_part = top_part.astype(LOW)
            branch_out_ref[doc] = top_part
            rows = slice(doc * length, (doc + 1) * length)
            whole_part = jnp.concatenate([top_part, branch_ref[doc, top_rows:, :]], axis=0)
            left, right = whole_part[:, :half], whole_part[:, half:]
            swap_ref[rows, :half] = jnp.where(core == 0, right, left)
            swap_ref[rows, half:] = jnp.where(core == 0, left, right)

    grad = dot_lt(active_ref[...], swap_ref[...]).astype(LOW)
    sent_ref[...] = grad[:, :half]
    kept_ref[...] = grad[:, half:]


def top_back(back, cross_out, seg_low, seg_len, normed, rstd, g2, sums, branch, active):
    total, width = branch.shape
    hidden = active.shape[1]
    docs = total // seg_len
    first = (docs, 16, width)
    by_doc = (docs, seg_len, width)
    out = pl.pallas_call(
        functools.partial(top_kernel, back.shape[0] // docs),
        grid=(hidden // TILE,),
        in_specs=[
            whole(back.shape),
            whole(back.shape),
            whole(first),
            whole(first),
            whole((docs, 8, 128)),
            whole((2, width)),
            whole((8, width)),
            whole(by_doc),
            pl.BlockSpec((total, TILE), lambda i: (0, i)),
        ],
        out_specs=[
            whole((8, width)),
            pl.BlockSpec((TILE, width // 2), lambda i: (i, 0)),
            pl.BlockSpec((TILE, width // 2), lambda i: (i, 0)),
            whole(first),
            whole(first),
        ],
        out_shape=[
            jax.ShapeDtypeStruct((8, width), F32),
            jax.ShapeDtypeStruct((hidden, width // 2), LOW),
            jax.ShapeDtypeStruct((hidden, width // 2), LOW),
            jax.ShapeDtypeStruct(by_doc, LOW),
            jax.ShapeDtypeStruct(by_doc, LOW),
        ],
        input_output_aliases={2: 3, 7: 4},
        scratch_shapes=[pltpu.VMEM((total, width), LOW)],
        compiler_params=params(),
        cost_estimate=cost(),
        name="top_back",
    )(
        back, cross_out, seg_low.reshape(by_doc), normed.reshape(by_doc), rstd.reshape(docs, seg_len, 128), g2, sums,
        branch.reshape(by_doc), active,
    )
    return out[0], out[1], out[2], out[3], out[4].reshape(total, width)


def middle_step(branch_ref, low_ref, slope_ref, w1_ref, w2_ref, acc_ref, bias_ref, grad_ref, finished=None):
    parts = []
    chunks = [slice(at, at + CHUNK) for at in range(0, branch_ref.shape[0], CHUNK)]
    following = dot_rt(branch_ref[chunks[0], :], w2_ref[0])
    for at, rows in enumerate(chunks):
        part = (following * slope_ref[rows, :].astype(F32)).astype(LOW)
        if at + 1 < len(chunks):
            following = dot_rt(branch_ref[chunks[at + 1], :], w2_ref[0])
        total = acc_ref[rows, :] + dot_rt(part, w1_ref[0])
        if finished:
            finished(rows, total)
        else:
            acc_ref[rows, :] = total
        parts.append(part)
    inner_grad = jnp.concatenate(parts, axis=0)
    bias_ref[...] = jnp.broadcast_to(colsum(inner_grad.astype(F32)), bias_ref.shape)
    grad_ref[...] = dot_lt(low_ref[...], inner_grad).astype(LOW)


def middle_first_kernel(core_ref, branch_ref, low_ref, slope_ref, w1_ref, w2_ref, *refs):
    half_ref, bias_ref, sent_ref, acc_ref = refs[-4:]
    step = pl.program_id(0)
    last = pl.num_programs(0) - 1

    @pl.when(step == 0)
    def _():
        acc_ref[...] = jnp.zeros_like(acc_ref)

    def finished(rows, total):
        half_ref[rows, :] = total.astype(LOW)

    operands = (branch_ref, low_ref, slope_ref, w1_ref, w2_ref, acc_ref, bias_ref, sent_ref)
    pl.when(step < last)(lambda: middle_step(*operands))
    pl.when(step == last)(lambda: middle_step(*operands, finished))


def middle_last_kernel(core_ref, branch_ref, low_ref, slope_ref, w1_ref, w2_ref, g1_ref, *refs):
    half_hbm, normed_hbm, rstd_hbm = refs[:3]
    branch1_ref, sums_ref, bias_ref, kept_ref, acc_ref, half_ref, normed_ref, rstd_ref, sems = refs[-9:]
    step = pl.program_id(0)
    last = pl.num_programs(0) - 1
    width = branch_ref.shape[1]
    copies = [
        pltpu.make_async_copy(source, target, sems.at[at])
        for at, (source, target) in enumerate(
            ((half_hbm, half_ref), (normed_hbm, normed_ref), (rstd_hbm, rstd_ref))
        )
    ]

    @pl.when(step == 0)
    def _():
        for copy in copies:
            copy.start()
        acc_ref[...] = jnp.zeros_like(acc_ref)

    sums = [jnp.zeros((1, width), F32)] * 3

    def finished(rows, total):
        hidden_grad = total + half_ref[rows, :].astype(F32) + branch_ref[rows, :].astype(F32)
        normed = normed_ref[rows, :].astype(F32)
        resid = norm_back(hidden_grad, g1_ref[0:1, :].astype(F32), normed, rstd_ref[rows, 0:1])
        branch = resid.astype(LOW)
        branch1_ref[rows, :] = branch
        for at, item in enumerate((hidden_grad * normed, hidden_grad, branch.astype(F32))):
            sums[at] = sums[at] + colsum(item)

    operands = (branch_ref, low_ref, slope_ref, w1_ref, w2_ref, acc_ref, bias_ref, kept_ref)
    pl.when(step < last)(lambda: middle_step(*operands))

    @pl.when(step == last)
    def _():
        for copy in copies:
            copy.wait()
        middle_step(*operands, finished)
        sums_ref[...] = jnp.concatenate(sums + [jnp.zeros((5, width), F32)], axis=0)


def half_order(steps):
    half = steps // 2

    def pick(step, core_ref):
        return jnp.where(step < half, 1 - core_ref[0], core_ref[0]) * half + step % half

    return pick


def middle_specs(total, width, steps, offset):
    pick = half_order(2 * steps)
    return [
        whole((total, width)),
        whole((total, width)),
        pl.BlockSpec((total, TILE), lambda i, c: (0, pick(i + offset, c))),
        pl.BlockSpec((1, width, TILE), lambda i, c: (0, 0, pick(i + offset, c))),
        pl.BlockSpec((1, TILE, width), lambda i, c: (0, pick(i + offset, c), 0)),
    ]


def middle_first(core, branch, low, slope, inner_weight, outer_weight, tokens=()):
    total, width = branch.shape
    steps = slope.shape[1] // TILE // 2
    return pl.pallas_call(
        middle_first_kernel,
        grid_spec=pltpu.PrefetchScalarGridSpec(
            num_scalar_prefetch=1,
            grid=(steps,),
            in_specs=middle_specs(total, width, steps, 0) + token_specs(tokens),
            out_specs=[
                whole((total, width)),
                pl.BlockSpec((8, TILE), lambda i, c: (0, i)),
                pl.BlockSpec((width, TILE), lambda i, c: (0, i)),
            ],
            scratch_shapes=[pltpu.VMEM((total, width), F32)],
        ),
        out_shape=[
            jax.ShapeDtypeStruct((total, width), LOW),
            jax.ShapeDtypeStruct((8, steps * TILE), F32),
            jax.ShapeDtypeStruct((width, steps * TILE), LOW),
        ],
        compiler_params=params(),
        cost_estimate=cost(),
        name="middle_first",
    )(core, branch, low, slope, inner_weight, outer_weight, *tokens)


def middle_last(core, branch, low, slope, inner_weight, outer_weight, g1, half, normed, rstd, tokens=()):
    total, width = branch.shape
    steps = slope.shape[1] // TILE // 2
    return pl.pallas_call(
        middle_last_kernel,
        grid_spec=pltpu.PrefetchScalarGridSpec(
            num_scalar_prefetch=1,
            grid=(steps,),
            in_specs=middle_specs(total, width, steps, steps)
            + [whole((2, width))]
            + token_specs((half, normed, rstd) + tuple(tokens)),
            out_specs=[
                whole((total, width)),
                whole((8, width)),
                pl.BlockSpec((8, TILE), lambda i, c: (0, i)),
                pl.BlockSpec((width, TILE), lambda i, c: (0, i)),
            ],
            scratch_shapes=[
                pltpu.VMEM((total, width), F32),
                pltpu.VMEM((total, width), LOW),
                pltpu.VMEM((total, width), LOW),
                pltpu.VMEM((total, 128), F32),
                pltpu.SemaphoreType.DMA((3,)),
            ],
        ),
        out_shape=[
            jax.ShapeDtypeStruct((total, width), LOW),
            jax.ShapeDtypeStruct((8, width), F32),
            jax.ShapeDtypeStruct((8, steps * TILE), F32),
            jax.ShapeDtypeStruct((width, steps * TILE), LOW),
        ],
        compiler_params=params(),
        cost_estimate=cost(),
        name="middle_last",
    )(core, branch, low, slope, inner_weight, outer_weight, g1, half, normed, rstd, *tokens)


def attend_back_kernel(groups, length, *refs):
    len_ref, branch_ref, qkv_ref, w_ref, pw_ref = refs[:5]
    dmix_ref, back_ref, sums_ref = refs[-3:]
    step = pl.program_id(0)
    start = lax.axis_index("seg") * length
    width = branch_ref.shape[1]
    scale = LOW(1.0 / math.sqrt(HEAD))
    att_grad = dot_rt(branch_ref[...], pw_ref[0]).astype(LOW)
    lane, first, second = head_masks()
    key_row = lax.broadcasted_iota(jnp.int32, (length, 1), 0)

    def stacked(both):
        return jnp.concatenate([both * first, both * second], axis=0)

    places = []
    for group in range(groups):
        count = jnp.clip(len_ref[step * groups + group] - start, 1, length)
        rows = slice(group * length, (group + 1) * length)
        for at in range(0, width, PAIR):
            cols, cols_k, cols_v = (slice(at + part * width, at + part * width + PAIR) for part in range(3))
            places.append((rows, cols, cols_k, cols_v, key_row < count))
    queries = [stacked(qkv_ref[rows, cols] * scale) for rows, cols, _, _, _ in places]
    att_both = [stacked(att_grad[rows, cols]) for rows, cols, _, _, _ in places]
    scores = [dot_rt(qkv_ref[rows, cols_k], item) for item, (rows, _, cols_k, _, _) in zip(queries, places)]
    prob_grads = [dot_rt(qkv_ref[rows, cols_v], item) for item, (rows, _, _, cols_v, _) in zip(att_both, places)]
    probs, score_grads = [], []
    for item, prob_grad, (_, _, _, _, valid) in zip(scores, prob_grads, places):
        item = jnp.where(valid, item, NEG)
        weights = jnp.exp(item - jnp.max(item, axis=0, keepdims=True))
        prob = weights * (1.0 / jnp.sum(weights, axis=0, keepdims=True))
        score_grad = prob * (prob_grad - jnp.sum(prob_grad * prob, axis=0, keepdims=True))
        probs.append(prob.astype(LOW))
        score_grads.append(score_grad.astype(LOW))
    for at, (rows, cols, cols_k, cols_v, _) in enumerate(places):
        by_query = dot_lt(score_grads[at], qkv_ref[rows, cols_k] * scale)
        dmix_ref[rows, cols] = jnp.where(lane < HEAD, by_query[:length], by_query[length:]).astype(LOW)
        dmix_ref[rows, cols_k] = dot(score_grads[at], queries[at]).astype(LOW)
        dmix_ref[rows, cols_v] = dot(probs[at], att_both[at]).astype(LOW)
    mixed = dmix_ref[...]
    back_ref[...] = branch_ref[...].astype(F32) + dot_rt(mixed, w_ref[0])

    @pl.when(step == 0)
    def _():
        sums_ref[...] = jnp.zeros_like(sums_ref)

    sums_ref[0:1, :] += colsum(mixed[:, :width].astype(F32))
    sums_ref[1:2, :] += colsum(mixed[:, 2 * width :].astype(F32))


def attend_back(branch, qkv, doc_length, seg_len, attn_weight, proj_weight, tokens=()):
    total, width = branch.shape
    groups = 2
    size = groups * seg_len
    return pl.pallas_call(
        functools.partial(attend_back_kernel, groups, seg_len),
        grid=(total // size,),
        in_specs=[
            pl.BlockSpec(memory_space=pltpu.SMEM),
            pl.BlockSpec((size, width), lambda i: (i, 0)),
            pl.BlockSpec((size, 3 * width), lambda i: (i, 0)),
            of_block(0, (width, 3 * width)),
            of_block(0, (width, width)),
        ]
        + token_specs(tokens),
        out_specs=[
            pl.BlockSpec((size, 3 * width), lambda i: (i, 0)),
            pl.BlockSpec((size, width), lambda i: (i, 0)),
            whole((8, width)),
        ],
        out_shape=[
            jax.ShapeDtypeStruct((total, 3 * width), LOW),
            jax.ShapeDtypeStruct((total, width), F32),
            jax.ShapeDtypeStruct((8, width), F32),
        ],
        compiler_params=params(),
        cost_estimate=cost(
            2 * total * width * 4 * width + 20 * total * seg_len * width, 20 * MIB, total * seg_len * HEADS
        ),
        name="attend_back",
    )(doc_length, branch, qkv, attn_weight, proj_weight, *tokens)


def last_grads_kernel(core_ref, rows_ref, att_ref, mixed_ref, branch_ref, *refs):
    left, right = refs[-2:]
    third = branch_ref.shape[1]
    turned = rows_ref[...].T
    left[:, :third] = dot(turned, mixed_ref[:, :third]).astype(LOW)
    right[...] = dot(turned, mixed_ref[:, third:]).astype(LOW)
    left[:, third:] = dot_lt(att_ref[...], branch_ref[...]).astype(LOW)


def last_grads(core, rows, attended, mixed, branch, tokens=()):
    total, width = rows.shape
    out = jax.ShapeDtypeStruct((width, width), LOW)
    return pl.pallas_call(
        last_grads_kernel,
        grid_spec=pltpu.PrefetchScalarGridSpec(
            num_scalar_prefetch=1,
            grid=(width // CHUNK,),
            in_specs=[
                pl.BlockSpec((total, CHUNK), lambda i, c: (0, i)),
                pl.BlockSpec((total, CHUNK), lambda i, c: (0, i)),
                pl.BlockSpec((total, mixed.shape[1] // 2), lambda i, c: (0, c[0])),
                pl.BlockSpec((total, width // 2), lambda i, c: (0, c[0])),
            ]
            + token_specs(tokens),
            out_specs=[pl.BlockSpec((CHUNK, width), lambda i, c: (i, 0))] * 2,
        ),
        out_shape=[out] * 2,
        compiler_params=params(),
        cost_estimate=cost(),
        name="last_grads",
    )(core, rows, attended, mixed, branch, *tokens)


def bits_of(axis):
    return lax.axis_size(axis).bit_length() - 1


def partner(value, axis, bit):
    return flipped(value, axis, 1 << bit)


def flipped(value, axis, mask):
    return lax.ppermute(value, axis, [(i, i ^ mask) for i in range(lax.axis_size(axis))])


def my_bit(axis, bit):
    return (lax.axis_index(axis) >> bit) & 1


def first_rows_pieces(value):
    pair = jnp.concatenate([value, partner(value, "seg", 0)], axis=0)
    return [pair] + [flipped(pair, "seg", flip) for flip in range(2, lax.axis_size("seg"), 2)]


class Job:
    def __init__(self, blocks, columns):
        self.blocks = blocks
        self.columns = columns
        self.operands = []
        self.parts = []

    def add(self, array, place):
        self.operands.append((array, place))
        return len(self.operands) - 1

    def rows(self):
        return sum(rows for rows, _ in self.parts)


def joined(first, second):
    job = Job(first.blocks, first.columns)
    job.operands = first.operands + second.operands
    shift = len(first.operands)
    job.parts = first.parts + [
        (rows, [(at + shift, start) for at, start in addends]) for rows, addends in second.parts
    ]
    return job


def run_kernel(jobs, skip, *refs):
    count = sum(len(job.operands) for job in jobs)
    sources = refs[skip : skip + count]
    outs = refs[skip + count : skip + count + len(jobs)]
    buffers = refs[skip + count + len(jobs) : -len(jobs) - 2]
    ready = refs[-len(jobs) - 2 : -2]
    in_sems, out_sems = refs[-2:]
    arriving, leaving = [], []
    at = sem = 0
    for job in jobs:
        copies = []
        for _, place in job.operands:
            before, after, part = place()
            copies.append(
                [
                    pltpu.make_async_copy(
                        sources[at].at[before, i, after, part], buffers[at].at[i], in_sems.at[sem + i]
                    )
                    for i in range(job.blocks)
                ]
            )
            at += 1
            sem += job.blocks
        for i in range(job.blocks):
            for copy in copies:
                copy[i].start()
        arriving.append(copies)
    at = sem = 0
    for job, copies, out, value in zip(jobs, arriving, outs, ready):
        mine = buffers[at : at + len(job.operands)]
        at += len(job.operands)
        for i in range(job.blocks):
            for copy in copies:
                copy[i].wait()
            start = 0
            for rows, addends in job.parts:
                total = None
                for which, first in addends:
                    item = mine[which][i, first : first + rows, :].astype(F32)
                    total = item if total is None else total + item
                value[i, start : start + rows, :] = total.astype(LOW)
                start += rows
            leaving.append(pltpu.make_async_copy(value.at[i], out.at[i], out_sems.at[sem]))
            leaving[-1].start()
            sem += 1
    for copy in leaving:
        copy.wait()


def run(jobs, tokens=()):
    operands = [array for job in jobs for array, _ in job.operands]
    buffers = [pltpu.VMEM((job.blocks,) + array.shape[4:], LOW) for job in jobs for array, _ in job.operands]
    ready = [pltpu.VMEM((job.blocks, job.rows(), job.columns), LOW) for job in jobs]
    arrivals = sum(job.blocks * len(job.operands) for job in jobs)
    return pl.pallas_call(
        functools.partial(run_kernel, jobs, len(tokens)),
        in_specs=token_specs(tokens) + token_specs(operands),
        out_specs=token_specs(jobs),
        out_shape=[jax.ShapeDtypeStruct((job.blocks, job.rows(), job.columns), LOW) for job in jobs],
        scratch_shapes=buffers
        + ready
        + [pltpu.SemaphoreType.DMA((arrivals,)), pltpu.SemaphoreType.DMA((sum(job.blocks for job in jobs),))],
        compiler_params=params(),
        cost_estimate=cost(),
        name="pick",
    )(*tokens, *operands)


def gate_kernel(*_):
    pass


def gated(values, tokens):
    count = len(values)
    return pl.pallas_call(
        gate_kernel,
        in_specs=token_specs(values) + token_specs(tokens),
        out_specs=token_specs(values),
        out_shape=[jax.ShapeDtypeStruct(item.shape, item.dtype) for item in values],
        input_output_aliases={at: at for at in range(count)},
        cost_estimate=cost(),
        name="gate",
    )(*values, *tokens)


class Flow:
    def __init__(self, groups, order):
        self.groups = groups
        self.received = []
        self.order = order
        self.seg_done = 0
        self.docs_done = []
        self.bits = list(range(bits_of("seg") - 1, -1, -1))
        self.columns = groups[0][0].shape[2]

    def job(self, sent_bit, last):
        docs_done = list(self.docs_done)
        level = len(docs_done) + (last is not None)
        done = self.order[: self.seg_done] + ([sent_bit] if sent_bit is not None else [])
        left = [bit for bit in self.bits if bit not in done]
        job = Job(1 << len(left), self.columns)

        def value(bits):
            index = 0
            for bit in bits:
                mine = my_bit("seg", bit)
                index = index * 2 + (1 - mine if bit == sent_bit else mine)
            return index

        def add(array, bits, docs_level):
            choices = 1 << (level - docs_level)
            rows = array.shape[1] // choices
            before = bits[: bits.index(left[0])] if left else []
            after = bits[bits.index(left[-1]) + 1 :] if left else bits

            def place():
                part = 0
                for bit in [my_bit("docs", bit) for bit in docs_done][docs_level:] + ([last()] if last else []):
                    part = part * 2 + bit
                return value(before), value(after), part

            array = array.reshape(1 << len(before), job.blocks, 1 << len(after), choices, rows, self.columns)
            return rows, job.add(array, place)

        shares = 1 << (bits_of("docs") - 1 - level) if len(self.groups) > 1 else 1
        added = [[add(array, self.bits, 0) for array in group] for group in self.groups]
        for share in range(shares):
            for group in added:
                rows = group[0][0] // shares
                job.parts.append((rows, [(at, share * rows) for _, at in group]))
        for array, bits, docs_level in self.received:
            _, at = add(array, bits, docs_level)
            start = 0
            for rows, addends in job.parts:
                addends.append((at, start))
                start += rows
        return job

    def seg_job(self):
        bit = self.order[self.seg_done]
        job = self.job(bit, None)
        self.seg_done += 1
        self.waiting = ("seg", bit)
        return job

    def docs_job(self, bit):
        job = self.job(None, lambda: 1 - my_bit("docs", bit))
        self.docs_done.append(bit)
        self.waiting = ("docs", bit)
        return job

    def settle_job(self):
        return self.job(None, None)

    def send(self, value):
        axis, bit = self.waiting
        left = [bit for bit in self.bits if bit not in self.order[: self.seg_done]]
        self.received.append((partner(value, axis, bit), left, len(self.docs_done)))

    def further(self, bits, tokens=()):
        while self.seg_done < bits:
            (value,) = run([self.seg_job()], tokens)
            self.send(value)


def finish_kernel(groups, outputs, small_at, *refs):
    me = lax.axis_index("docs")
    outs = refs[-outputs:]
    for first, count, reduce_x, span, cuts in groups:
        pieces = refs[first : first + count]
        rows = span[1] - span[0]

        def piece(target):
            value = pieces[0][span[0] : span[1], :].astype(F32)
            for flip in range(1, count):
                value = jnp.where(
                    (me & (count - 1)) ^ flip == target, pieces[flip][span[0] : span[1], :].astype(F32), value
                )
            return value

        for core in range(2):
            parts = [piece(2 * x + core) for x in range(count // 2)]
            if reduce_x:
                total = parts[0]
                for part in parts[1:]:
                    total = total + part
                parts = [total]
            for x, part in enumerate(parts):
                place = slice(x * rows, (x + 1) * rows)
                for which, start, end, at in cuts:
                    out = outs[which]
                    base = core * (out.shape[2] // 2) + at
                    out[0, place, base : base + end - start] = part[:, start:end]
    if small_at is None:
        return
    first, count, _, span, _ = groups[-1]
    pieces = refs[first : first + count]
    bias_ref, wide_ref, norm_ref = refs[first + count : first + count + 3]
    total = []
    for x in range(count // 2):
        value = pieces[0][span[1] :, :].astype(F32)
        for flip in range(2, count, 2):
            value = jnp.where((me ^ flip) >> 1 == x, pieces[flip][span[1] :, :].astype(F32), value)
        total.append(value)
    total = jnp.concatenate(total, axis=0)
    below = [(bias_ref, at) for at in range(4)] + [(norm_ref, at) for at in range(4)] + [(wide_ref, 0)]
    for row, (ref, at) in enumerate(below):
        out = outs[small_at + row]
        size = out.shape[1]
        out[0:1, :] = total[row : row + 1, :size]
        out[1:2, :] = ref[at : at + 1, :size]


def docs_pieces(value, count=None, tokens=()):
    pieces = []
    for flip in range(0, count or lax.axis_size("docs"), 2):
        pieces.append(flipped(value, "docs", flip) if flip else value)
        if flip and tokens:
            (pieces[-1],) = gated((pieces[-1],), tokens)
        pieces.append(partner(pieces[-1], "docs", 0))
    return pieces


def finish(groups, outputs, small=None, tokens=()):
    operands, layout, seen = [], [], {}
    for pieces, reduce_x, span, cuts in groups:
        if id(pieces) not in seen:
            seen[id(pieces)] = len(operands)
            operands += pieces
        layout.append((seen[id(pieces)], len(pieces), reduce_x, span, cuts))
    out_specs = [pl.BlockSpec((1,) + item.shape[1:], lambda i: (0, 0, 0)) for item in outputs]
    out_shape = [jax.ShapeDtypeStruct(item.shape, F32) for item in outputs]
    if small:
        operands += small[0]
        out_specs += [whole((2, size)) for size in small[1]]
        out_shape += [jax.ShapeDtypeStruct((2, size), F32) for size in small[1]]
    count = len(operands)
    return pl.pallas_call(
        functools.partial(finish_kernel, layout, len(out_shape), len(outputs) if small else None),
        grid=(1,),
        in_specs=[whole(item.shape) for item in operands] + token_specs(outputs) + token_specs(tokens),
        out_specs=out_specs,
        out_shape=out_shape,
        input_output_aliases={count + at: at for at in range(len(outputs))},
        compiler_params=params(),
        cost_estimate=cost(),
        name="finish",
    )(*operands, *outputs, *tokens)


def small_kernel(low_ref, middle_ref, top_ref, kept_ref, sent_ref, out_ref):
    first = lax.axis_index("docs") % 2 == 0
    out_ref[...] = jnp.zeros_like(out_ref)
    shards, _, _ = out_ref.shape
    part = low_ref.shape[1] // shards
    items = [(low_ref, 0), (low_ref, 1), (middle_ref, 2), (top_ref, 2)]
    items += [(middle_ref, 0), (middle_ref, 1), (top_ref, 0), (top_ref, 1)]
    for shard in range(shards):
        for row, (ref, at) in enumerate(items):
            value = ref[at : at + 1, shard * part : (shard + 1) * part]
            out_ref[shard, row : row + 1, :part] = value.astype(LOW)
        half = shards // 2
        wide = kept_ref.shape[1] // half
        place = slice(shard % half * wide, (shard % half + 1) * wide)
        mine = first if shard < half else jnp.logical_not(first)
        value = jnp.where(mine, kept_ref[0:1, place], sent_ref[0:1, place])
        out_ref[shard, 8:9, :wide] = value.astype(LOW)


def small_rows(low, middle, top, kept, sent, segments):
    width = low.shape[1]
    return pl.pallas_call(
        small_kernel,
        out_shape=jax.ShapeDtypeStruct((segments, 16, width), LOW),
        compiler_params=params(),
        cost_estimate=cost(),
        name="small_rows",
    )(low, middle, top, kept, sent)


def cross_grad_kernel(segments, width, hidden, count, *refs):
    bundles = refs[:count]
    attn_ref, proj_ref, inner_ref, outer_ref, bias_ref, wide_ref, norm_ref, place_ref = refs[-8:]
    places, _ = bundle_places(width, hidden, segments)

    def rows(at):
        start, size = places[at]
        return jnp.concatenate([ref[:, start : start + size] for ref in bundles], axis=0)

    outs = (attn_ref, proj_ref, inner_ref, outer_ref)
    biases = []
    for at, out in enumerate(outs):
        right = rows(4 + at)
        out[0] = dot_lt(rows(at), right)[: out.shape[1]]
        biases.append(colsum(right.astype(F32)))
    seg = lax.axis_index("seg")

    def own(value, slot):
        step = value.shape[1] // segments
        value = jnp.broadcast_to(value, (8, value.shape[1]))
        return pltpu.roll(value, lax.rem(value.shape[1] - seg * step, value.shape[1]), 1)[0:1, :slot]

    slot = places[0][1]
    mixed = biases[0]
    parts = [mixed[:, :width], mixed[:, 2 * width :], biases[1], biases[3]]
    bias_ref[...] = jnp.concatenate([own(part, slot) for part in parts] + [jnp.zeros((4, slot), F32)], axis=0)
    wide_ref[...] = jnp.broadcast_to(own(biases[2], places[3][1]), wide_ref.shape)
    start, size = places[8]
    sums = bundles[0][:, start : start + size].astype(F32)
    for ref in bundles[1:]:
        sums = sums + ref[:, start : start + size].astype(F32)
    norm_ref[...] = sums[:8]
    place_ref[...] = sums[8 : 8 + segments, : place_ref.shape[1]]


def cross_grads(bundles, segments, width, hidden, tokens=()):
    part, wide = width // segments, hidden // segments
    places, _ = bundle_places(width, hidden, segments)
    slot = places[0][1]
    stacked = [(part, 3 * width), (part, width), (part, hidden), (wide, width)]
    plain = [(8, slot), (8, places[3][1]), (8, slot), (segments, part)]
    return pl.pallas_call(
        functools.partial(cross_grad_kernel, segments, width, hidden, len(bundles)),
        grid=(1,),
        in_specs=[whole(bundles[0].shape)] * len(bundles) + token_specs(tokens),
        out_specs=[pl.BlockSpec((1,) + item, lambda i: (1, 0, 0)) for item in stacked]
        + [whole(item) for item in plain],
        out_shape=[jax.ShapeDtypeStruct((2,) + item, F32) for item in stacked]
        + [jax.ShapeDtypeStruct(item, F32) for item in plain],
        compiler_params=params(),
        cost_estimate=cost(),
        name="cross_grads",
    )(*bundles, *tokens)


def on_device(
    tokens,
    doc_length,
    attn_weight,
    query_bias,
    value_bias,
    proj_weight,
    proj_bias,
    norm1_gain,
    norm1_shift,
    inner_weight,
    inner_bias,
    outer_weight,
    outer_bias,
    norm2_gain,
    norm2_shift,
    seg_position,
    cotangent,
):
    docs_here, _, seg_len, width = tokens.shape
    hidden = inner_weight.shape[2]
    segments = lax.axis_size("seg")
    core = (lax.axis_index("docs") % 2).astype(jnp.int32).reshape(1)
    total = docs_here * seg_len
    rows_low = tokens.reshape(total, width)
    cots = cotangent.reshape(total, width)
    seg_bits = bits_of("seg")
    across_bits = list(range(bits_of("docs") - 1, 0, -1))

    qkv, attended, normed_one, hidden_low, rstd_one = attend(
        rows_low, doc_length, seg_len, attn_weight, query_bias, value_bias, proj_weight, proj_bias,
        norm1_gain, norm1_shift,
    )
    ff_weights = (inner_weight, inner_bias, outer_weight, outer_bias, norm2_gain, norm2_shift)
    leaders = lead(hidden_low, cots, docs_here, *ff_weights)
    pieces = first_rows_pieces(leaders)
    active, slope, seg_low, normed_two, rstd_two = feed(hidden_low, *ff_weights)

    cross_out, cross_back, bundle, branch_two, top_sums = cross_block(
        pieces, seg_position, doc_length, seg_len,
        attn_weight, query_bias, value_bias, proj_weight, proj_bias, norm1_gain, norm1_shift,
        inner_weight, inner_bias, outer_weight, outer_bias, norm2_gain, norm2_shift, cots, normed_two, rstd_two,
    )

    bundles = [bundle]
    for bit in across_bits:
        bundles = bundles + [partner(item, "docs", bit) for item in bundles]

    top_sums, outer_sent, outer_kept, layer_out, branch_two = top_back(
        cross_back, cross_out, seg_low, seg_len, normed_two, rstd_two, norm2_gain, top_sums, branch_two, active
    )
    outer_got = partner(outer_sent, "docs", 0)
    half_grad, inner_sums_sent, inner_sent = middle_first(
        core, branch_two, hidden_low, slope, inner_weight, outer_weight
    )

    def sharded(value):
        return value.reshape(segments, -1, value.shape[-1])

    rising = list(range(seg_bits))
    far_first = [0] + rising[:0:-1]
    outer = Flow([[sharded(outer_kept), sharded(outer_got)]], far_first)
    (outer_next,) = run([outer.seg_job()], (inner_sent,))
    outer.send(outer_next)
    inner_got = partner(inner_sent, "docs", 0)
    branch_one, mid_sums, inner_sums_kept, inner_kept = middle_last(
        core, branch_two, hidden_low, slope, inner_weight, outer_weight, norm1_gain,
        half_grad, normed_one, rstd_one, (outer_next,),
    )
    inner = Flow([[sharded(inner_kept), sharded(inner_got)]], rising)
    for bit in across_bits:
        (inner_next,) = run([inner.docs_job(bit)])
        inner.send(inner_next)
    mixed_grad, input_grad, low_sums = attend_back(
        branch_one, qkv, doc_length, seg_len, attn_weight, proj_weight, (inner_next,) + tuple(bundles[1:])
    )
    input_grad = input_grad.reshape(tokens.shape)
    others = [partner(item, "docs", 0) for item in bundles]
    left_sent, right_sent = last_grads(1 - core, rows_low, attended, mixed_grad, branch_one)
    for bit in across_bits[:-1]:
        (outer_next,) = run([outer.docs_job(bit)], (left_sent,))
        outer.send(outer_next)
    outer_next, inner_next = run([outer.docs_job(across_bits[-1]), inner.seg_job()], (left_sent, *others))
    outer.send(outer_next)
    inner.send(inner_next)
    bundles = bundles + others
    small = small_rows(low_sums, mid_sums, top_sums, inner_sums_kept, inner_sums_sent, segments)
    left_sent, right_sent, small = gated((left_sent, right_sent, small), (outer_next, inner_next))
    left_got, right_got, small_got = (partner(item, "docs", 0) for item in (left_sent, right_sent, small))
    left_kept, right_kept = last_grads(core, rows_low, attended, mixed_grad, branch_one, (left_sent,))
    attn_out, proj_out, inner_out, outer_out, cross_bias, cross_wide, cross_norm, position_grad = cross_grads(
        bundles, segments, width, hidden, (left_kept,)
    )
    left = Flow([[sharded(left_kept), sharded(left_got)]], rising)
    right = Flow([[sharded(right_kept), sharded(right_got)], [small, small_got]], far_first)
    flows = (left, right, inner, outer)

    def advance(jobs, of, tokens=()):
        values = run(jobs, tokens)
        for flow, value in zip(of, values):
            flow.send(value)
        return values

    for bit in across_bits[:-1]:
        advance([left.docs_job(bit)], (left,))
    last = advance(
        [left.docs_job(across_bits[-1]), right.seg_job(), inner.seg_job(), outer.seg_job()], flows, (cross_bias,)
    )
    for bit in across_bits[:-1]:
        advance([right.docs_job(bit)], (right,))
    last = advance([left.seg_job(), right.docs_job(across_bits[-1]), inner.seg_job(), outer.seg_job()], flows)
    inner.further(seg_bits, last)
    outer.further(seg_bits, last)
    values = run([left.seg_job(), right.seg_job(), inner.settle_job(), outer.settle_job()])
    left.send(values[0])
    right.send(values[1])
    inner, outer = (docs_pieces(value.reshape(value.shape[1:])) for value in values[2:])
    while left.seg_done < seg_bits:
        last = advance([left.seg_job(), right.seg_job()], (left, right))
    (last,) = run([joined(left.settle_job(), right.settle_job())], tuple(outer[1:] + inner[1:]))
    (outer_out,) = finish(
        [(outer, False, (0, outer[0].shape[0]), [(0, 0, width // 2, 0)])], [outer_out], tokens=(last,)
    )
    span = inner[0].shape[0]
    (inner_out,) = finish([(inner, False, (0, span), [(0, 0, hidden // 2, 0)])], [inner_out], tokens=(outer_out,))
    last = docs_pieces(last.reshape(last.shape[1:]), tokens=(inner_out,))
    part, wide = width // segments, hidden // segments
    third = width // 2
    attn_out, proj_out, *smalls = finish(
        [
            (last, False, (0, span), [(0, 0, third, 0), (1, third, width, 0)]),
            (last, False, (span, 2 * span), [(0, 0, width, third)]),
        ],
        [attn_out, proj_out],
        ([cross_bias, cross_wide, cross_norm], [part] * 8 + [wide]),
        (inner_out,),
    )
    qb, vb, pb, ob, g1, s1, g2, s2, ib = smalls
    return (
        layer_out.reshape(tokens.shape),
        input_grad,
        attn_out,
        qb,
        vb,
        proj_out,
        pb,
        g1,
        s1,
        inner_out,
        ib,
        outer_out,
        ob,
        g2,
        s2,
        position_grad,
    )


def solution(mesh):
    return jax.shard_map(
        on_device,
        mesh=mesh,
        in_specs=(
            P("docs", "seg", None, None),
            P("docs"),
            P(),
            P(),
            P(),
            P(),
            P(),
            P(),
            P(),
            P(),
            P(),
            P(),
            P(),
            P(),
            P(),
            P(),
            P("docs", "seg", None, None),
        ),
        out_specs=(
            P("docs", "seg", None, None),
            P("docs", "seg", None, None),
            P(None, "seg", None),
            P(None, "seg"),
            P(None, "seg"),
            P(None, "seg", None),
            P(None, "seg"),
            P(None, "seg"),
            P(None, "seg"),
            P(None, "seg", None),
            P(None, "seg"),
            P(None, "seg", None),
            P(None, "seg"),
            P(None, "seg"),
            P(None, "seg"),
            P(None, "seg"),
        ),
        check_vma=False,
    )
```

```python
import functools
import math

import jax
import jax.numpy as jnp
from jax import lax
from jax.experimental import pallas as pl
from jax.experimental.pallas import tpu as pltpu
from jax.sharding import PartitionSpec as P

HEADS = 12
HEAD = 64
PAIR = 2 * HEAD


NEG = -1e30
EPS = 1e-05
LOW = jnp.bfloat16
F32 = jnp.float32
MIB = 1024 * 1024
TILE = 512
WIDE = 1024


def dot(left, right):
    return lax.dot_general(left, right, (((1,), (0,)), ((), ())), preferred_element_type=F32)


def dot_rt(left, right):
    return lax.dot_general(left, right, (((1,), (1,)), ((), ())), preferred_element_type=F32)


def dot_lt(left, right):
    return lax.dot_general(left, right, (((0,), (0,)), ((), ())), preferred_element_type=F32)


def normalize(rows):
    center = rows - jnp.mean(rows, axis=-1, keepdims=True)
    rstd = lax.rsqrt(jnp.mean(center * center, axis=-1, keepdims=True) + EPS)
    return center * rstd, rstd


def norm_back(grad, gain, normed, rstd):
    scaled = grad * gain
    return rstd * (
        scaled
        - jnp.mean(scaled, axis=-1, keepdims=True)
        - normed * jnp.mean(scaled * normed, axis=-1, keepdims=True)
    )


def gelu_and_slope(inner):
    kind = inner.dtype.type
    size = jnp.abs(inner)
    t = kind(1.0) / (kind(1.0) + kind(0.3275911 * 0.7071067811865476) * size)
    bell = jnp.exp(kind(-0.5) * inner * inner)
    series = kind(0.5 * 1.061405429) * t - kind(0.5 * 1.453152027)
    series = series * t + kind(0.5 * 1.421413741)
    series = series * t - kind(0.5 * 0.284496736)
    series = series * t + kind(0.5 * 0.254829592)
    tail = series * t * bell
    below = jnp.where(inner >= kind(0.0), kind(1.0) - tail, tail)
    return inner * below, below + inner * bell * kind(0.3989422804014327)


def colsum(rows):
    return jnp.sum(rows, axis=0, keepdims=True)


def head_masks():
    lane = lax.broadcasted_iota(jnp.int32, (1, PAIR), 1)
    first = (lane < HEAD).astype(F32).astype(LOW)
    second = (lane >= HEAD).astype(F32).astype(LOW)
    return lane, first, second


def whole(shape):
    return pl.BlockSpec(shape, lambda *_: (0,) * len(shape))


def of_block(index, shape):
    return pl.BlockSpec((1,) + shape, lambda *_: (index,) + (0,) * len(shape))


def params(limit_mib=64):
    return pltpu.CompilerParams(vmem_limit_bytes=limit_mib * MIB)


def token_specs(tokens):
    return [pl.BlockSpec(memory_space=pl.ANY)] * len(tokens)


def cost(*_):
    return pl.CostEstimate(flops=1024, bytes_accessed=1024, transcendentals=0)


def attend_kernel(
    groups, length, len_ref, x_ref, w_ref, qb_ref, vb_ref, pw_ref, pb_ref, g1_ref, s1_ref,
    qkv_ref, att_ref, normed_ref, hidden_ref, rstd_ref,
):
    step = pl.program_id(0)
    start = lax.axis_index("seg") * length
    rows_low = x_ref[...]
    width = rows_low.shape[1]
    queries = (dot(rows_low, w_ref[0, :, :width]) + qb_ref[0:1, :].astype(F32)).astype(LOW)
    keys = dot(rows_low, w_ref[0, :, width : 2 * width]).astype(LOW)
    values = (dot(rows_low, w_ref[0, :, 2 * width :]) + vb_ref[0:1, :].astype(F32)).astype(LOW)
    qkv_ref[:, :width] = queries
    qkv_ref[:, width : 2 * width] = keys
    qkv_ref[:, 2 * width :] = values
    queries = queries * LOW(1.0 / math.sqrt(HEAD))
    lane, first, second = head_masks()
    key_lane = lax.broadcasted_iota(jnp.int32, (1, length), 1)
    ones = jnp.ones((length, PAIR), LOW)
    places = []
    for group in range(groups):
        count = jnp.clip(len_ref[step * groups + group] - start, 1, length)
        rows = slice(group * length, (group + 1) * length)
        places += [(rows, slice(at, at + PAIR), key_lane < count) for at in range(0, width, PAIR)]
    scores = []
    for rows, cols, _ in places:
        both = queries[rows, cols]
        both = jnp.concatenate([both * first, both * second], axis=0)
        scores.append(dot_rt(both, keys[rows, cols]))
    weights = []
    for item, (_, _, valid) in zip(scores, places):
        item = jnp.where(valid, item, NEG)
        weights.append(jnp.exp(item - jnp.max(item, axis=1, keepdims=True)).astype(LOW))
    for item, (rows, cols, _) in zip(weights, places):
        mixed = dot(item, jnp.concatenate([values[rows, cols], ones], axis=1))
        mixed = mixed[:, :PAIR] / mixed[:, PAIR:]
        att_ref[rows, cols] = jnp.where(lane < HEAD, mixed[:length], mixed[length:]).astype(LOW)
    resid = rows_low.astype(F32) + dot(att_ref[...], pw_ref[0]) + pb_ref[0:1, :].astype(F32)
    normed, rstd = normalize(resid)
    normed_ref[...] = normed.astype(LOW)
    hidden_ref[...] = (normed * g1_ref[0:1, :].astype(F32) + s1_ref[0:1, :].astype(F32)).astype(LOW)
    rstd_ref[...] = jnp.broadcast_to(rstd, rstd_ref.shape)


def attend(rows_low, doc_length, seg_len, attn_weight, query_bias, value_bias, proj_weight, proj_bias, g1, s1):
    total, width = rows_low.shape
    groups = 2
    size = groups * seg_len
    return pl.pallas_call(
        functools.partial(attend_kernel, groups, seg_len),
        grid=(total // size,),
        in_specs=[
            pl.BlockSpec(memory_space=pltpu.SMEM),
            pl.BlockSpec((size, width), lambda i: (i, 0)),
            of_block(0, (width, 3 * width)),
            whole(query_bias.shape),
            whole(value_bias.shape),
            of_block(0, (width, width)),
            whole(proj_bias.shape),
            whole(g1.shape),
            whole(s1.shape),
        ],
        out_specs=[
            pl.BlockSpec((size, 3 * width), lambda i: (i, 0)),
            pl.BlockSpec((size, width), lambda i: (i, 0)),
            pl.BlockSpec((size, width), lambda i: (i, 0)),
            pl.BlockSpec((size, width), lambda i: (i, 0)),
            pl.BlockSpec((size, 128), lambda i: (i, 0)),
        ],
        out_shape=[
            jax.ShapeDtypeStruct((total, 3 * width), LOW),
            jax.ShapeDtypeStruct((total, width), LOW),
            jax.ShapeDtypeStruct((total, width), LOW),
            jax.ShapeDtypeStruct((total, width), LOW),
            jax.ShapeDtypeStruct((total, 128), F32),
        ],
        compiler_params=params(),
        cost_estimate=cost(
            2 * total * width * 4 * width + 8 * total * seg_len * width, 16 * MIB, total * seg_len * HEADS
        ),
        name="attend",
    )(doc_length, rows_low, attn_weight, query_bias, value_bias, proj_weight, proj_bias, g1, s1)


def leader_kernel(
    hidden_ref, cot_ref, b1_ref, b2_ref, g2_ref, s2_ref, w1_hbm, w2_hbm, out_ref, w1_ref, w2_ref, sems,
):
    tiles = w1_ref.shape[1] // TILE
    copies = []
    for at in range(tiles):
        cols = slice(at * TILE, (at + 1) * TILE)
        copies.append(
            (
                pltpu.make_async_copy(w1_hbm.at[0, :, cols], w1_ref.at[:, cols], sems.at[0, at]),
                pltpu.make_async_copy(w2_hbm.at[0, cols, :], w2_ref.at[cols, :], sems.at[1, at]),
            )
        )
    for pair in copies:
        for copy in pair:
            copy.start()
    hidden = hidden_ref[:, 0, :]
    total = hidden.astype(F32) + b2_ref[0:1, :].astype(F32)
    for at, pair in enumerate(copies):
        cols = slice(at * TILE, (at + 1) * TILE)
        pair[0].wait()
        active, _ = gelu_and_slope(dot(hidden, w1_ref[:, cols]) + b1_ref[0:1, cols].astype(F32))
        pair[1].wait()
        total = total + dot(active.astype(LOW), w2_ref[cols, :])
    normed, _ = normalize(total)
    out = normed * g2_ref[0:1, :].astype(F32) + s2_ref[0:1, :].astype(F32)
    out_ref[0] = out.astype(LOW)
    out_ref[1] = cot_ref[:, 0, :]


def ff_specs(width, tile, pick=lambda i: i):
    return [
        pl.BlockSpec((1, width, tile), lambda i, *_: (0, 0, pick(i))),
        pl.BlockSpec((2, tile), lambda i, *_: (0, pick(i))),
        pl.BlockSpec((1, tile, width), lambda i, *_: (0, pick(i), 0)),
    ]


def lead(hidden_low, cots, docs, inner_weight, inner_bias, outer_weight, outer_bias, g2, s2):
    width, hidden = inner_weight.shape[1:]
    hidden_low = hidden_low.reshape(docs, -1, width)
    cots = cots.reshape(docs, -1, width)
    hbm = pl.BlockSpec(memory_space=pl.ANY)
    return pl.pallas_call(
        leader_kernel,
        grid=(1,),
        in_specs=[whole((docs, 16, width))] * 2 + [whole((2, hidden))] + [whole((2, width))] * 3 + [hbm] * 2,
        out_specs=whole((2, docs, width)),
        out_shape=jax.ShapeDtypeStruct((2, docs, width), LOW),
        scratch_shapes=[
            pltpu.VMEM((width, hidden), LOW),
            pltpu.VMEM((hidden, width), LOW),
            pltpu.SemaphoreType.DMA((2, hidden // TILE)),
        ],
        compiler_params=params(),
        cost_estimate=cost(),
        name="leaders",
    )(hidden_low, cots, inner_bias, outer_bias, g2, s2, inner_weight, outer_weight)


CHUNK = 256
FEED_CHUNK = 512


def feed_kernel(
    low_ref, w1_ref, b1_ref, w2_ref, b2_ref, g2_ref, s2_ref,
    active_ref, slope_ref, out_ref, normed2_ref, rstd2_ref, acc_ref,
):
    step = pl.program_id(0)
    last = pl.num_programs(0) - 1
    chunks = [slice(at, at + FEED_CHUNK) for at in range(0, low_ref.shape[0], FEED_CHUNK)]
    bias = b1_ref[0:1, :].astype(F32)

    @pl.when(step == 0)
    def _():
        for rows in chunks:
            acc_ref[rows, :] = low_ref[rows, :].astype(F32) + b2_ref[0:1, :].astype(F32)

    inner = dot(low_ref[chunks[0], :], w1_ref[0])
    for at, rows in enumerate(chunks):
        active, slope = gelu_and_slope((inner + bias).astype(LOW))
        if at + 1 < len(chunks):
            inner = dot(low_ref[chunks[at + 1], :], w1_ref[0])
        active_ref[rows, :] = active
        slope_ref[rows, :] = slope
        acc_ref[rows, :] += dot(active, w2_ref[0])

    @pl.when(step == last)
    def _():
        for rows in chunks:
            normed, rstd = normalize(acc_ref[rows, :])
            normed2_ref[rows, :] = normed.astype(LOW)
            rstd2_ref[rows, :] = jnp.broadcast_to(rstd, (FEED_CHUNK, 128))
            out = normed * g2_ref[0:1, :].astype(F32) + s2_ref[0:1, :].astype(F32)
            out_ref[rows, :] = out.astype(LOW)


def feed(hidden_low, inner_weight, inner_bias, outer_weight, outer_bias, g2, s2):
    total, width = hidden_low.shape
    hidden = inner_weight.shape[2]
    return pl.pallas_call(
        feed_kernel,
        grid=(hidden // TILE,),
        in_specs=[whole((total, width))] + ff_specs(width, TILE) + [whole((2, width))] * 3,
        out_specs=[
            pl.BlockSpec((total, TILE), lambda i: (0, i)),
            pl.BlockSpec((total, TILE), lambda i: (0, i)),
            whole((total, width)),
            whole((total, width)),
            whole((total, 128)),
        ],
        out_shape=[
            jax.ShapeDtypeStruct((total, hidden), LOW),
            jax.ShapeDtypeStruct((total, hidden), LOW),
            jax.ShapeDtypeStruct((total, width), LOW),
            jax.ShapeDtypeStruct((total, width), LOW),
            jax.ShapeDtypeStruct((total, 128), F32),
        ],
        scratch_shapes=[pltpu.VMEM((total, width), F32)],
        compiler_params=params(),
        cost_estimate=cost(),
        name="feed",
    )(hidden_low, inner_weight, inner_bias, outer_weight, outer_bias, g2, s2)


def slots(columns):
    return -(-columns // 128) * 128


def bundle_places(width, hidden, segments):
    own = slots(width // segments)
    sizes = [own, own, own, slots(hidden // segments), 3 * width, width, hidden, width, own]
    places, start = [], 0
    for size in sizes:
        places.append((start, size))
        start += size
    return places, start


def cross_kernel(docs, segments, length, len_ref, *refs):
    pieces, refs = refs[: segments // 2], refs[segments // 2 :]
    (
        pos_ref, qb_ref, vb_ref, pb_ref, g1_ref, s1_ref, b1_ref, b2_ref, g2_ref, s2_ref,
        seg_cot_ref, seg_normed_ref, seg_rstd_ref, aw_hbm, pw_hbm, w1_hbm, w2_hbm,
        out_ref, back_ref, bundle_ref, seg_branch_ref, seg_sums_ref,
        aw_ref, pw_ref, w1_ref, w2_ref, inner_ref, probs_ref, low_ref, att_ref, hid_ref, act_ref,
        lead_ref, cot_ref, sems,
    ) = refs
    width = lead_ref.shape[1]
    hidden = w1_ref.shape[1]
    places, _ = bundle_places(width, hidden, segments)
    dmix_ref, dproj_ref, dinner_ref, dout_ref = (
        bundle_ref.at[:, places[at][0] : places[at][0] + places[at][1]] for at in range(4, 8)
    )
    copies = [
        pltpu.make_async_copy(src.at[1], dst, sems.at[i])
        for i, (src, dst) in enumerate(
            [(aw_hbm, aw_ref), (pw_hbm, pw_ref), (w1_hbm, w1_ref), (w2_hbm, w2_ref)]
        )
    ]
    for copy in copies:
        copy.start()
    total = lead_ref.shape[0]
    scale = 1.0 / math.sqrt(HEAD)

    def row(ref):
        return ref[1:2, :].astype(F32)

    me = lax.axis_index("seg")
    for at, piece in enumerate(pieces):
        for half in range(2):
            seg = me ^ (2 * at + half)
            for doc in range(docs):
                place = pl.ds(doc * segments + seg, 1)
                lead_ref[place, :] = piece[2 * half, doc : doc + 1, :].astype(F32)
                cot_ref[place, :] = piece[2 * half + 1, doc : doc + 1, :].astype(F32)
    rows = lead_ref[...] + jnp.concatenate([pos_ref[...].astype(F32)] * docs, axis=0)
    rows_low = rows.astype(LOW)
    low_ref[...] = rows_low
    both_heads = (total, 2 * total)
    key = lax.broadcasted_iota(jnp.int32, both_heads, 0)
    query = lax.broadcasted_iota(jnp.int32, both_heads, 1) % total
    key_doc = key // segments
    reach = jnp.zeros(both_heads, jnp.int32)
    for doc in range(docs):
        reach = jnp.where(key_doc == doc, len_ref[doc], reach)
    valid = (key_doc == query // segments) & ((key - key_doc * segments) * length < reach)
    lane, first, second = head_masks()

    later_row = lax.broadcasted_iota(jnp.int32, (length, 1), 0) > 0
    seg_gain = g2_ref[0:1, :].astype(F32)
    seg_sums = [jnp.zeros((1, width), F32)] * 3
    for at in range(0, seg_cot_ref.shape[0], length):
        span = slice(at, at + length)
        upper = jnp.where(later_row, seg_cot_ref[span, :].astype(F32), 0.0)
        normed = seg_normed_ref[span, :].astype(F32)
        branch = norm_back(upper, seg_gain, normed, seg_rstd_ref[span, 0:1]).astype(LOW)
        seg_branch_ref[span, :] = branch
        for which, item in enumerate((upper * normed, upper, branch.astype(F32))):
            seg_sums[which] = seg_sums[which] + colsum(item)
    seg_sums_ref[...] = jnp.concatenate(seg_sums + [jnp.zeros((5, width), F32)], axis=0)

    copies[0].wait()
    queries = (dot(rows_low, aw_ref[:, :width]) + row(qb_ref)).astype(LOW)
    keys = dot(rows_low, aw_ref[:, width : 2 * width]).astype(LOW)
    values = (dot(rows_low, aw_ref[:, 2 * width :]) + row(vb_ref)).astype(LOW)

    def stacked(both):
        return jnp.concatenate([both * first, both * second], axis=0)

    def picked(both):
        return jnp.where(lane < HEAD, both[:total], both[total:])

    pair_cols = [slice(at, at + PAIR) for at in range(0, width, PAIR)]
    query_both = [stacked(queries[:, cols]) for cols in pair_cols]
    scores = [dot_rt(keys[:, cols], both) for cols, both in zip(pair_cols, query_both)]
    probs_low = []
    for pair, item in enumerate(scores):
        item = jnp.where(valid, item * scale, NEG)
        weights = jnp.exp(item - jnp.max(item, axis=0, keepdims=True))
        probs = weights / jnp.sum(weights, axis=0, keepdims=True)
        probs_ref[pair] = probs
        probs_low.append(probs.astype(LOW))
    for cols, item in zip(pair_cols, probs_low):
        att_ref[:, cols] = picked(dot_lt(item, values[:, cols])).astype(LOW)
    copies[1].wait()
    resid = rows + dot(att_ref[...], pw_ref[...]) + row(pb_ref)
    normed_one, rstd_one = normalize(resid)
    hidden = normed_one * row(g1_ref) + row(s1_ref)
    hidden_low = hidden.astype(LOW)
    hid_ref[...] = hidden_low
    copies[2].wait()
    copies[3].wait()
    count = w1_ref.shape[1] // WIDE
    branch = jnp.zeros((total, width), F32)
    for at in range(count):
        cols = slice(at * WIDE, (at + 1) * WIDE)
        active, slope = gelu_and_slope(dot(hidden_low, w1_ref[:, cols]) + b1_ref[1:2, cols].astype(F32))
        inner_ref[:, cols] = slope
        active = active.astype(LOW)
        act_ref[:, cols] = active
        branch += dot(active, w2_ref[cols, :])
    normed_two, rstd_two = normalize(hidden + branch + row(b2_ref))
    out_ref[...] = normed_two * row(g2_ref) + row(s2_ref)

    upper = cot_ref[...]
    sums = [colsum(upper * normed_two), colsum(upper)]
    resid_two = norm_back(upper, row(g2_ref), normed_two, rstd_two)
    branch_two = resid_two.astype(LOW)
    dout_ref[...] = branch_two
    hidden_grad = resid_two
    for at in range(count):
        cols = slice(at * WIDE, (at + 1) * WIDE)
        inner_grad = (dot_rt(branch_two, w2_ref[cols, :]) * inner_ref[:, cols]).astype(LOW)
        dinner_ref[:, cols] = inner_grad
        hidden_grad += dot_rt(inner_grad, w1_ref[:, cols])
    sums = [colsum(hidden_grad * normed_one), colsum(hidden_grad)] + sums
    resid_one = norm_back(hidden_grad, row(g1_ref), normed_one, rstd_one)
    branch_one = resid_one.astype(LOW)
    dproj_ref[...] = branch_one
    att_grad = dot_rt(branch_one, pw_ref[...]).astype(LOW)
    att_both = [stacked(att_grad[:, cols]) for cols in pair_cols]
    prob_grads = [dot_rt(values[:, cols], both) for cols, both in zip(pair_cols, att_both)]
    score_grads = []
    for pair, prob_grad in enumerate(prob_grads):
        probs = probs_ref[pair]
        score_grad = probs * (prob_grad - jnp.sum(prob_grad * probs, axis=0, keepdims=True))
        score_grads.append(score_grad.astype(LOW))
    for pair, cols in enumerate(pair_cols):
        cols_k, cols_v = (slice(cols.start + at * width, cols.stop + at * width) for at in (1, 2))
        dmix_ref[:, cols] = (picked(dot_lt(score_grads[pair], keys[:, cols])) * scale).astype(LOW)
        dmix_ref[:, cols_k] = (dot(score_grads[pair], query_both[pair]) * scale).astype(LOW)
        dmix_ref[:, cols_v] = dot(probs_ref[pair].astype(LOW), att_both[pair]).astype(LOW)
    back = resid_one + dot_rt(dmix_ref[...], aw_ref[...])
    back_ref[...] = back
    seg = lax.axis_index("seg")

    def own(value, slot):
        step = value.shape[1] // segments
        return pltpu.roll(value.astype(F32), lax.rem(value.shape[1] - seg * step, value.shape[1]), 1)[:, :slot]

    for at, item in enumerate((low_ref, att_ref, hid_ref, act_ref)):
        start, slot = places[at]
        bundle_ref[:, start : start + slot] = own(item[...], slot).astype(LOW)
    start, slot = places[8]
    by_segment = back[:segments]
    for doc in range(1, docs):
        by_segment += back[doc * segments : (doc + 1) * segments]
    pieces = [own(jnp.concatenate(sums + [jnp.zeros((4, width), F32)], axis=0), slot), own(by_segment, slot)]
    rest = total - 8 - segments
    if rest:
        pieces.append(jnp.zeros((rest, slot), F32))
    bundle_ref[:, start : start + slot] = jnp.concatenate(pieces, axis=0).astype(LOW)


def cross_block(
    pieces, position, doc_length, seg_len,
    attn_weight, query_bias, value_bias, proj_weight, proj_bias, g1, s1,
    inner_weight, inner_bias, outer_weight, outer_bias, g2, s2, seg_cots, seg_normed, seg_rstd,
):
    segments, width = position.shape
    docs = pieces[0].shape[1]
    total = docs * segments
    hidden = inner_weight.shape[2]
    vmem = pl.BlockSpec(memory_space=pltpu.VMEM)
    hbm = pl.BlockSpec(memory_space=pl.ANY)

    def shape(columns, dtype=LOW):
        return jax.ShapeDtypeStruct((total, columns), dtype)

    return pl.pallas_call(
        functools.partial(cross_kernel, docs, segments, seg_len),
        in_specs=[pl.BlockSpec(memory_space=pltpu.SMEM)] + [vmem] * (len(pieces) + 13) + [hbm] * 4,
        out_specs=[vmem] * 5,
        out_shape=[
            shape(width, F32),
            shape(width, F32),
            shape(bundle_places(width, hidden, segments)[1]),
            jax.ShapeDtypeStruct(seg_cots.shape, LOW),
            jax.ShapeDtypeStruct((8, width), F32),
        ],
        scratch_shapes=[
            pltpu.VMEM((width, 3 * width), LOW),
            pltpu.VMEM((width, width), LOW),
            pltpu.VMEM((width, hidden), LOW),
            pltpu.VMEM((hidden, width), LOW),
            pltpu.VMEM((total, hidden), F32),
            pltpu.VMEM((HEADS // 2, total, 2 * total), F32),
            pltpu.VMEM((total, width), LOW),
            pltpu.VMEM((total, width), LOW),
            pltpu.VMEM((total, width), LOW),
            pltpu.VMEM((total, hidden), LOW),
            pltpu.VMEM((total, width), F32),
            pltpu.VMEM((total, width), F32),
            pltpu.SemaphoreType.DMA((4,)),
        ],
        compiler_params=params(),
        cost_estimate=cost(4 * total * width * (4 * width + 2 * hidden) * 2, 2 * width * (4 * width + 2 * hidden)),
        name="cross_block",
    )(
        doc_length, *pieces, position, query_bias, value_bias, proj_bias, g1, s1,
        inner_bias, outer_bias, g2, s2, seg_cots, seg_normed, seg_rstd,
        attn_weight, proj_weight, inner_weight, outer_weight,
    )


def top_kernel(
    segments, back_ref, cross_ref, low_ref, normed_ref, rstd_ref, g2_ref, first_sums_ref, branch_ref, active_ref,
    sums_ref, sent_ref, kept_ref, patched_ref, branch_out_ref, swap_ref,
):
    step = pl.program_id(0)
    docs, length, width = branch_ref.shape
    half = width // 2

    @pl.when(step == 0)
    def _():
        core = lax.axis_index("docs") % 2
        seg = lax.axis_index("seg")
        first_row = lax.broadcasted_iota(jnp.int32, (low_ref.shape[1], 1), 0) == 0

        def own(ref):
            return jnp.concatenate([ref[pl.ds(doc * segments + seg, 1), :] for doc in range(docs)], axis=0)

        upper = own(back_ref)
        normed = normed_ref[:, 0, :].astype(F32)
        branch = norm_back(upper, g2_ref[0:1, :].astype(F32), normed, rstd_ref[:, 0, 0:1]).astype(LOW).astype(F32)
        for at, item in enumerate((upper * normed, upper, branch)):
            sums_ref[at : at + 1, :] = first_sums_ref[at : at + 1, :] + colsum(item)
        sums_ref[3:8, :] = jnp.zeros((5, width), F32)
        cross = own(cross_ref)
        top_rows = low_ref.shape[1]
        for doc in range(docs):
            patched_ref[doc] = jnp.where(first_row, cross[doc : doc + 1, :], low_ref[doc].astype(F32)).astype(LOW)
            top_part = jnp.where(first_row, branch[doc : doc + 1, :], branch_ref[doc, :top_rows, :].astype(F32))
            top_part = top_part.astype(LOW)
            branch_out_ref[doc] = top_part
            rows = slice(doc * length, (doc + 1) * length)
            whole_part = jnp.concatenate([top_part, branch_ref[doc, top_rows:, :]], axis=0)
            left, right = whole_part[:, :half], whole_part[:, half:]
            swap_ref[rows, :half] = jnp.where(core == 0, right, left)
            swap_ref[rows, half:] = jnp.where(core == 0, left, right)

    grad = dot_lt(active_ref[...], swap_ref[...]).astype(LOW)
    sent_ref[...] = grad[:, :half]
    kept_ref[...] = grad[:, half:]


def top_back(back, cross_out, seg_low, seg_len, normed, rstd, g2, sums, branch, active):
    total, width = branch.shape
    hidden = active.shape[1]
    docs = total // seg_len
    first = (docs, 16, width)
    by_doc = (docs, seg_len, width)
    out = pl.pallas_call(
        functools.partial(top_kernel, back.shape[0] // docs),
        grid=(hidden // TILE,),
        in_specs=[
            whole(back.shape),
            whole(back.shape),
            whole(first),
            whole(first),
            whole((docs, 8, 128)),
            whole((2, width)),
            whole((8, width)),
            whole(by_doc),
            pl.BlockSpec((total, TILE), lambda i: (0, i)),
        ],
        out_specs=[
            whole((8, width)),
            pl.BlockSpec((TILE, width // 2), lambda i: (i, 0)),
            pl.BlockSpec((TILE, width // 2), lambda i: (i, 0)),
            whole(first),
            whole(first),
        ],
        out_shape=[
            jax.ShapeDtypeStruct((8, width), F32),
            jax.ShapeDtypeStruct((hidden, width // 2), LOW),
            jax.ShapeDtypeStruct((hidden, width // 2), LOW),
            jax.ShapeDtypeStruct(by_doc, LOW),
            jax.ShapeDtypeStruct(by_doc, LOW),
        ],
        input_output_aliases={2: 3, 7: 4},
        scratch_shapes=[pltpu.VMEM((total, width), LOW)],
        compiler_params=params(),
        cost_estimate=cost(),
        name="top_back",
    )(
        back, cross_out, seg_low.reshape(by_doc), normed.reshape(by_doc), rstd.reshape(docs, seg_len, 128), g2, sums,
        branch.reshape(by_doc), active,
    )
    return out[0], out[1], out[2], out[3], out[4].reshape(total, width)


def middle_step(branch_ref, low_ref, slope_ref, w1_ref, w2_ref, acc_ref, bias_ref, grad_ref, finished=None):
    parts = []
    chunks = [slice(at, at + CHUNK) for at in range(0, branch_ref.shape[0], CHUNK)]
    following = dot_rt(branch_ref[chunks[0], :], w2_ref[0])
    for at, rows in enumerate(chunks):
        part = (following * slope_ref[rows, :].astype(F32)).astype(LOW)
        if at + 1 < len(chunks):
            following = dot_rt(branch_ref[chunks[at + 1], :], w2_ref[0])
        total = acc_ref[rows, :] + dot_rt(part, w1_ref[0])
        if finished:
            finished(rows, total)
        else:
            acc_ref[rows, :] = total
        parts.append(part)
    inner_grad = jnp.concatenate(parts, axis=0)
    bias_ref[...] = jnp.broadcast_to(colsum(inner_grad.astype(F32)), bias_ref.shape)
    grad_ref[...] = dot_lt(low_ref[...], inner_grad).astype(LOW)


def middle_first_kernel(core_ref, branch_ref, low_ref, slope_ref, w1_ref, w2_ref, *refs):
    half_ref, bias_ref, sent_ref, acc_ref = refs[-4:]
    step = pl.program_id(0)
    last = pl.num_programs(0) - 1

    @pl.when(step == 0)
    def _():
        acc_ref[...] = jnp.zeros_like(acc_ref)

    def finished(rows, total):
        half_ref[rows, :] = total.astype(LOW)

    operands = (branch_ref, low_ref, slope_ref, w1_ref, w2_ref, acc_ref, bias_ref, sent_ref)
    pl.when(step < last)(lambda: middle_step(*operands))
    pl.when(step == last)(lambda: middle_step(*operands, finished))


def middle_last_kernel(core_ref, branch_ref, low_ref, slope_ref, w1_ref, w2_ref, g1_ref, *refs):
    half_hbm, normed_hbm, rstd_hbm = refs[:3]
    branch1_ref, sums_ref, bias_ref, kept_ref, acc_ref, half_ref, normed_ref, rstd_ref, sems = refs[-9:]
    step = pl.program_id(0)
    last = pl.num_programs(0) - 1
    width = branch_ref.shape[1]
    copies = [
        pltpu.make_async_copy(source, target, sems.at[at])
        for at, (source, target) in enumerate(
            ((half_hbm, half_ref), (normed_hbm, normed_ref), (rstd_hbm, rstd_ref))
        )
    ]

    @pl.when(step == 0)
    def _():
        for copy in copies:
            copy.start()
        acc_ref[...] = jnp.zeros_like(acc_ref)

    sums = [jnp.zeros((1, width), F32)] * 3

    def finished(rows, total):
        hidden_grad = total + half_ref[rows, :].astype(F32) + branch_ref[rows, :].astype(F32)
        normed = normed_ref[rows, :].astype(F32)
        resid = norm_back(hidden_grad, g1_ref[0:1, :].astype(F32), normed, rstd_ref[rows, 0:1])
        branch = resid.astype(LOW)
        branch1_ref[rows, :] = branch
        for at, item in enumerate((hidden_grad * normed, hidden_grad, branch.astype(F32))):
            sums[at] = sums[at] + colsum(item)

    operands = (branch_ref, low_ref, slope_ref, w1_ref, w2_ref, acc_ref, bias_ref, kept_ref)
    pl.when(step < last)(lambda: middle_step(*operands))

    @pl.when(step == last)
    def _():
        for copy in copies:
            copy.wait()
        middle_step(*operands, finished)
        sums_ref[...] = jnp.concatenate(sums + [jnp.zeros((5, width), F32)], axis=0)


def half_order(steps):
    half = steps // 2

    def pick(step, core_ref):
        return jnp.where(step < half, 1 - core_ref[0], core_ref[0]) * half + step % half

    return pick


def middle_specs(total, width, steps, offset):
    pick = half_order(2 * steps)
    return [
        whole((total, width)),
        whole((total, width)),
        pl.BlockSpec((total, TILE), lambda i, c: (0, pick(i + offset, c))),
        pl.BlockSpec((1, width, TILE), lambda i, c: (0, 0, pick(i + offset, c))),
        pl.BlockSpec((1, TILE, width), lambda i, c: (0, pick(i + offset, c), 0)),
    ]


def middle_first(core, branch, low, slope, inner_weight, outer_weight, tokens=()):
    total, width = branch.shape
    steps = slope.shape[1] // TILE // 2
    return pl.pallas_call(
        middle_first_kernel,
        grid_spec=pltpu.PrefetchScalarGridSpec(
            num_scalar_prefetch=1,
            grid=(steps,),
            in_specs=middle_specs(total, width, steps, 0) + token_specs(tokens),
            out_specs=[
                whole((total, width)),
                pl.BlockSpec((8, TILE), lambda i, c: (0, i)),
                pl.BlockSpec((width, TILE), lambda i, c: (0, i)),
            ],
            scratch_shapes=[pltpu.VMEM((total, width), F32)],
        ),
        out_shape=[
            jax.ShapeDtypeStruct((total, width), LOW),
            jax.ShapeDtypeStruct((8, steps * TILE), F32),
            jax.ShapeDtypeStruct((width, steps * TILE), LOW),
        ],
        compiler_params=params(),
        cost_estimate=cost(),
        name="middle_first",
    )(core, branch, low, slope, inner_weight, outer_weight, *tokens)


def middle_last(core, branch, low, slope, inner_weight, outer_weight, g1, half, normed, rstd, tokens=()):
    total, width = branch.shape
    steps = slope.shape[1] // TILE // 2
    return pl.pallas_call(
        middle_last_kernel,
        grid_spec=pltpu.PrefetchScalarGridSpec(
            num_scalar_prefetch=1,
            grid=(steps,),
            in_specs=middle_specs(total, width, steps, steps)
            + [whole((2, width))]
            + token_specs((half, normed, rstd) + tuple(tokens)),
            out_specs=[
                whole((total, width)),
                whole((8, width)),
                pl.BlockSpec((8, TILE), lambda i, c: (0, i)),
                pl.BlockSpec((width, TILE), lambda i, c: (0, i)),
            ],
            scratch_shapes=[
                pltpu.VMEM((total, width), F32),
                pltpu.VMEM((total, width), LOW),
                pltpu.VMEM((total, width), LOW),
                pltpu.VMEM((total, 128), F32),
                pltpu.SemaphoreType.DMA((3,)),
            ],
        ),
        out_shape=[
            jax.ShapeDtypeStruct((total, width), LOW),
            jax.ShapeDtypeStruct((8, width), F32),
            jax.ShapeDtypeStruct((8, steps * TILE), F32),
            jax.ShapeDtypeStruct((width, steps * TILE), LOW),
        ],
        compiler_params=params(),
        cost_estimate=cost(),
        name="middle_last",
    )(core, branch, low, slope, inner_weight, outer_weight, g1, half, normed, rstd, *tokens)


def attend_back_kernel(groups, length, *refs):
    len_ref, branch_ref, qkv_ref, w_ref, pw_ref = refs[:5]
    dmix_ref, back_ref, sums_ref = refs[-3:]
    step = pl.program_id(0)
    start = lax.axis_index("seg") * length
    width = branch_ref.shape[1]
    scale = LOW(1.0 / math.sqrt(HEAD))
    att_grad = dot_rt(branch_ref[...], pw_ref[0]).astype(LOW)
    lane, first, second = head_masks()
    key_row = lax.broadcasted_iota(jnp.int32, (length, 1), 0)

    def stacked(both):
        return jnp.concatenate([both * first, both * second], axis=0)

    places = []
    for group in range(groups):
        count = jnp.clip(len_ref[step * groups + group] - start, 1, length)
        rows = slice(group * length, (group + 1) * length)
        for at in range(0, width, PAIR):
            cols, cols_k, cols_v = (slice(at + part * width, at + part * width + PAIR) for part in range(3))
            places.append((rows, cols, cols_k, cols_v, key_row < count))
    queries = [stacked(qkv_ref[rows, cols] * scale) for rows, cols, _, _, _ in places]
    att_both = [stacked(att_grad[rows, cols]) for rows, cols, _, _, _ in places]
    scores = [dot_rt(qkv_ref[rows, cols_k], item) for item, (rows, _, cols_k, _, _) in zip(queries, places)]
    prob_grads = [dot_rt(qkv_ref[rows, cols_v], item) for item, (rows, _, _, cols_v, _) in zip(att_both, places)]
    probs, score_grads = [], []
    for item, prob_grad, (_, _, _, _, valid) in zip(scores, prob_grads, places):
        item = jnp.where(valid, item, NEG)
        weights = jnp.exp(item - jnp.max(item, axis=0, keepdims=True))
        prob = weights * (1.0 / jnp.sum(weights, axis=0, keepdims=True))
        score_grad = prob * (prob_grad - jnp.sum(prob_grad * prob, axis=0, keepdims=True))
        probs.append(prob.astype(LOW))
        score_grads.append(score_grad.astype(LOW))
    for at, (rows, cols, cols_k, cols_v, _) in enumerate(places):
        by_query = dot_lt(score_grads[at], qkv_ref[rows, cols_k] * scale)
        dmix_ref[rows, cols] = jnp.where(lane < HEAD, by_query[:length], by_query[length:]).astype(LOW)
        dmix_ref[rows, cols_k] = dot(score_grads[at], queries[at]).astype(LOW)
        dmix_ref[rows, cols_v] = dot(probs[at], att_both[at]).astype(LOW)
    mixed = dmix_ref[...]
    back_ref[...] = branch_ref[...].astype(F32) + dot_rt(mixed, w_ref[0])

    @pl.when(step == 0)
    def _():
        sums_ref[...] = jnp.zeros_like(sums_ref)

    sums_ref[0:1, :] += colsum(mixed[:, :width].astype(F32))
    sums_ref[1:2, :] += colsum(mixed[:, 2 * width :].astype(F32))


def attend_back(branch, qkv, doc_length, seg_len, attn_weight, proj_weight, tokens=()):
    total, width = branch.shape
    groups = 2
    size = groups * seg_len
    return pl.pallas_call(
        functools.partial(attend_back_kernel, groups, seg_len),
        grid=(total // size,),
        in_specs=[
            pl.BlockSpec(memory_space=pltpu.SMEM),
            pl.BlockSpec((size, width), lambda i: (i, 0)),
            pl.BlockSpec((size, 3 * width), lambda i: (i, 0)),
            of_block(0, (width, 3 * width)),
            of_block(0, (width, width)),
        ]
        + token_specs(tokens),
        out_specs=[
            pl.BlockSpec((size, 3 * width), lambda i: (i, 0)),
            pl.BlockSpec((size, width), lambda i: (i, 0)),
            whole((8, width)),
        ],
        out_shape=[
            jax.ShapeDtypeStruct((total, 3 * width), LOW),
            jax.ShapeDtypeStruct((total, width), F32),
            jax.ShapeDtypeStruct((8, width), F32),
        ],
        compiler_params=params(),
        cost_estimate=cost(
            2 * total * width * 4 * width + 20 * total * seg_len * width, 20 * MIB, total * seg_len * HEADS
        ),
        name="attend_back",
    )(doc_length, branch, qkv, attn_weight, proj_weight, *tokens)


def last_grads_kernel(core_ref, rows_ref, att_ref, mixed_ref, branch_ref, *refs):
    left, right = refs[-2:]
    third = branch_ref.shape[1]
    turned = rows_ref[...].T
    left[:, :third] = dot(turned, mixed_ref[:, :third]).astype(LOW)
    right[...] = dot(turned, mixed_ref[:, third:]).astype(LOW)
    left[:, third:] = dot_lt(att_ref[...], branch_ref[...]).astype(LOW)


def last_grads(core, rows, attended, mixed, branch, tokens=()):
    total, width = rows.shape
    out = jax.ShapeDtypeStruct((width, width), LOW)
    return pl.pallas_call(
        last_grads_kernel,
        grid_spec=pltpu.PrefetchScalarGridSpec(
            num_scalar_prefetch=1,
            grid=(width // CHUNK,),
            in_specs=[
                pl.BlockSpec((total, CHUNK), lambda i, c: (0, i)),
                pl.BlockSpec((total, CHUNK), lambda i, c: (0, i)),
                pl.BlockSpec((total, mixed.shape[1] // 2), lambda i, c: (0, c[0])),
                pl.BlockSpec((total, width // 2), lambda i, c: (0, c[0])),
            ]
            + token_specs(tokens),
            out_specs=[pl.BlockSpec((CHUNK, width), lambda i, c: (i, 0))] * 2,
        ),
        out_shape=[out] * 2,
        compiler_params=params(),
        cost_estimate=cost(),
        name="last_grads",
    )(core, rows, attended, mixed, branch, *tokens)


def bits_of(axis):
    return lax.axis_size(axis).bit_length() - 1


def partner(value, axis, bit):
    return flipped(value, axis, 1 << bit)


def flipped(value, axis, mask):
    return lax.ppermute(value, axis, [(i, i ^ mask) for i in range(lax.axis_size(axis))])


def my_bit(axis, bit):
    return (lax.axis_index(axis) >> bit) & 1


def first_rows_pieces(value):
    pair = jnp.concatenate([value, partner(value, "seg", 0)], axis=0)
    return [pair] + [flipped(pair, "seg", flip) for flip in range(2, lax.axis_size("seg"), 2)]


class Job:
    def __init__(self, blocks, columns):
        self.blocks = blocks
        self.columns = columns
        self.operands = []
        self.parts = []

    def add(self, array, place):
        self.operands.append((array, place))
        return len(self.operands) - 1

    def rows(self):
        return sum(rows for rows, _ in self.parts)


def joined(first, second):
    job = Job(first.blocks, first.columns)
    job.operands = first.operands + second.operands
    shift = len(first.operands)
    job.parts = first.parts + [
        (rows, [(at + shift, start) for at, start in addends]) for rows, addends in second.parts
    ]
    return job


def run_kernel(jobs, skip, *refs):
    count = sum(len(job.operands) for job in jobs)
    sources = refs[skip : skip + count]
    outs = refs[skip + count : skip + count + len(jobs)]
    buffers = refs[skip + count + len(jobs) : -len(jobs) - 2]
    ready = refs[-len(jobs) - 2 : -2]
    in_sems, out_sems = refs[-2:]
    arriving, leaving = [], []
    at = sem = 0
    for job in jobs:
        copies = []
        for _, place in job.operands:
            before, after, part = place()
            copies.append(
                [
                    pltpu.make_async_copy(
                        sources[at].at[before, i, after, part], buffers[at].at[i], in_sems.at[sem + i]
                    )
                    for i in range(job.blocks)
                ]
            )
            at += 1
            sem += job.blocks
        for i in range(job.blocks):
            for copy in copies:
                copy[i].start()
        arriving.append(copies)
    at = sem = 0
    for job, copies, out, value in zip(jobs, arriving, outs, ready):
        mine = buffers[at : at + len(job.operands)]
        at += len(job.operands)
        for i in range(job.blocks):
            for copy in copies:
                copy[i].wait()
            start = 0
            for rows, addends in job.parts:
                total = None
                for which, first in addends:
                    item = mine[which][i, first : first + rows, :].astype(F32)
                    total = item if total is None else total + item
                value[i, start : start + rows, :] = total.astype(LOW)
                start += rows
            leaving.append(pltpu.make_async_copy(value.at[i], out.at[i], out_sems.at[sem]))
            leaving[-1].start()
            sem += 1
    for copy in leaving:
        copy.wait()


def run(jobs, tokens=()):
    operands = [array for job in jobs for array, _ in job.operands]
    buffers = [pltpu.VMEM((job.blocks,) + array.shape[4:], LOW) for job in jobs for array, _ in job.operands]
    ready = [pltpu.VMEM((job.blocks, job.rows(), job.columns), LOW) for job in jobs]
    arrivals = sum(job.blocks * len(job.operands) for job in jobs)
    return pl.pallas_call(
        functools.partial(run_kernel, jobs, len(tokens)),
        in_specs=token_specs(tokens) + token_specs(operands),
        out_specs=token_specs(jobs),
        out_shape=[jax.ShapeDtypeStruct((job.blocks, job.rows(), job.columns), LOW) for job in jobs],
        scratch_shapes=buffers
        + ready
        + [pltpu.SemaphoreType.DMA((arrivals,)), pltpu.SemaphoreType.DMA((sum(job.blocks for job in jobs),))],
        compiler_params=params(),
        cost_estimate=cost(),
        name="pick",
    )(*tokens, *operands)


def gate_kernel(*_):
    pass


def gated(values, tokens):
    count = len(values)
    return pl.pallas_call(
        gate_kernel,
        in_specs=token_specs(values) + token_specs(tokens),
        out_specs=token_specs(values),
        out_shape=[jax.ShapeDtypeStruct(item.shape, item.dtype) for item in values],
        input_output_aliases={at: at for at in range(count)},
        cost_estimate=cost(),
        name="gate",
    )(*values, *tokens)


class Flow:
    def __init__(self, groups, order):
        self.groups = groups
        self.received = []
        self.order = order
        self.seg_done = 0
        self.docs_done = []
        self.bits = list(range(bits_of("seg") - 1, -1, -1))
        self.columns = groups[0][0].shape[2]

    def job(self, sent_bit, last):
        docs_done = list(self.docs_done)
        level = len(docs_done) + (last is not None)
        done = self.order[: self.seg_done] + ([sent_bit] if sent_bit is not None else [])
        left = [bit for bit in self.bits if bit not in done]
        job = Job(1 << len(left), self.columns)

        def value(bits):
            index = 0
            for bit in bits:
                mine = my_bit("seg", bit)
                index = index * 2 + (1 - mine if bit == sent_bit else mine)
            return index

        def add(array, bits, docs_level):
            choices = 1 << (level - docs_level)
            rows = array.shape[1] // choices
            before = bits[: bits.index(left[0])] if left else []
            after = bits[bits.index(left[-1]) + 1 :] if left else bits

            def place():
                part = 0
                for bit in [my_bit("docs", bit) for bit in docs_done][docs_level:] + ([last()] if last else []):
                    part = part * 2 + bit
                return value(before), value(after), part

            array = array.reshape(1 << len(before), job.blocks, 1 << len(after), choices, rows, self.columns)
            return rows, job.add(array, place)

        shares = 1 << (bits_of("docs") - 1 - level) if len(self.groups) > 1 else 1
        added = [[add(array, self.bits, 0) for array in group] for group in self.groups]
        for share in range(shares):
            for group in added:
                rows = group[0][0] // shares
                job.parts.append((rows, [(at, share * rows) for _, at in group]))
        for array, bits, docs_level in self.received:
            _, at = add(array, bits, docs_level)
            start = 0
            for rows, addends in job.parts:
                addends.append((at, start))
                start += rows
        return job

    def seg_job(self):
        bit = self.order[self.seg_done]
        job = self.job(bit, None)
        self.seg_done += 1
        self.waiting = ("seg", bit)
        return job

    def docs_job(self, bit):
        job = self.job(None, lambda: 1 - my_bit("docs", bit))
        self.docs_done.append(bit)
        self.waiting = ("docs", bit)
        return job

    def settle_job(self):
        return self.job(None, None)

    def send(self, value):
        axis, bit = self.waiting
        left = [bit for bit in self.bits if bit not in self.order[: self.seg_done]]
        self.received.append((partner(value, axis, bit), left, len(self.docs_done)))

    def further(self, bits, tokens=()):
        while self.seg_done < bits:
            (value,) = run([self.seg_job()], tokens)
            self.send(value)


def finish_kernel(groups, outputs, small_at, *refs):
    me = lax.axis_index("docs")
    outs = refs[-outputs:]
    for first, count, reduce_x, span, cuts in groups:
        pieces = refs[first : first + count]
        rows = span[1] - span[0]

        def piece(target):
            value = pieces[0][span[0] : span[1], :].astype(F32)
            for flip in range(1, count):
                value = jnp.where(
                    (me & (count - 1)) ^ flip == target, pieces[flip][span[0] : span[1], :].astype(F32), value
                )
            return value

        for core in range(2):
            parts = [piece(2 * x + core) for x in range(count // 2)]
            if reduce_x:
                total = parts[0]
                for part in parts[1:]:
                    total = total + part
                parts = [total]
            for x, part in enumerate(parts):
                place = slice(x * rows, (x + 1) * rows)
                for which, start, end, at in cuts:
                    out = outs[which]
                    base = core * (out.shape[2] // 2) + at
                    out[0, place, base : base + end - start] = part[:, start:end]
    if small_at is None:
        return
    first, count, _, span, _ = groups[-1]
    pieces = refs[first : first + count]
    bias_ref, wide_ref, norm_ref = refs[first + count : first + count + 3]
    total = []
    for x in range(count // 2):
        value = pieces[0][span[1] :, :].astype(F32)
        for flip in range(2, count, 2):
            value = jnp.where((me ^ flip) >> 1 == x, pieces[flip][span[1] :, :].astype(F32), value)
        total.append(value)
    total = jnp.concatenate(total, axis=0)
    below = [(bias_ref, at) for at in range(4)] + [(norm_ref, at) for at in range(4)] + [(wide_ref, 0)]
    for row, (ref, at) in enumerate(below):
        out = outs[small_at + row]
        size = out.shape[1]
        out[0:1, :] = total[row : row + 1, :size]
        out[1:2, :] = ref[at : at + 1, :size]


def docs_pieces(value, count=None, tokens=()):
    pieces = []
    for flip in range(0, count or lax.axis_size("docs"), 2):
        pieces.append(flipped(value, "docs", flip) if flip else value)
        if flip and tokens:
            (pieces[-1],) = gated((pieces[-1],), tokens)
        pieces.append(partner(pieces[-1], "docs", 0))
    return pieces


def finish(groups, outputs, small=None, tokens=()):
    operands, layout, seen = [], [], {}
    for pieces, reduce_x, span, cuts in groups:
        if id(pieces) not in seen:
            seen[id(pieces)] = len(operands)
            operands += pieces
        layout.append((seen[id(pieces)], len(pieces), reduce_x, span, cuts))
    out_specs = [pl.BlockSpec((1,) + item.shape[1:], lambda i: (0, 0, 0)) for item in outputs]
    out_shape = [jax.ShapeDtypeStruct(item.shape, F32) for item in outputs]
    if small:
        operands += small[0]
        out_specs += [whole((2, size)) for size in small[1]]
        out_shape += [jax.ShapeDtypeStruct((2, size), F32) for size in small[1]]
    count = len(operands)
    return pl.pallas_call(
        functools.partial(finish_kernel, layout, len(out_shape), len(outputs) if small else None),
        grid=(1,),
        in_specs=[whole(item.shape) for item in operands] + token_specs(outputs) + token_specs(tokens),
        out_specs=out_specs,
        out_shape=out_shape,
        input_output_aliases={count + at: at for at in range(len(outputs))},
        compiler_params=params(),
        cost_estimate=cost(),
        name="finish",
    )(*operands, *outputs, *tokens)


def small_kernel(low_ref, middle_ref, top_ref, kept_ref, sent_ref, out_ref):
    first = lax.axis_index("docs") % 2 == 0
    out_ref[...] = jnp.zeros_like(out_ref)
    shards, _, _ = out_ref.shape
    part = low_ref.shape[1] // shards
    items = [(low_ref, 0), (low_ref, 1), (middle_ref, 2), (top_ref, 2)]
    items += [(middle_ref, 0), (middle_ref, 1), (top_ref, 0), (top_ref, 1)]
    for shard in range(shards):
        for row, (ref, at) in enumerate(items):
            value = ref[at : at + 1, shard * part : (shard + 1) * part]
            out_ref[shard, row : row + 1, :part] = value.astype(LOW)
        half = shards // 2
        wide = kept_ref.shape[1] // half
        place = slice(shard % half * wide, (shard % half + 1) * wide)
        mine = first if shard < half else jnp.logical_not(first)
        value = jnp.where(mine, kept_ref[0:1, place], sent_ref[0:1, place])
        out_ref[shard, 8:9, :wide] = value.astype(LOW)


def small_rows(low, middle, top, kept, sent, segments):
    width = low.shape[1]
    return pl.pallas_call(
        small_kernel,
        out_shape=jax.ShapeDtypeStruct((segments, 16, width), LOW),
        compiler_params=params(),
        cost_estimate=cost(),
        name="small_rows",
    )(low, middle, top, kept, sent)


def cross_grad_kernel(segments, width, hidden, count, *refs):
    bundles = refs[:count]
    attn_ref, proj_ref, inner_ref, outer_ref, bias_ref, wide_ref, norm_ref, place_ref = refs[-8:]
    places, _ = bundle_places(width, hidden, segments)

    def rows(at):
        start, size = places[at]
        return jnp.concatenate([ref[:, start : start + size] for ref in bundles], axis=0)

    outs = (attn_ref, proj_ref, inner_ref, outer_ref)
    biases = []
    for at, out in enumerate(outs):
        right = rows(4 + at)
        out[0] = dot_lt(rows(at), right)[: out.shape[1]]
        biases.append(colsum(right.astype(F32)))
    seg = lax.axis_index("seg")

    def own(value, slot):
        step = value.shape[1] // segments
        value = jnp.broadcast_to(value, (8, value.shape[1]))
        return pltpu.roll(value, lax.rem(value.shape[1] - seg * step, value.shape[1]), 1)[0:1, :slot]

    slot = places[0][1]
    mixed = biases[0]
    parts = [mixed[:, :width], mixed[:, 2 * width :], biases[1], biases[3]]
    bias_ref[...] = jnp.concatenate([own(part, slot) for part in parts] + [jnp.zeros((4, slot), F32)], axis=0)
    wide_ref[...] = jnp.broadcast_to(own(biases[2], places[3][1]), wide_ref.shape)
    start, size = places[8]
    sums = bundles[0][:, start : start + size].astype(F32)
    for ref in bundles[1:]:
        sums = sums + ref[:, start : start + size].astype(F32)
    norm_ref[...] = sums[:8]
    place_ref[...] = sums[8 : 8 + segments, : place_ref.shape[1]]


def cross_grads(bundles, segments, width, hidden, tokens=()):
    part, wide = width // segments, hidden // segments
    places, _ = bundle_places(width, hidden, segments)
    slot = places[0][1]
    stacked = [(part, 3 * width), (part, width), (part, hidden), (wide, width)]
    plain = [(8, slot), (8, places[3][1]), (8, slot), (segments, part)]
    return pl.pallas_call(
        functools.partial(cross_grad_kernel, segments, width, hidden, len(bundles)),
        grid=(1,),
        in_specs=[whole(bundles[0].shape)] * len(bundles) + token_specs(tokens),
        out_specs=[pl.BlockSpec((1,) + item, lambda i: (1, 0, 0)) for item in stacked]
        + [whole(item) for item in plain],
        out_shape=[jax.ShapeDtypeStruct((2,) + item, F32) for item in stacked]
        + [jax.ShapeDtypeStruct(item, F32) for item in plain],
        compiler_params=params(),
        cost_estimate=cost(),
        name="cross_grads",
    )(*bundles, *tokens)


def on_device(
    tokens,
    doc_length,
    attn_weight,
    query_bias,
    value_bias,
    proj_weight,
    proj_bias,
    norm1_gain,
    norm1_shift,
    inner_weight,
    inner_bias,
    outer_weight,
    outer_bias,
    norm2_gain,
    norm2_shift,
    seg_position,
    cotangent,
):
    docs_here, _, seg_len, width = tokens.shape
    hidden = inner_weight.shape[2]
    segments = lax.axis_size("seg")
    core = (lax.axis_index("docs") % 2).astype(jnp.int32).reshape(1)
    total = docs_here * seg_len
    rows_low = tokens.reshape(total, width)
    cots = cotangent.reshape(total, width)
    seg_bits = bits_of("seg")
    across_bits = list(range(bits_of("docs") - 1, 0, -1))

    qkv, attended, normed_one, hidden_low, rstd_one = attend(
        rows_low, doc_length, seg_len, attn_weight, query_bias, value_bias, proj_weight, proj_bias,
        norm1_gain, norm1_shift,
    )
    ff_weights = (inner_weight, inner_bias, outer_weight, outer_bias, norm2_gain, norm2_shift)
    leaders = lead(hidden_low, cots, docs_here, *ff_weights)
    pieces = first_rows_pieces(leaders)
    active, slope, seg_low, normed_two, rstd_two = feed(hidden_low, *ff_weights)

    cross_out, cross_back, bundle, branch_two, top_sums = cross_block(
        pieces, seg_position, doc_length, seg_len,
        attn_weight, query_bias, value_bias, proj_weight, proj_bias, norm1_gain, norm1_shift,
        inner_weight, inner_bias, outer_weight, outer_bias, norm2_gain, norm2_shift, cots, normed_two, rstd_two,
    )

    bundles = [bundle]
    for bit in across_bits:
        bundles = bundles + [partner(item, "docs", bit) for item in bundles]

    top_sums, outer_sent, outer_kept, layer_out, branch_two = top_back(
        cross_back, cross_out, seg_low, seg_len, normed_two, rstd_two, norm2_gain, top_sums, branch_two, active
    )
    outer_got = partner(outer_sent, "docs", 0)
    half_grad, inner_sums_sent, inner_sent = middle_first(
        core, branch_two, hidden_low, slope, inner_weight, outer_weight
    )

    def sharded(value):
        return value.reshape(segments, -1, value.shape[-1])

    rising = list(range(seg_bits))
    far_first = [0] + rising[:0:-1]
    outer = Flow([[sharded(outer_kept), sharded(outer_got)]], far_first)
    (outer_next,) = run([outer.seg_job()], (inner_sent,))
    outer.send(outer_next)
    inner_got = partner(inner_sent, "docs", 0)
    branch_one, mid_sums, inner_sums_kept, inner_kept = middle_last(
        core, branch_two, hidden_low, slope, inner_weight, outer_weight, norm1_gain,
        half_grad, normed_one, rstd_one, (outer_next,),
    )
    inner = Flow([[sharded(inner_kept), sharded(inner_got)]], rising)
    for bit in across_bits:
        (inner_next,) = run([inner.docs_job(bit)])
        inner.send(inner_next)
    mixed_grad, input_grad, low_sums = attend_back(
        branch_one, qkv, doc_length, seg_len, attn_weight, proj_weight, (inner_next,) + tuple(bundles[1:])
    )
    input_grad = input_grad.reshape(tokens.shape)
    others = [partner(item, "docs", 0) for item in bundles]
    left_sent, right_sent = last_grads(1 - core, rows_low, attended, mixed_grad, branch_one)
    for bit in across_bits[:-1]:
        (outer_next,) = run([outer.docs_job(bit)], (left_sent,))
        outer.send(outer_next)
    outer_next, inner_next = run([outer.docs_job(across_bits[-1]), inner.seg_job()], (left_sent, *others))
    outer.send(outer_next)
    inner.send(inner_next)
    bundles = bundles + others
    small = small_rows(low_sums, mid_sums, top_sums, inner_sums_kept, inner_sums_sent, segments)
    left_sent, right_sent, small = gated((left_sent, right_sent, small), (outer_next, inner_next))
    left_got, right_got, small_got = (partner(item, "docs", 0) for item in (left_sent, right_sent, small))
    left_kept, right_kept = last_grads(core, rows_low, attended, mixed_grad, branch_one, (left_sent,))
    attn_out, proj_out, inner_out, outer_out, cross_bias, cross_wide, cross_norm, position_grad = cross_grads(
        bundles, segments, width, hidden, (left_kept,)
    )
    left = Flow([[sharded(left_kept), sharded(left_got)]], rising)
    right = Flow([[sharded(right_kept), sharded(right_got)], [small, small_got]], far_first)
    flows = (left, right, inner, outer)

    def advance(jobs, of, tokens=()):
        values = run(jobs, tokens)
        for flow, value in zip(of, values):
            flow.send(value)
        return values

    for bit in across_bits[:-1]:
        advance([left.docs_job(bit)], (left,))
    last = advance(
        [left.docs_job(across_bits[-1]), right.seg_job(), inner.seg_job(), outer.seg_job()], flows, (cross_bias,)
    )
    for bit in across_bits[:-1]:
        advance([right.docs_job(bit)], (right,))
    last = advance([left.seg_job(), right.docs_job(across_bits[-1]), inner.seg_job(), outer.seg_job()], flows)
    inner.further(seg_bits, last)
    outer.further(seg_bits, last)
    values = run([left.seg_job(), right.seg_job(), inner.settle_job(), outer.settle_job()])
    left.send(values[0])
    right.send(values[1])
    inner, outer = (docs_pieces(value.reshape(value.shape[1:])) for value in values[2:])
    while left.seg_done < seg_bits:
        last = advance([left.seg_job(), right.seg_job()], (left, right))
    (last,) = run([joined(left.settle_job(), right.settle_job())], tuple(outer[1:] + inner[1:]))
    (outer_out,) = finish(
        [(outer, False, (0, outer[0].shape[0]), [(0, 0, width // 2, 0)])], [outer_out], tokens=(last,)
    )
    span = inner[0].shape[0]
    (inner_out,) = finish([(inner, False, (0, span), [(0, 0, hidden // 2, 0)])], [inner_out], tokens=(outer_out,))
    last = docs_pieces(last.reshape(last.shape[1:]), tokens=(inner_out,))
    part, wide = width // segments, hidden // segments
    third = width // 2
    attn_out, proj_out, *smalls = finish(
        [
            (last, False, (0, span), [(0, 0, third, 0), (1, third, width, 0)]),
            (last, False, (span, 2 * span), [(0, 0, width, third)]),
        ],
        [attn_out, proj_out],
        ([cross_bias, cross_wide, cross_norm], [part] * 8 + [wide]),
        (inner_out,),
    )
    qb, vb, pb, ob, g1, s1, g2, s2, ib = smalls
    return (
        layer_out.reshape(tokens.shape),
        input_grad,
        attn_out,
        qb,
        vb,
        proj_out,
        pb,
        g1,
        s1,
        inner_out,
        ib,
        outer_out,
        ob,
        g2,
        s2,
        position_grad,
    )


def solution(mesh):
    return jax.shard_map(
        on_device,
        mesh=mesh,
        in_specs=(
            P("docs", "seg", None, None),
            P("docs"),
            P(),
            P(),
            P(),
            P(),
            P(),
            P(),
            P(),
            P(),
            P(),
            P(),
            P(),
            P(),
            P(),
            P(),
            P("docs", "seg", None, None),
        ),
        out_specs=(
            P("docs", "seg", None, None),
            P("docs", "seg", None, None),
            P(None, "seg", None),
            P(None, "seg"),
            P(None, "seg"),
            P(None, "seg", None),
            P(None, "seg"),
            P(None, "seg"),
            P(None, "seg"),
            P(None, "seg", None),
            P(None, "seg"),
            P(None, "seg", None),
            P(None, "seg"),
            P(None, "seg"),
            P(None, "seg"),
            P(None, "seg"),
        ),
        check_vma=False,
    )
```
